256 devices in a mesh: ctx: 32 (over z, x), head: 8 (over y, core).
Axes of the slice: x: 4, y: 4, z: 8, core: 2. Of those that a mesh axis runs over, the one named last changes fastest.
Arguments:
- queries: bfloat16 [65536, 1024], P('ctx', 'head'), may hold values from -8 to 8
- block_picks: int32 [128, 8, 4], P('ctx', 'head'), may hold values from 0 to 255, as said below
- span_keys: bfloat16 [65536, 256], P('ctx'), may hold values from -8 to 8
- span_values: bfloat16 [65536, 256], P('ctx'), may hold values from -3.5 to 3.5
- cache_keys: bfloat16 [131072, 256], P('ctx'), may hold values from -4 to 4
- cache_values: bfloat16 [131072, 256], P('ctx'), may hold values from -3.5 to 3.5
- out_weight: bfloat16 [1024, 2048], P('head'), may hold values from -0.1875 to 0.1875
Outputs:
- attention: bfloat16 [65536, 1024], P('ctx', 'head')
- projected: bfloat16 [65536, 2048], P(('ctx', 'head'))
The draws below stay inside these ranges and needn't reach their ends.
Inputs may be any that keep to these rules, and one draw needn't show every extreme that they name: `block_picks`: the 4 picks of one query block and query head are distinct. Cache block b is held by ctx index b // 8. For each query head, at most 2 of the picks of the 4 query blocks of one ctx index lie in the blocks of any one ctx index; for each query head there is a ctx index into whose blocks exactly 2 picks fall from every ctx index.
All inputs are finite; a program needn't handle non-finite values.
Results may differ from the reference program's by a relative error of at most 0.017.
Values may be sent and summed in bfloat16 or wider, within the bound.
No kernel may reach another device: no remote copies, remote signals or barrier semaphores. Data moves between devices by JAX's collectives and lax.ppermute only.
A program may use at most 128 MiB of HBM per device.

```python
import math
import jax
import jax.numpy as jnp
from jax import lax

HD = 128
GROUP = 4
KVH = 2
D_OUT = 2048
BLK = 512
SEL = 4
QHEADS = 8
QB_DEV = 4
BLK_DEV = 8
QTOK = 65536
QBLOCKS = 128
CACHE = 131072
CACHE_BLOCKS = 256
CAP = 2
N_HEAD = 8


def draw_queries(key, part):
    key = jax.random.fold_in(key, 21)
    return (2.0 * jax.random.truncated_normal(key, -4.0, 4.0, (QTOK, QHEADS * HD), jnp.float32)).astype(jnp.bfloat16)


def draw_span_keys(key, part):
    key = jax.random.fold_in(key, 31)
    return jax.random.truncated_normal(key, -4.0, 4.0, (QTOK, KVH * HD), jnp.float32).astype(jnp.bfloat16)


def draw_span_values(key, part):
    key = jax.random.fold_in(key, 41)
    key_noise, key_level = jax.random.split(key)
    noise = jax.random.truncated_normal(key_noise, -4.0, 4.0, (QTOK, KVH * HD), jnp.float32)
    level = 0.8 * jax.random.truncated_normal(key_level, -3.0, 3.0, (QTOK // BLK, KVH * HD), jnp.float32)
    return (0.5 * (noise + jnp.repeat(level, BLK, axis=0))).astype(jnp.bfloat16)


def draw_cache_values(key, part):
    key = jax.random.fold_in(key, 51)
    key_noise, key_level = jax.random.split(key)
    noise = jax.random.truncated_normal(key_noise, -4.0, 4.0, (CACHE, KVH * HD), jnp.float32)
    level = 0.8 * jax.random.truncated_normal(key_level, -3.0, 3.0, (CACHE // BLK, KVH * HD), jnp.float32)
    return (0.5 * (noise + jnp.repeat(level, BLK, axis=0))).astype(jnp.bfloat16)


def draw_block_picks(key, part):
    key = jax.random.fold_in(key, 61)
    owners_total = QBLOCKS // QB_DEV
    pick_total = QB_DEV * SEL
    hot_owner = jax.random.randint(jax.random.fold_in(key, 1), (QHEADS,), 0, owners_total)
    owner_pool = jnp.arange((owners_total - 1) * CAP, dtype=jnp.int32) // CAP
    sender_keys = jax.random.split(jax.random.fold_in(key, 2), owners_total * QHEADS)
    slot_index = jnp.arange(SEL, dtype=jnp.int32)

    def one_sender(sender_key, hot_one):
        key_others, key_shuffle, key_offset = jax.random.split(sender_key, 3)
        others = jax.random.permutation(key_others, owner_pool)[:pick_total - CAP]
        others = others + (others >= hot_one).astype(jnp.int32)
        owners = jnp.concatenate([jnp.full((CAP,), hot_one, jnp.int32), others])
        owners = jax.random.permutation(key_shuffle, owners).reshape(QB_DEV, SEL)
        base_offset = jax.random.randint(key_offset, (QB_DEV, SEL), 0, BLK_DEV)
        same_owner = owners[:, :, None] == owners[:, None, :]
        earlier = slot_index[None, :] < slot_index[:, None]
        rank_in_row = jnp.sum((same_owner & earlier[None]).astype(jnp.int32), axis=2)
        first_pick = jnp.min(jnp.where(same_owner, slot_index[None, None, :], SEL), axis=2)
        first_offset = jnp.take_along_axis(base_offset, first_pick, axis=1)
        return owners * BLK_DEV + (first_offset + rank_in_row) % BLK_DEV
    hot_each = jnp.tile(hot_owner, owners_total)
    picks = jax.vmap(one_sender)(sender_keys, hot_each)
    picks = picks.reshape(owners_total, QHEADS, QB_DEV, SEL).transpose(0, 2, 1, 3)
    return picks.reshape(QBLOCKS, QHEADS, SEL).astype(jnp.int32)


def level_of(key, dims, cuts, low, top_value):
    def one(dim, shards_of):
        steps = jax.random.uniform(jax.random.fold_in(jax.random.fold_in(key, 6), dim), (shards_of,), jnp.float32, low / len(cuts), top_value / len(cuts))
        return jnp.repeat(jnp.exp(steps), dims[dim] // shards_of).reshape((-1,) + (1,) * (len(dims) - dim - 1))

    factor_of = one(*cuts[0])
    for cut in cuts[1:]:
        factor_of = factor_of * one(*cut)
    return factor_of


def centred(own_key, extent, deviation, bound, cuts=(), held_as=jnp.bfloat16):
    drawn = jax.random.normal(own_key, extent, jnp.float32) * deviation
    if len(cuts) > 0:
        drawn = level_of(own_key, extent, cuts, -0.22, 0.18) * drawn
    return jnp.clip(drawn, min=-bound, max=bound).astype(held_as)


def setup_inputs(seed: int = 0) -> dict:
    seeds = jax.random.split(jax.random.key(seed), 8)
    queries = draw_queries(jax.random.fold_in(seeds[7], 71), 0)
    block_picks = draw_block_picks(jax.random.fold_in(seeds[7], 71), 0)
    span_keys = draw_span_keys(jax.random.fold_in(seeds[7], 71), 0)
    span_values = draw_span_values(jax.random.fold_in(seeds[7], 71), 0)
    cache_keys = centred(seeds[4], (CACHE, KVH * HD), 1.0, 4.0, ((0, 32),))
    cache_values = draw_cache_values(jax.random.fold_in(seeds[7], 71), 0)
    out_weight = centred(seeds[6], (QHEADS * HD, D_OUT), (QHEADS * HD) ** -0.5, 0.1875, ((0, 8),))
    return dict(queries=queries, block_picks=block_picks, span_keys=span_keys, span_values=span_values, cache_keys=cache_keys, cache_values=cache_values, out_weight=out_weight)


NEG_FILL = -1e+30

def block_partial(query_tile, key_block, value_block, allowed):
    scores = jnp.einsum('qd,kd->qk', query_tile.astype(jnp.float32), key_block.astype(jnp.float32)) * (1.0 / math.sqrt(HD))
    scores = jnp.where(allowed, scores, NEG_FILL)
    highest = lax.optimization_barrier(jnp.max(scores, axis=1))
    weights = jnp.where(allowed, jnp.exp(scores - highest[:, None]), 0.0)
    totals = lax.optimization_barrier(jnp.sum(weights, axis=1))
    rounded = weights.astype(jnp.bfloat16).astype(jnp.float32)
    block_out = jnp.einsum('qk,kd->qd', rounded, value_block.astype(jnp.float32)).astype(jnp.bfloat16)
    return (block_out, highest, totals)

def merge_partials(block_out, highest, totals):
    overall_top = lax.optimization_barrier(jnp.max(highest, axis=0))
    factor = jnp.exp(highest - overall_top[None, :])
    denominator = lax.optimization_barrier(jnp.sum(factor * totals, axis=0))
    numerator = lax.optimization_barrier(jnp.sum(factor[:, :, None] * block_out.astype(jnp.float32), axis=0))
    return (numerator / denominator[:, None]).astype(jnp.bfloat16)

def reference(queries, block_picks, span_keys, span_values, cache_keys, cache_values, out_weight):
    cache_key_view = cache_keys.reshape(CACHE_BLOCKS, BLK, KVH, HD)
    cache_value_view = cache_values.reshape(CACHE_BLOCKS, BLK, KVH, HD)
    span_key_view = span_keys.reshape(QBLOCKS, BLK, KVH, HD)
    span_value_view = span_values.reshape(QBLOCKS, BLK, KVH, HD)
    query_view = queries.reshape(QBLOCKS, BLK, QHEADS, HD)
    causal = jnp.arange(BLK)[:, None] >= jnp.arange(BLK)[None, :]
    kv_of_head = (jnp.arange(QHEADS) // GROUP).astype(jnp.int32)

    def one_block(block_index):
        query_tiles = lax.dynamic_index_in_dim(query_view, block_index, 0, keepdims=False)
        row_picks = lax.dynamic_index_in_dim(block_picks, block_index, 0, keepdims=False)
        own_keys = lax.dynamic_index_in_dim(span_key_view, block_index, 0, keepdims=False)
        own_values = lax.dynamic_index_in_dim(span_value_view, block_index, 0, keepdims=False)

        def one_head(head_query, head_picks, kv_head):
            remote_keys = cache_key_view[head_picks, :, kv_head, :]
            remote_values = cache_value_view[head_picks, :, kv_head, :]
            far_out, far_top, far_totals = jax.vmap(lambda key_tile, value_tile: block_partial(head_query, key_tile, value_tile, True))(remote_keys, remote_values)
            near_out, near_top, near_totals = block_partial(head_query, own_keys[:, kv_head, :], own_values[:, kv_head, :], causal)
            return merge_partials(jnp.concatenate([far_out, near_out[None]], axis=0), jnp.concatenate([far_top, near_top[None]], axis=0), jnp.concatenate([far_totals, near_totals[None]], axis=0))
        head_outputs = jax.vmap(one_head)(jnp.transpose(query_tiles, (1, 0, 2)), row_picks, kv_of_head)
        return jnp.transpose(head_outputs, (1, 0, 2)).reshape(BLK, QHEADS * HD)
    attention = lax.map(one_block, jnp.arange(QBLOCKS, dtype=jnp.int32)).reshape(QTOK, QHEADS * HD)
    group_width = QHEADS * HD // N_HEAD
    projected = jnp.zeros((QTOK, D_OUT), jnp.float32)
    for member in range(N_HEAD):
        group_term = jnp.dot(attention[:, member * group_width:(member + 1) * group_width], out_weight[member * group_width:(member + 1) * group_width], preferred_element_type=jnp.float32)
        projected = projected + group_term.astype(jnp.bfloat16).astype(jnp.float32)
    return (attention, projected.astype(jnp.bfloat16))
```

```python
import functools
import math

import jax
import jax.numpy as jnp
from jax import lax
from jax.experimental import pallas as pl
from jax.experimental.pallas import tpu as pltpu
from jax.sharding import PartitionSpec as P

HD = 128
GROUP = 4
BLK = 512
SEL = 4
QB = 4
HEADS = 8
CHUNKS = 2
PAY = HD + 16
SCALE = math.log2(math.e) / math.sqrt(HD)
NEG = -1e30
F32 = jnp.float32
BF16 = jnp.bfloat16


def dot_nt(a, b):
    return lax.dot_general(a, b, (((1,), (1,)), ((), ())), preferred_element_type=F32)


def dot_tn(a, b):
    return lax.dot_general(a, b, (((0,), (0,)), ((), ())), preferred_element_type=F32)


def rounded_top(raw):
    return (raw * SCALE).astype(BF16).astype(F32)


def near_kernel(kv_ref, q_ref, k_ref, v_ref, acc_ref, m_ref, l_ref):
    scores = dot_nt(k_ref[...], q_ref[...])
    keys = lax.broadcasted_iota(jnp.int32, (BLK, BLK), 0)
    rows = lax.broadcasted_iota(jnp.int32, (BLK, BLK), 1)
    scores = jnp.where(keys <= rows, scores, NEG)
    top = rounded_top(jnp.max(scores, axis=0, keepdims=True))
    weights = jnp.exp2(scores * SCALE - top)
    m_ref[0] = top
    l_ref[0] = jnp.sum(weights, axis=0, keepdims=True)
    acc_ref[0] = dot_tn(v_ref[...], weights.astype(BF16))


def near(queries, span_keys, span_values, kv):
    grid_spec = pltpu.PrefetchScalarGridSpec(
        num_scalar_prefetch=1,
        grid=(QB,),
        in_specs=[
            pl.BlockSpec((BLK, HD), lambda i, kv: (i, 0)),
            pl.BlockSpec((BLK, HD), lambda i, kv: (i, kv[0])),
            pl.BlockSpec((BLK, HD), lambda i, kv: (i, kv[0])),
        ],
        out_specs=[
            pl.BlockSpec((1, HD, BLK), lambda i, kv: (i, 0, 0)),
            pl.BlockSpec((1, 1, BLK), lambda i, kv: (i, 0, 0)),
            pl.BlockSpec((1, 1, BLK), lambda i, kv: (i, 0, 0)),
        ],
    )
    return pl.pallas_call(
        near_kernel,
        grid_spec=grid_spec,
        out_shape=[
            jax.ShapeDtypeStruct((QB, HD, BLK), F32),
            jax.ShapeDtypeStruct((QB, 1, BLK), F32),
            jax.ShapeDtypeStruct((QB, 1, BLK), F32),
        ],
        cost_estimate=pl.CostEstimate(
            flops=QB * 4 * BLK * BLK * HD, bytes_accessed=4 << 20, transcendentals=QB * BLK * BLK
        ),
        name="near",
    )(kv, queries, span_keys, span_values)


def far_kernel(picks_ref, pos_ref, q_ref, *refs, first, last):
    kv_refs = refs[:SEL]
    refs = refs[SEL:]
    if not first:
        acc_in, m_in, l_in = refs[:3]
        refs = refs[3:]
    keys = jnp.concatenate([ref[0, 0] for ref in kv_refs], axis=0)
    values = jnp.concatenate([ref[0, 1] for ref in kv_refs], axis=0)
    scores = dot_nt(keys, q_ref[0])
    top = rounded_top(jnp.max(scores, axis=0, keepdims=True))
    if not first:
        top = jnp.maximum(top, m_in[0])
    weights = jnp.exp2(scores * SCALE - top)
    total = jnp.sum(weights, axis=0, keepdims=True)
    out = dot_tn(values, weights.astype(BF16))
    if not first:
        factor = jnp.exp2(m_in[0] - top)
        total = total + factor * l_in[0]
        out = out + factor * acc_in[0]
    if last:
        pack_state(refs[0], out, top, total)
    else:
        refs[0][0] = out
        refs[1][0] = top
        refs[2][0] = total


def pack_state(ref, out, top, total):
    ref[0, :HD, :] = out.astype(BF16)
    high = total.astype(BF16)
    low = (total - high.astype(F32)).astype(BF16)
    ref[0, HD:, :] = jnp.concatenate(
        [top.astype(BF16), high, low, jnp.zeros((PAY - HD - 3, BLK), BF16)], axis=0
    )


def unpack_state(ref):
    tail = ref[0, HD:, :].astype(F32)
    return ref[0, :HD, :].astype(F32), tail[0:1], tail[1:2] + tail[2:3]


def far(queries, gathered, picks, pos, state, last):
    rows = gathered.shape[2]
    units = GROUP * QB
    first = state is None

    def pick_spec(i):
        return pl.BlockSpec(
            (1, 2, rows, HD),
            lambda u, picks, pos: (picks[((u // QB) ^ pos[0]) * QB * SEL + (u % QB) * SEL + i], 0, 0, 0),
        )

    state_specs = [
        pl.BlockSpec((1, HD, BLK), lambda u, picks, pos: (u, 0, 0)),
        pl.BlockSpec((1, 1, BLK), lambda u, picks, pos: (u, 0, 0)),
        pl.BlockSpec((1, 1, BLK), lambda u, picks, pos: (u, 0, 0)),
    ]
    state_shapes = [
        jax.ShapeDtypeStruct((units, HD, BLK), F32),
        jax.ShapeDtypeStruct((units, 1, BLK), F32),
        jax.ShapeDtypeStruct((units, 1, BLK), F32),
    ]
    if last:
        out_specs = [pl.BlockSpec((1, PAY, BLK), lambda u, picks, pos: (u, 0, 0))]
        out_shapes = [jax.ShapeDtypeStruct((units, PAY, BLK), BF16)]
    else:
        out_specs, out_shapes = state_specs, state_shapes
    grid_spec = pltpu.PrefetchScalarGridSpec(
        num_scalar_prefetch=2,
        grid=(units,),
        in_specs=[
            pl.BlockSpec((1, BLK, HD), lambda u, picks, pos: ((u // QB) ^ pos[0], u % QB, 0))
        ]
        + [pick_spec(i) for i in range(SEL)]
        + ([] if first else state_specs),
        out_specs=out_specs,
    )
    result = pl.pallas_call(
        functools.partial(far_kernel, first=first, last=last),
        grid_spec=grid_spec,
        out_shape=out_shapes,
        cost_estimate=pl.CostEstimate(
            flops=units * 4 * BLK * SEL * rows * HD,
            bytes_accessed=8 << 20,
            transcendentals=units * BLK * SEL * rows,
        ),
        name="far",
    )(picks, pos, queries, *([gathered] * SEL), *(() if first else state))
    return result[0] if last else result


def merge_two_kernel(a_ref, b_ref, out_ref):
    acc_a, m_a, l_a = unpack_state(a_ref)
    acc_b, m_b, l_b = unpack_state(b_ref)
    top = jnp.maximum(m_a, m_b)
    f_a = jnp.exp2(m_a - top)
    f_b = jnp.exp2(m_b - top)
    pack_state(out_ref, f_a * acc_a + f_b * acc_b, top, f_a * l_a + f_b * l_b)


def merge_two(mine, mine_base, other, other_base):
    return pl.pallas_call(
        merge_two_kernel,
        grid=(QB,),
        in_specs=[
            pl.BlockSpec((1, PAY, BLK), lambda i: (mine_base + i, 0, 0)),
            pl.BlockSpec((1, PAY, BLK), lambda i: (other_base + i, 0, 0)),
        ],
        out_specs=pl.BlockSpec((1, PAY, BLK), lambda i: (i, 0, 0)),
        out_shape=jax.ShapeDtypeStruct((QB, PAY, BLK), BF16),
        name="merge_two",
    )(mine, other)


def merge_all_kernel(a_ref, b_ref, c_ref, acc_ref, m_ref, l_ref, out_ref):
    states = [unpack_state(a_ref), unpack_state(b_ref), unpack_state(c_ref)]
    states.append((acc_ref[0], m_ref[0], l_ref[0]))
    top = functools.reduce(jnp.maximum, [m for _, m, _ in states])
    factors = [jnp.exp2(m - top) for _, m, _ in states]
    total = sum(f * l for f, (_, _, l) in zip(factors, states))
    out = sum(f * acc for f, (acc, _, _) in zip(factors, states))
    out_ref[...] = (out / total).T.astype(BF16)


def merge_all(mine, core_part, chip_part, near_state):
    return pl.pallas_call(
        merge_all_kernel,
        grid=(QB,),
        in_specs=[
            pl.BlockSpec((1, PAY, BLK), lambda i: (i, 0, 0)),
            pl.BlockSpec((1, PAY, BLK), lambda i: (i, 0, 0)),
            pl.BlockSpec((1, PAY, BLK), lambda i: (i, 0, 0)),
            pl.BlockSpec((1, HD, BLK), lambda i: (i, 0, 0)),
            pl.BlockSpec((1, 1, BLK), lambda i: (i, 0, 0)),
            pl.BlockSpec((1, 1, BLK), lambda i: (i, 0, 0)),
        ],
        out_specs=pl.BlockSpec((BLK, HD), lambda i: (i, 0)),
        out_shape=jax.ShapeDtypeStruct((QB * BLK, HD), BF16),
        name="merge_all",
    )(mine, core_part, chip_part, *near_state)


def project_kernel(a_ref, w_ref, out_ref):
    rows = jnp.concatenate([a_ref[i] for i in range(HEADS)], axis=1)
    out_ref[...] = jnp.dot(rows, w_ref[...], preferred_element_type=F32).astype(BF16)


def project(parts, weight):
    rows = parts.shape[1]
    width = weight.shape[1]
    tile = 512
    return pl.pallas_call(
        project_kernel,
        grid=(width // tile,),
        in_specs=[
            pl.BlockSpec((HEADS, rows, HD), lambda i: (0, 0, 0)),
            pl.BlockSpec((HEADS * HD, tile), lambda i: (0, i)),
        ],
        out_specs=pl.BlockSpec((rows, tile), lambda i: (0, i)),
        out_shape=jax.ShapeDtypeStruct((rows, width), BF16),
        name="project",
    )(parts, weight)


def body(queries, block_picks, span_keys, span_values, cache_keys, cache_values, out_weight):
    head = lax.axis_index("head")
    part = head % GROUP
    kv = head // GROUP
    blocks = cache_keys.shape[0] // BLK
    share = BLK // GROUP
    rows = share // CHUNKS
    groups = [list(range(g, g + GROUP)) for g in range(0, HEADS, GROUP)]

    def cut(cache, chunk):
        view = cache.reshape(blocks, BLK, cache.shape[1])
        return lax.dynamic_slice(
            view, (0, part * share + chunk * rows, kv * HD), (blocks, rows, HD)
        )

    group_queries = lax.all_gather(queries, "head", axis_index_groups=groups)
    group_picks = lax.all_gather(block_picks, "head", axis_index_groups=groups).reshape(-1)
    gathered = []
    for chunk in range(CHUNKS):
        piece = jnp.stack([cut(cache_keys, chunk), cut(cache_values, chunk)], axis=1)
        gathered.append(lax.all_gather(piece, "ctx", axis=0, tiled=True))
    weight = lax.all_gather(out_weight, "head", axis=0, tiled=True)

    near_state = near(queries, span_keys, span_values, kv[None])
    state = None
    for chunk in range(CHUNKS):
        state = far(
            group_queries, gathered[chunk], group_picks, part[None], state, chunk == CHUNKS - 1
        )

    core_perm = [(h, h ^ 1) for h in range(HEADS)]
    chip_perm = [(h, h ^ 2) for h in range(HEADS)]
    for_chip = lax.ppermute(state[3 * QB :], "head", core_perm)
    for_core = lax.ppermute(state[QB : 2 * QB], "head", core_perm)
    chip_part = lax.ppermute(merge_two(state, 2 * QB, for_chip, 0), "head", chip_perm)
    attention = merge_all(state, for_core, chip_part, near_state)

    share_rows = attention.shape[0] // HEADS
    parts = lax.all_to_all(
        attention.reshape(HEADS, share_rows, HD), "head", split_axis=0, concat_axis=0, tiled=True
    )
    return attention, project(parts, weight)


def solution(mesh):
    placed = (
        P("ctx", "head"),
        P("ctx", "head", None),
        P("ctx", None),
        P("ctx", None),
        P("ctx", None),
        P("ctx", None),
        P("head", None),
    )
    return jax.shard_map(
        body,
        mesh=mesh,
        in_specs=placed,
        out_specs=(P("ctx", "head"), P(("ctx", "head"), None)),
        check_vma=False,
    )
```

```python
import functools
import math

import jax
import jax.numpy as jnp
from jax import lax
from jax.experimental import pallas as pl
from jax.experimental.pallas import tpu as pltpu
from jax.sharding import PartitionSpec as P

HD = 128
GROUP = 4
BLK = 512
SEL = 4
QB = 4
BLOCKS = 8
NX = 4
NZ = 8
TAIL = 16
SCALE = math.log2(math.e) / math.sqrt(HD)
NEG = -1e30
F32 = jnp.float32
BF16 = jnp.bfloat16
SPLIT = (8, 4, 4)
VMEM_BYTES = 48 << 20


def dot_nt(a, b):
    return lax.dot_general(a, b, (((1,), (1,)), ((), ())), preferred_element_type=F32)


def dot_tn(a, b):
    return lax.dot_general(a, b, (((0,), (0,)), ((), ())), preferred_element_type=F32)


def rounded_top(raw):
    return (raw * SCALE).astype(BF16).astype(F32)


def near_kernel(kv_ref, q_ref, k_ref, v_ref, acc_ref, m_ref, l_ref):
    scores = dot_nt(k_ref[...], q_ref[...])
    keys = lax.broadcasted_iota(jnp.int32, (BLK, BLK), 0)
    rows = lax.broadcasted_iota(jnp.int32, (BLK, BLK), 1)
    scores = jnp.where(keys <= rows, scores, NEG)
    top = rounded_top(jnp.max(scores, axis=0, keepdims=True))
    weights = jnp.exp2(scores * SCALE - top)
    m_ref[0] = top
    l_ref[0] = jnp.sum(weights, axis=0, keepdims=True)
    acc_ref[0] = dot_tn(v_ref[...], weights.astype(BF16))


def state_shapes():
    return [
        jax.ShapeDtypeStruct((QB, HD, BLK), F32),
        jax.ShapeDtypeStruct((QB, 1, BLK), F32),
        jax.ShapeDtypeStruct((QB, 1, BLK), F32),
    ]


def near(queries, span_keys, span_values, kv):
    grid_spec = pltpu.PrefetchScalarGridSpec(
        num_scalar_prefetch=1,
        grid=(QB,),
        in_specs=[
            pl.BlockSpec((BLK, HD), lambda i, kv: (i, 0)),
            pl.BlockSpec((BLK, HD), lambda i, kv: (i, kv[0])),
            pl.BlockSpec((BLK, HD), lambda i, kv: (i, kv[0])),
        ],
        out_specs=[
            pl.BlockSpec((1, HD, BLK), lambda i, kv: (i, 0, 0)),
            pl.BlockSpec((1, 1, BLK), lambda i, kv: (i, 0, 0)),
            pl.BlockSpec((1, 1, BLK), lambda i, kv: (i, 0, 0)),
        ],
    )
    return pl.pallas_call(
        near_kernel,
        grid_spec=grid_spec,
        out_shape=state_shapes(),
        cost_estimate=pl.CostEstimate(
            flops=QB * 4 * BLK * BLK * HD, bytes_accessed=4 << 20, transcendentals=QB * BLK * BLK
        ),
        name="near",
    )(kv, queries, span_keys, span_values)


def pack_state(ref, i, out, top, total):
    ref[i, :HD, :] = out.astype(BF16)
    high = total.astype(BF16)
    low = (total - high.astype(F32)).astype(BF16)
    ref[i, HD:, :] = jnp.concatenate(
        [top.astype(BF16), high, low, jnp.zeros((TAIL - 3, out.shape[1]), BF16)], axis=0
    )


def unpack_state(ref, i):
    tail = ref[i, HD:, :].astype(F32)
    return ref[i, :HD, :].astype(F32), tail[0:1], tail[1:2] + tail[2:3]


def far_kernel(where_ref, *refs, counts):
    q_refs, refs = refs[:2], refs[2:]
    sources = []
    for count in counts:
        sources.append(refs[:count])
        refs = refs[count:]
    out_refs, refs = refs[:2], refs[2:]
    buffers, sems = refs[:-1], refs[-1]
    parts = len(counts)

    def fetch(pick, carry):
        for part in range(parts):
            array = where_ref[pick, 2 * part]
            index = where_ref[pick, 2 * part + 1]
            for number, source in enumerate(sources[part]):

                def start(source=source, part=part, index=index):
                    pltpu.make_async_copy(
                        source.at[index], buffers[part].at[pick], sems.at[pick // SEL, part]
                    ).start()

                if counts[part] == 1:
                    start()
                else:
                    pl.when(array == number)(start)
        return carry

    lax.fori_loop(0, 2 * QB * SEL, fetch, 0)

    def unit(row, q_ref, out_ref, i):
        for part in range(parts):
            held = buffers[part].at[pl.ds(row * SEL, SEL)]
            pltpu.make_async_copy(held, held, sems.at[row, part]).wait()

        def joined(which):
            return jnp.concatenate(
                [buffers[part][row * SEL + j, which] for part in range(parts) for j in range(SEL)],
                axis=0,
            )

        scores = dot_nt(joined(0), q_ref[pl.ds(i * BLK, BLK), :])
        top = rounded_top(jnp.max(scores, axis=0, keepdims=True))
        weights = jnp.exp2(scores * SCALE - top)
        total = jnp.sum(weights, axis=0, keepdims=True)
        pack_state(out_ref, i, dot_tn(joined(1), weights.astype(BF16)), top, total)

    for half in range(2):

        def pair(step, carry, half=half):
            for k in range(2):
                i = 2 * step + k
                unit(half * QB + i, q_refs[half], out_refs[half], i)
            return carry

        lax.fori_loop(0, QB // 2, pair, 0)


def far(where, queries, parts):
    pay = HD + TAIL
    vmem = pl.BlockSpec(memory_space=pltpu.VMEM)
    arrays = [array for part in parts for array in part]
    return pl.pallas_call(
        functools.partial(far_kernel, counts=tuple(len(part) for part in parts)),
        in_specs=[pl.BlockSpec(memory_space=pltpu.SMEM)]
        + [vmem] * 2
        + [pl.BlockSpec(memory_space=pl.ANY)] * len(arrays),
        out_specs=[vmem] * 2,
        out_shape=[jax.ShapeDtypeStruct((QB, pay, BLK), BF16)] * 2,
        scratch_shapes=[
            pltpu.VMEM((2 * QB * SEL,) + part[0].shape[1:], BF16) for part in parts
        ]
        + [pltpu.SemaphoreType.DMA((2 * QB, len(parts)))],
        compiler_params=pltpu.CompilerParams(vmem_limit_bytes=VMEM_BYTES),
        cost_estimate=pl.CostEstimate(
            flops=2 * QB * 4 * BLK * BLK * HD,
            bytes_accessed=5 << 20,
            transcendentals=2 * QB * BLK * BLK,
        ),
        name="far",
    )(where, *queries, *arrays)


def merge_two_kernel(a_ref, b_ref, *out_refs):
    per = QB // len(out_refs)
    for i in range(QB):
        acc_a, m_a, l_a = unpack_state(a_ref, i)
        acc_b, m_b, l_b = unpack_state(b_ref, i)
        top = jnp.maximum(m_a, m_b)
        f_a = jnp.exp2(m_a - top)
        f_b = jnp.exp2(m_b - top)
        pack_state(
            out_refs[i // per], i % per, f_a * acc_a + f_b * acc_b, top, f_a * l_a + f_b * l_b
        )


def merge_two(mine, other, pieces):
    vmem = pl.BlockSpec(memory_space=pltpu.VMEM)
    shape = (QB // pieces,) + mine.shape[1:]
    return pl.pallas_call(
        merge_two_kernel,
        in_specs=[vmem] * 2,
        out_specs=[vmem] * pieces,
        out_shape=[jax.ShapeDtypeStruct(shape, BF16)] * pieces,
        name="merge_two",
    )(mine, other)


def merge_here_kernel(a_ref, b_ref, acc_ref, m_ref, l_ref, acc_out, m_out, l_out):
    for i in range(QB):
        states = [unpack_state(a_ref, i), unpack_state(b_ref, i)]
        states.append((acc_ref[i], m_ref[i], l_ref[i]))
        top = functools.reduce(jnp.maximum, [m for _, m, _ in states])
        factors = [jnp.exp2(m - top) for _, m, _ in states]
        m_out[i] = top
        l_out[i] = sum(f * l for f, (_, _, l) in zip(factors, states))
        acc_out[i] = sum(f * acc for f, (acc, _, _) in zip(factors, states))


def merge_here(mine, core_part, near_state):
    vmem = pl.BlockSpec(memory_space=pltpu.VMEM)
    return pl.pallas_call(
        merge_here_kernel,
        in_specs=[vmem] * 5,
        out_specs=[vmem] * 3,
        out_shape=state_shapes(),
        name="merge_here",
    )(mine, core_part, *near_state)


def merge_last_kernel(acc_ref, m_ref, l_ref, *refs):
    chip_refs, out_ref = refs[:-1], refs[-1]
    per = QB // len(chip_refs)
    for i in range(QB):
        acc, m, l = unpack_state(chip_refs[i // per], i % per)
        top = jnp.maximum(m, m_ref[i])
        f_far = jnp.exp2(m - top)
        f_here = jnp.exp2(m_ref[i] - top)
        total = f_far * l + f_here * l_ref[i]
        out = (f_far * acc + f_here * acc_ref[i]) / total
        out_ref[i * BLK : (i + 1) * BLK, :] = out.T.astype(BF16)


def merge_last(here, chip_parts):
    vmem = pl.BlockSpec(memory_space=pltpu.VMEM)
    return pl.pallas_call(
        merge_last_kernel,
        in_specs=[vmem] * (3 + len(chip_parts)),
        out_specs=vmem,
        out_shape=jax.ShapeDtypeStruct((QB * BLK, HD), BF16),
        name="merge_last",
    )(*here, *chip_parts)


def project_kernel(head_ref, a_ref, *refs):
    w_refs, out_ref = refs[:-1], refs[-1]
    rows = jnp.concatenate([a_ref[head_ref[0] ^ i] for i in range(len(w_refs))], axis=1)
    weight = jnp.concatenate([w_ref[...] for w_ref in w_refs], axis=0)
    out_ref[...] = jnp.dot(rows, weight, preferred_element_type=F32).astype(BF16)


def project(head, parts, weights):
    heads, rows, _ = parts.shape
    width = weights[0].shape[1]
    tile = 512
    grid_spec = pltpu.PrefetchScalarGridSpec(
        num_scalar_prefetch=1,
        grid=(width // tile,),
        in_specs=[pl.BlockSpec((heads, rows, HD), lambda i, head: (0, 0, 0))]
        + [pl.BlockSpec((HD, tile), lambda i, head: (0, i))] * heads,
        out_specs=pl.BlockSpec((rows, tile), lambda i, head: (0, i)),
    )
    return pl.pallas_call(
        project_kernel,
        grid_spec=grid_spec,
        out_shape=jax.ShapeDtypeStruct((rows, width), BF16),
        name="project",
    )(head, parts, *weights)


def shift(array, dz, dx):
    pairs = []
    for z in range(NZ):
        for x in range(NX):
            pairs.append((z * NX + x, (z + dz) % NZ * NX + (x + dx) % NX))
    return lax.ppermute(array, "ctx", pairs)


def swap(array, bits):
    return lax.ppermute(array, "head", [(h, h ^ bits) for h in range(lax.axis_size("head"))])


def ring_four(piece):
    half = piece.shape[0] // 2
    below = shift(piece, 0, 1)
    above = shift(piece, 0, -1)
    return [piece, below, above, shift(below[:half], 0, 1), shift(above[half:], 0, -1)]


def ring_eight(piece):
    half = piece.shape[0] // 2
    result = [piece]
    below = above = piece
    for _ in range(3):
        below = shift(below, 1, 0)
        above = shift(above, -1, 0)
        result += [below, above]
    return result + [shift(below[:half], 1, 0), shift(above[half:], -1, 0)]


def body(queries, block_picks, span_keys, span_values, cache_keys, cache_values, out_weight):
    heads = lax.axis_size("head")
    head = lax.axis_index("head")
    ctx = lax.axis_index("ctx")
    part = head % GROUP
    kv = head // GROUP
    share = BLK // GROUP

    def cut(cache, first, rows):
        view = cache.reshape(BLOCKS, BLK, cache.shape[1])
        return lax.dynamic_slice(view, (0, part * share + first, kv * HD), (BLOCKS, rows, HD))

    pieces = []
    first = 0
    for sixteenths in SPLIT:
        rows = share * sixteenths // 16
        pieces.append(
            jnp.stack([cut(cache_keys, first, rows), cut(cache_values, first, rows)], axis=1)
        )
        first += rows
    gathered = lax.all_gather(pieces[0], "ctx", axis=0, tiled=True)
    by_x = jnp.concatenate(ring_four(pieces[1]), axis=0)
    by_z = jnp.concatenate(ring_eight(pieces[2]), axis=0)
    ring_a = ring_eight(by_x)
    ring_b = ring_four(by_z)
    ring_a = [jnp.concatenate(ring_a[:5], axis=0)] + ring_a[5:]

    swapped = swap(queries, 2)
    group_queries = [queries, swap(queries, 1), swapped, swap(swapped, 1)]
    group_picks = jnp.stack([block_picks] + [swap(block_picks, r) for r in range(1, GROUP)])
    picks = group_picks.reshape(GROUP, QB * SEL)
    owner, local = picks // BLOCKS, picks % BLOCKS
    dz = (owner // NX - ctx // NX) % NZ
    dx = (owner % NX - ctx % NX) % NX
    order_x = jnp.where(dx == 0, 0, jnp.where(dx == 3, 1, jnp.where(dx == 1, 2, 3)))
    order_z = jnp.where(dz == 0, 0, jnp.where(dz > NZ // 2, 2 * (NZ - dz) - 1, 2 * dz))
    order_z = jnp.where(dz == NZ // 2, NZ - 1, order_z)
    place_a = order_x * BLOCKS + local
    width_a = NX * BLOCKS
    upper_a = place_a >= width_a // 2
    array_a = jnp.where(
        order_z < 5, 0, jnp.where(order_z < 7, order_z - 4, jnp.where(upper_a, 4, 3))
    )
    index_a = jnp.where(
        order_z < 5,
        order_z * width_a + place_a,
        jnp.where((order_z == 7) & upper_a, place_a - width_a // 2, place_a),
    )
    place_b = order_z * BLOCKS + local
    width_b = NZ * BLOCKS
    upper_b = place_b >= width_b // 2
    array_b = jnp.where(order_x < 3, order_x, jnp.where(upper_b, 4, 3))
    index_b = jnp.where((order_x == 3) & upper_b, place_b - width_b // 2, place_b)
    where = jnp.stack(
        [jnp.zeros_like(picks), picks, array_a, index_a, array_b, index_b], axis=-1
    ).astype(jnp.int32)

    weights = [out_weight] + [None] * (heads - 1)
    for bits in range(2, heads, 2):
        weights[bits] = swap(out_weight, bits)
    for bits in range(0, heads, 2):
        weights[bits + 1] = swap(weights[bits], 1)

    near_state = near(queries, span_keys, span_values, kv[None])

    def far_of(first, second):
        return far(
            jnp.concatenate([where[first], where[second]], axis=0),
            [group_queries[first], group_queries[second]],
            [[gathered], ring_a, ring_b],
        )

    far_corner, far_chip = far_of(3, 2)
    for_chip = merge_two(far_chip, swap(far_corner, 1), QB)
    chip_parts = [swap(piece, 2) for piece in for_chip]
    far_core, far_own = far_of(1, 0)
    here = merge_here(far_own, swap(far_core, 1), near_state)
    attention = merge_last(here, chip_parts)

    share_rows = attention.shape[0] // heads
    parts = lax.all_to_all(
        attention.reshape(heads, share_rows, HD), "head", split_axis=0, concat_axis=0, tiled=True
    )
    return attention, project(head[None], parts, weights)


def solution(mesh):
    placed = (
        P("ctx", "head"),
        P("ctx", "head", None),
        P("ctx", None),
        P("ctx", None),
        P("ctx", None),
        P("ctx", None),
        P("head", None),
    )
    return jax.shard_map(
        body,
        mesh=mesh,
        in_specs=placed,
        out_specs=(P("ctx", "head"), P(("ctx", "head"), None)),
        check_vma=False,
    )
```

```python
import functools
import math

import jax
import jax.numpy as jnp
from jax import lax
from jax.experimental import pallas as pl
from jax.experimental.pallas import tpu as pltpu
from jax.sharding import PartitionSpec as P

HD = 128
GROUP = 4
BLK = 512
SEL = 4
QB = 4
BLOCKS = 8
NX = 4
NZ = 8
TAIL = 16
SCALE = math.log2(math.e) / math.sqrt(HD)
NEG = -1e30
F32 = jnp.float32
BF16 = jnp.bfloat16
SPLIT = (6, 4, 6)
VMEM_BYTES = 56 << 20


def dot_nt(a, b):
    return lax.dot_general(a, b, (((1,), (1,)), ((), ())), preferred_element_type=F32)


def dot_tn(a, b):
    return lax.dot_general(a, b, (((0,), (0,)), ((), ())), preferred_element_type=F32)


def rounded_top(raw):
    return (raw * SCALE).astype(BF16).astype(F32)


def near_kernel(kv_ref, q_ref, k_ref, v_ref, acc_ref, m_ref, l_ref):
    scores = dot_nt(k_ref[...], q_ref[...])
    keys = lax.broadcasted_iota(jnp.int32, (BLK, BLK), 0)
    rows = lax.broadcasted_iota(jnp.int32, (BLK, BLK), 1)
    scores = jnp.where(keys <= rows, scores, NEG)
    top = rounded_top(jnp.max(scores, axis=0, keepdims=True))
    weights = jnp.exp2(scores * SCALE - top)
    m_ref[0] = top
    l_ref[0] = jnp.sum(weights, axis=0, keepdims=True)
    acc_ref[0] = dot_tn(v_ref[...], weights.astype(BF16))


def state_shapes():
    return [
        jax.ShapeDtypeStruct((QB, HD, BLK), F32),
        jax.ShapeDtypeStruct((QB, 1, BLK), F32),
        jax.ShapeDtypeStruct((QB, 1, BLK), F32),
    ]


def near(queries, span_keys, span_values, kv):
    grid_spec = pltpu.PrefetchScalarGridSpec(
        num_scalar_prefetch=1,
        grid=(QB,),
        in_specs=[
            pl.BlockSpec((BLK, HD), lambda i, kv: (i, 0)),
            pl.BlockSpec((BLK, HD), lambda i, kv: (i, kv[0])),
            pl.BlockSpec((BLK, HD), lambda i, kv: (i, kv[0])),
        ],
        out_specs=[
            pl.BlockSpec((1, HD, BLK), lambda i, kv: (i, 0, 0)),
            pl.BlockSpec((1, 1, BLK), lambda i, kv: (i, 0, 0)),
            pl.BlockSpec((1, 1, BLK), lambda i, kv: (i, 0, 0)),
        ],
    )
    return pl.pallas_call(
        near_kernel,
        grid_spec=grid_spec,
        out_shape=state_shapes(),
        cost_estimate=pl.CostEstimate(
            flops=QB * 4 * BLK * BLK * HD, bytes_accessed=4 << 20, transcendentals=QB * BLK * BLK
        ),
        name="near",
    )(kv, queries, span_keys, span_values)


def pack_state(ref, i, out, top, total):
    ref[i, :HD, :] = out.astype(BF16)
    high = total.astype(BF16)
    low = (total - high.astype(F32)).astype(BF16)
    ref[i, HD:, :] = jnp.concatenate(
        [top.astype(BF16), high, low, jnp.zeros((TAIL - 3, out.shape[1]), BF16)], axis=0
    )


def unpack_state(ref, i):
    tail = ref[i, HD:, :].astype(F32)
    return ref[i, :HD, :].astype(F32), tail[0:1], tail[1:2] + tail[2:3]


def fetch(where_ref, sources, targets, picks, sem_of):
    def one(pick, carry):
        for part, arrays in enumerate(sources):
            array = where_ref[pick, 2 * part]
            index = where_ref[pick, 2 * part + 1]
            for number, source in enumerate(arrays):

                def start(source=source, part=part, index=index):
                    pltpu.make_async_copy(
                        source.at[index], targets[part].at[pick], sem_of(pick, part)
                    ).start()

                if len(arrays) == 1:
                    start()
                else:
                    pl.when(array == number)(start)
        return carry

    lax.fori_loop(0, picks, one, 0)


def split_refs(refs, counts):
    groups = []
    for count in counts:
        groups.append(refs[:count])
        refs = refs[count:]
    return groups, refs


def collect_kernel(where_ref, *refs, counts):
    sources, refs = split_refs(refs, counts)
    targets, sem = refs[:-1], refs[-1]
    picks = GROUP * QB * SEL
    fetch(where_ref, sources, targets, picks, lambda pick, part: sem.at[part])

    def wait(pick, carry):
        for part in range(len(counts)):

            def done(part=part):
                pltpu.make_async_copy(
                    sources[part][0].at[0], targets[part].at[pick], sem.at[part]
                ).wait()

            pl.when(where_ref[pick, 2 * part] >= 0)(done)
        return carry

    lax.fori_loop(0, picks, wait, 0)


def collect(where, parts):
    arrays = [array for part in parts for array in part]
    hbm = pl.BlockSpec(memory_space=pl.ANY)
    return pl.pallas_call(
        functools.partial(collect_kernel, counts=tuple(len(part) for part in parts)),
        in_specs=[pl.BlockSpec(memory_space=pltpu.SMEM)] + [hbm] * len(arrays),
        out_specs=[hbm] * len(parts),
        out_shape=[
            jax.ShapeDtypeStruct((GROUP * QB * SEL,) + part[0].shape[1:], BF16) for part in parts
        ],
        scratch_shapes=[pltpu.SemaphoreType.DMA((len(parts),))],
        compiler_params=pltpu.CompilerParams(vmem_limit_bytes=VMEM_BYTES),
        name="collect",
    )(where, *arrays)


def cut_kernel(place_ref, k_ref, v_ref, *refs, spans):
    out_refs, sem = refs[:-1], refs[-1]
    row0 = pl.multiple_of(place_ref[0], BLK // GROUP)
    col0 = pl.multiple_of(place_ref[1], HD)
    copies = []
    for out_ref, (block, blocks, first, rows) in zip(out_refs, spans):
        for which, source in enumerate((k_ref, v_ref)):
            copy = pltpu.make_async_copy(
                source.at[pl.ds(block, blocks), pl.ds(row0 + first, rows), pl.ds(col0, HD)],
                out_ref.at[:, which],
                sem.at[len(copies)],
            )
            copy.start()
            copies.append(copy)
    for copy in copies:
        copy.wait()


def cut(place, cache_keys, cache_values, spans):
    hbm = pl.BlockSpec(memory_space=pl.ANY)
    view = (BLOCKS, BLK, cache_keys.shape[1])
    return pl.pallas_call(
        functools.partial(cut_kernel, spans=spans),
        in_specs=[pl.BlockSpec(memory_space=pltpu.SMEM)] + [hbm] * 2,
        out_specs=[hbm] * len(spans),
        out_shape=[
            jax.ShapeDtypeStruct((blocks, 2, rows, HD), BF16) for _, blocks, _, rows in spans
        ],
        scratch_shapes=[pltpu.SemaphoreType.DMA((2 * len(spans),))],
        compiler_params=pltpu.CompilerParams(vmem_limit_bytes=VMEM_BYTES),
        name="cut",
    )(place, cache_keys.reshape(view), cache_values.reshape(view))


def far_kernel(where_ref, *refs, counts):
    q_refs, refs = refs[:2], refs[2:]
    sources, refs = split_refs(refs, counts)
    out_refs, refs = refs[:2], refs[2:]
    parts = len(counts)
    buffers, refs = refs[:parts], refs[parts:]
    score_refs, weight_refs, sems = refs[:2], refs[2:4], refs[4]
    fetch(where_ref, sources, buffers, 2 * QB * SEL, lambda pick, part: sems.at[pick // SEL, part])

    def joined(row, which):
        return jnp.concatenate(
            [buffers[part][row * SEL + j, which] for part in range(parts) for j in range(SEL)],
            axis=0,
        )

    def score(row, q_ref, i, score_ref):
        for part in range(parts):
            held = buffers[part].at[pl.ds(row * SEL, SEL)]
            pltpu.make_async_copy(held, held, sems.at[row, part]).wait()
        score_ref[...] = dot_nt(joined(row, 0), q_ref[pl.ds(i * BLK, BLK), :])

    def soften(score_ref, weight_ref):
        tops, totals = [], []
        for lane in range(0, BLK, HD):
            lanes = slice(lane, lane + HD)
            top = rounded_top(jnp.max(score_ref[:, lanes], axis=0, keepdims=True))
            total = jnp.zeros((8, HD), F32)
            for row in range(0, BLK, 64):
                weights = jnp.exp2(score_ref[row : row + 64, lanes] * SCALE - top)
                weight_ref[row : row + 64, lanes] = weights.astype(BF16)
                total = total + jnp.sum(weights.reshape(8, 8, HD), axis=0)
            tops.append(top)
            totals.append(jnp.sum(total, axis=0, keepdims=True))
        return jnp.concatenate(tops, axis=1), jnp.concatenate(totals, axis=1)

    def finish(row, weight_ref, out_ref, i, top, total):
        pack_state(out_ref, i, dot_tn(joined(row, 1), weight_ref[...]), top, total)

    for half in range(2):

        def pair(step, carry, half=half):
            units = [(half * QB + 2 * step + k, 2 * step + k) for k in range(2)]
            for k, (row, i) in enumerate(units):
                score(row, q_refs[half], i, score_refs[k])
            for k, (row, i) in enumerate(units):
                top, total = soften(score_refs[k], weight_refs[k])
                finish(row, weight_refs[k], out_refs[half], i, top, total)
            return carry

        lax.fori_loop(0, QB // 2, pair, 0)


def far(where, queries, parts):
    pay = HD + TAIL
    vmem = pl.BlockSpec(memory_space=pltpu.VMEM)
    arrays = [array for part in parts for array in part]
    return pl.pallas_call(
        functools.partial(far_kernel, counts=tuple(len(part) for part in parts)),
        in_specs=[pl.BlockSpec(memory_space=pltpu.SMEM)]
        + [vmem] * 2
        + [pl.BlockSpec(memory_space=pl.ANY)] * len(arrays),
        out_specs=[vmem] * 2,
        out_shape=[jax.ShapeDtypeStruct((QB, pay, BLK), BF16)] * 2,
        scratch_shapes=[
            pltpu.VMEM((2 * QB * SEL,) + part[0].shape[1:], BF16) for part in parts
        ]
        + [pltpu.VMEM((BLK, BLK), F32)] * 2
        + [pltpu.VMEM((BLK, BLK), BF16)] * 2
        + [pltpu.SemaphoreType.DMA((2 * QB, len(parts)))],
        compiler_params=pltpu.CompilerParams(vmem_limit_bytes=VMEM_BYTES),
        cost_estimate=pl.CostEstimate(
            flops=2 * QB * 4 * BLK * BLK * HD,
            bytes_accessed=5 << 20,
            transcendentals=2 * QB * BLK * BLK,
        ),
        name="far",
    )(where, *queries, *arrays)


def merge_two_kernel(a_ref, b_ref, *out_refs):
    per = QB // len(out_refs)
    for i in range(QB):
        acc_a, m_a, l_a = unpack_state(a_ref, i)
        acc_b, m_b, l_b = unpack_state(b_ref, i)
        top = jnp.maximum(m_a, m_b)
        f_a = jnp.exp2(m_a - top)
        f_b = jnp.exp2(m_b - top)
        pack_state(
            out_refs[i // per], i % per, f_a * acc_a + f_b * acc_b, top, f_a * l_a + f_b * l_b
        )


def merge_two(mine, other, pieces):
    vmem = pl.BlockSpec(memory_space=pltpu.VMEM)
    shape = (QB // pieces,) + mine.shape[1:]
    return pl.pallas_call(
        merge_two_kernel,
        in_specs=[vmem] * 2,
        out_specs=[vmem] * pieces,
        out_shape=[jax.ShapeDtypeStruct(shape, BF16)] * pieces,
        name="merge_two",
    )(mine, other)


def merge_here_kernel(a_ref, b_ref, acc_ref, m_ref, l_ref, acc_out, m_out, l_out):
    for i in range(QB):
        states = [unpack_state(a_ref, i), unpack_state(b_ref, i)]
        states.append((acc_ref[i], m_ref[i], l_ref[i]))
        top = functools.reduce(jnp.maximum, [m for _, m, _ in states])
        factors = [jnp.exp2(m - top) for _, m, _ in states]
        m_out[i] = top
        l_out[i] = sum(f * l for f, (_, _, l) in zip(factors, states))
        acc_out[i] = sum(f * acc for f, (acc, _, _) in zip(factors, states))


def merge_here(mine, core_part, near_state):
    vmem = pl.BlockSpec(memory_space=pltpu.VMEM)
    return pl.pallas_call(
        merge_here_kernel,
        in_specs=[vmem] * 5,
        out_specs=[vmem] * 3,
        out_shape=state_shapes(),
        name="merge_here",
    )(mine, core_part, *near_state)


def merge_last_kernel(acc_ref, m_ref, l_ref, *refs):
    chip_refs, out_ref = refs[:-1], refs[-1]
    per = QB // len(chip_refs)
    for i in range(QB):
        acc, m, l = unpack_state(chip_refs[i // per], i % per)
        top = jnp.maximum(m, m_ref[i])
        f_far = jnp.exp2(m - top)
        f_here = jnp.exp2(m_ref[i] - top)
        total = f_far * l + f_here * l_ref[i]
        out = (f_far * acc + f_here * acc_ref[i]) / total
        out_ref[i * BLK : (i + 1) * BLK, :] = out.T.astype(BF16)


def merge_last(here, chip_parts):
    vmem = pl.BlockSpec(memory_space=pltpu.VMEM)
    return pl.pallas_call(
        merge_last_kernel,
        in_specs=[vmem] * (3 + len(chip_parts)),
        out_specs=vmem,
        out_shape=jax.ShapeDtypeStruct((QB * BLK, HD), BF16),
        name="merge_last",
    )(*here, *chip_parts)


def project_kernel(head_ref, a_ref, *refs):
    w_refs, out_ref = refs[:-1], refs[-1]
    rows = jnp.concatenate([a_ref[head_ref[0] ^ i] for i in range(len(w_refs))], axis=1)
    tile = 512
    for first in range(0, out_ref.shape[1], tile):
        weight = jnp.concatenate([w_ref[:, first : first + tile] for w_ref in w_refs], axis=0)
        out_ref[:, first : first + tile] = jnp.dot(
            rows, weight, preferred_element_type=F32
        ).astype(BF16)


def project(head, parts, weights):
    vmem = pl.BlockSpec(memory_space=pltpu.VMEM)
    return pl.pallas_call(
        project_kernel,
        in_specs=[pl.BlockSpec(memory_space=pltpu.SMEM)] + [vmem] * (1 + len(weights)),
        out_specs=vmem,
        out_shape=jax.ShapeDtypeStruct((parts.shape[1], weights[0].shape[1]), BF16),
        compiler_params=pltpu.CompilerParams(vmem_limit_bytes=24 << 20),
        name="project",
    )(head, parts, *weights)


def shift(arrays, dz, dx):
    pairs = []
    for z in range(NZ):
        for x in range(NX):
            pairs.append((z * NX + x, (z + dz) % NZ * NX + (x + dx) % NX))
    return [lax.ppermute(array, "ctx", pairs) for array in arrays]


def swap(array, bits):
    return lax.ppermute(array, "head", [(h, h ^ bits) for h in range(lax.axis_size("head"))])


def after(value, *earlier):
    return lax.optimization_barrier((value, earlier))[0]


def join(*groups):
    return jnp.concatenate([array for group in groups for array in group], axis=0)


def body(queries, block_picks, span_keys, span_values, cache_keys, cache_values, out_weight):
    heads = lax.axis_size("head")
    head = lax.axis_index("head")
    ctx = lax.axis_index("ctx")
    part = head % GROUP
    kv = head // GROUP
    share = BLK // GROUP

    rows_s, rows_a, rows_b = [share * sixteenths // 16 for sixteenths in SPLIT]
    half = BLOCKS // 2
    spans = [(0, BLOCKS, 0, rows_s)]
    spans += [(first, half, rows_s + rows_a, rows_b) for first in (0, half)]
    spans += [(first, half, rows_s, rows_a) for first in (0, half)]
    place = jnp.stack([part * share, kv * HD]).astype(jnp.int32)
    piece_s, *rest = cut(place, cache_keys, cache_values, tuple(spans))
    gathered = lax.all_gather(piece_s, "ctx", axis=0, tiled=True)
    piece_b, piece_a = rest[:2], rest[2:]

    b1, b2 = shift(piece_b, 1, 0), shift(piece_b, -1, 0)
    a1, a2 = shift(piece_a, 0, 1), shift(piece_a, 0, -1)
    a3 = shift(a1[:1], 0, 1) + shift(a2[1:], 0, -1)
    b3, b4 = shift(b1, 1, 0), shift(b2, -1, 0)
    wide_a = [join(piece_a, a1), join(a2, a3)]
    wide_a = after(wide_a, b1, b2)
    c1, c2 = shift(wide_a, 1, 0), shift(wide_a, -1, 0)
    b5, b6 = shift(b3, 1, 0), shift(b4, -1, 0)
    wide_b_low = join(piece_b, b1, b2, b3)
    d1_low, d2_low = shift([wide_b_low], 0, 1), shift([wide_b_low], 0, -1)
    b7 = shift(b5[:1], 1, 0) + shift(b6[1:], -1, 0)
    wide_b_high = join(b4, b5, b6, b7)
    d1_high, d2_high = shift([wide_b_high], 0, 1), shift([wide_b_high], 0, -1)

    queries_early, picks_early, weight_early = after(
        (queries, block_picks, out_weight), b3, b4
    )
    queries_chip = swap(queries_early, 2)
    picks_chip = swap(picks_early, 2)
    weights = [out_weight] + [None] * (heads - 1)
    for bits in range(2, heads, 2):
        weights[bits] = swap(weight_early, bits)
    near_queries = after(queries, b7)
    near_state = near(near_queries, span_keys, span_values, kv[None])

    c1, c2 = after((c1, c2), wide_b_high, *near_state)
    c3, c4 = shift(c1, 1, 0), shift(c2, -1, 0)
    queries_pair, picks_pair, weights_even = after(
        ([queries, queries_chip], jnp.stack([block_picks, picks_chip]), weights[::2]), c1, c2
    )
    picks_pair = [picks_pair, swap(picks_pair, 1)]
    group_queries = [
        queries,
        swap(queries_pair[0], 1),
        queries_chip,
        swap(queries_pair[1], 1),
    ]
    group_picks = [picks_pair[0][0], picks_pair[1][0], picks_pair[0][1], picks_pair[1][1]]
    d3 = shift(d1_low, 0, 1)
    c5, c6 = shift(c3, 1, 0), shift(c4, -1, 0)
    d3 += shift(d2_high, 0, -1)
    for i, bits in enumerate(range(0, heads, 2)):
        weights[bits + 1] = swap(weights_even[i], 1)
    c7 = shift(c5[:1], 1, 0) + shift(c6[1:], -1, 0)

    picks = jnp.stack(group_picks).reshape(GROUP, QB * SEL)
    owner, local = picks // BLOCKS, picks % BLOCKS
    dz = (owner // NX - ctx // NX) % NZ
    dx = (owner % NX - ctx % NX) % NX
    order_x = jnp.where(dx == 0, 0, jnp.where(dx == 3, 1, jnp.where(dx == 1, 2, 3)))
    order_z = jnp.where(dz == 0, 0, jnp.where(dz > NZ // 2, 2 * (NZ - dz) - 1, 2 * dz))
    order_z = jnp.where(dz == NZ // 2, NZ - 1, order_z)
    place_a = order_x * BLOCKS + local
    half_a = NX * BLOCKS // 2
    upper_a = (place_a >= half_a).astype(jnp.int32)
    far_a = order_z == NZ - 1
    place_b = order_z * BLOCKS + local
    half_b = NZ * BLOCKS // 2
    upper_b = (place_b >= half_b).astype(jnp.int32)
    far_b = order_x == NX - 1
    index_a = place_a - half_a * upper_a
    index_b = place_b - half_b * upper_b
    early = jnp.stack(
        [
            jnp.where(far_a, -1, 2 * order_z + upper_a),
            index_a,
            jnp.where(far_b, -1, 2 * order_x + upper_b),
            index_b,
        ],
        axis=-1,
    ).reshape(GROUP * QB * SEL, 4)
    order = jnp.arange(GROUP * QB * SEL, dtype=jnp.int32).reshape(GROUP, QB * SEL)
    late = jnp.stack(
        [
            jnp.zeros_like(picks),
            picks,
            jnp.where(far_a, 1 + upper_a, 0),
            jnp.where(far_a, index_a, order),
            jnp.where(far_b, 1 + upper_b, 0),
            jnp.where(far_b, index_b, order),
        ],
        axis=-1,
    ).astype(jnp.int32)
    held_a = [*wide_a, *c1, *c2, *c3, *c4, *c5, *c6]
    held_b = [wide_b_low, wide_b_high, *d1_low, *d1_high, *d2_low, *d2_high]
    early_a, early_b = collect(early.astype(jnp.int32), [held_a, held_b])

    def far_of(first, second, where):
        return far(
            jnp.concatenate([where[first], where[second]], axis=0),
            [group_queries[first], group_queries[second]],
            [[gathered], [early_a, *c7], [early_b, *d3]],
        )

    far_corner, far_chip = far_of(3, 2, late)
    for_chip = merge_two(far_chip, swap(far_corner, 1), QB)
    chip_parts = [swap(piece, 2) for piece in for_chip]
    far_core, far_own = far_of(1, 0, after(late, *for_chip))
    here = merge_here(far_own, swap(far_core, 1), near_state)
    attention = merge_last(here, chip_parts)

    share_rows = attention.shape[0] // heads
    parts = lax.all_to_all(
        attention.reshape(heads, share_rows, HD), "head", split_axis=0, concat_axis=0, tiled=True
    )
    return attention, project(head[None], parts, weights)


def solution(mesh):
    placed = (
        P("ctx", "head"),
        P("ctx", "head", None),
        P("ctx", None),
        P("ctx", None),
        P("ctx", None),
        P("ctx", None),
        P("head", None),
    )
    return jax.shard_map(
        body,
        mesh=mesh,
        in_specs=placed,
        out_specs=(P("ctx", "head"), P(("ctx", "head"), None)),
        check_vma=False,
    )
```

```python
import functools
import math

import jax
import jax.numpy as jnp
from jax import lax
from jax.experimental import pallas as pl
from jax.experimental.pallas import tpu as pltpu
from jax.sharding import PartitionSpec as P

HD = 128
GROUP = 4
BLK = 512
SEL = 4
QB = 4
BLOCKS = 8
NX = 4
NZ = 8
TAIL = 16
SCALE = math.log2(math.e) / math.sqrt(HD)
NEG = -1e30
F32 = jnp.float32
BF16 = jnp.bfloat16
SPLIT = (4, 6, 6)
VMEM_BYTES = 56 << 20


def dot_nt(a, b):
    return lax.dot_general(a, b, (((1,), (1,)), ((), ())), preferred_element_type=F32)


def dot_tn(a, b):
    return lax.dot_general(a, b, (((0,), (0,)), ((), ())), preferred_element_type=F32)


def rounded_top(raw):
    return (raw * SCALE).astype(BF16).astype(F32)


def near_kernel(kv_ref, q_ref, k_ref, v_ref, acc_ref, m_ref, l_ref):
    scores = dot_nt(k_ref[...], q_ref[...])
    keys = lax.broadcasted_iota(jnp.int32, (BLK, BLK), 0)
    rows = lax.broadcasted_iota(jnp.int32, (BLK, BLK), 1)
    scores = jnp.where(keys <= rows, scores, NEG)
    top = rounded_top(jnp.max(scores, axis=0, keepdims=True))
    weights = jnp.exp2(scores * SCALE - top)
    m_ref[0] = top
    l_ref[0] = jnp.sum(weights, axis=0, keepdims=True)
    acc_ref[0] = dot_tn(v_ref[...], weights.astype(BF16))


def state_shapes():
    return [
        jax.ShapeDtypeStruct((QB, HD, BLK), F32),
        jax.ShapeDtypeStruct((QB, 1, BLK), F32),
        jax.ShapeDtypeStruct((QB, 1, BLK), F32),
    ]


def near(queries, span_keys, span_values, kv):
    grid_spec = pltpu.PrefetchScalarGridSpec(
        num_scalar_prefetch=1,
        grid=(QB,),
        in_specs=[
            pl.BlockSpec((BLK, HD), lambda i, kv: (i, 0)),
            pl.BlockSpec((BLK, HD), lambda i, kv: (i, kv[0])),
            pl.BlockSpec((BLK, HD), lambda i, kv: (i, kv[0])),
        ],
        out_specs=[
            pl.BlockSpec((1, HD, BLK), lambda i, kv: (i, 0, 0)),
            pl.BlockSpec((1, 1, BLK), lambda i, kv: (i, 0, 0)),
            pl.BlockSpec((1, 1, BLK), lambda i, kv: (i, 0, 0)),
        ],
    )
    return pl.pallas_call(
        near_kernel,
        grid_spec=grid_spec,
        out_shape=state_shapes(),
        cost_estimate=pl.CostEstimate(
            flops=QB * 4 * BLK * BLK * HD, bytes_accessed=4 << 20, transcendentals=QB * BLK * BLK
        ),
        name="near",
    )(kv, queries, span_keys, span_values)


def pack_state(ref, i, out, top, total):
    ref[i, :HD, :] = out.astype(BF16)
    high = total.astype(BF16)
    low = (total - high.astype(F32)).astype(BF16)
    ref[i, HD:, :] = jnp.concatenate(
        [top.astype(BF16), high, low, jnp.zeros((TAIL - 3, out.shape[1]), BF16)], axis=0
    )


def unpack_state(ref, i):
    tail = ref[i, HD:, :].astype(F32)
    return ref[i, :HD, :].astype(F32), tail[0:1], tail[1:2] + tail[2:3]


def far_kernel(where_ref, *refs, arrays):
    q_refs, refs = refs[:2], refs[2:]
    whole_ref, refs = refs[0], refs[1:]
    sources, refs = (refs[:arrays], refs[arrays : 2 * arrays]), refs[2 * arrays :]
    piece_refs, whole_out_ref, refs = refs[:QB], refs[QB], refs[QB + 1 :]
    parts = 1 + len(sources)
    buffers, refs = refs[:parts], refs[parts:]
    score_refs, weight_refs, sems = refs[:2], refs[2:4], refs[4]

    def fetch(pick, carry):
        unit = pick // SEL
        pltpu.make_async_copy(
            whole_ref.at[where_ref[pick, 0]], buffers[0].at[pick], sems.at[unit, 0]
        ).start()
        array, index = where_ref[pick, 1], where_ref[pick, 2]
        for number in range(arrays):

            def start(number=number):
                for part in range(1, parts):
                    pltpu.make_async_copy(
                        sources[part - 1][number].at[index],
                        buffers[part].at[pick],
                        sems.at[unit, part],
                    ).start()

            pl.when(array == number)(start)
        return carry

    lax.fori_loop(0, 2 * QB * SEL, fetch, 0)

    def joined(row, which):
        return jnp.concatenate(
            [buffers[part][row * SEL + j, which] for part in range(parts) for j in range(SEL)],
            axis=0,
        )

    def score(row, q_ref, i, score_ref):
        for part in range(parts):
            held = buffers[part].at[pl.ds(row * SEL, SEL)]
            pltpu.make_async_copy(held, held, sems.at[row, part]).wait()
        score_ref[...] = dot_nt(joined(row, 0), q_ref[pl.ds(i * BLK, BLK), :])

    def soften(score_ref, weight_ref):
        tops, totals = [], []
        for lane in range(0, BLK, HD):
            lanes = slice(lane, lane + HD)
            top = rounded_top(jnp.max(score_ref[:, lanes], axis=0, keepdims=True))
            total = jnp.zeros((8, HD), F32)
            for row in range(0, BLK, 64):
                weights = jnp.exp2(score_ref[row : row + 64, lanes] * SCALE - top)
                weight_ref[row : row + 64, lanes] = weights.astype(BF16)
                total = total + jnp.sum(weights.reshape(8, 8, HD), axis=0)
            tops.append(top)
            totals.append(jnp.sum(total, axis=0, keepdims=True))
        return jnp.concatenate(tops, axis=1), jnp.concatenate(totals, axis=1)

    def finish(row, weight_ref, out_ref, i, top, total):
        pack_state(out_ref, i, dot_tn(joined(row, 1), weight_ref[...]), top, total)

    for first in range(0, 2 * QB, 2):
        units = [first, first + 1]
        for k, row in enumerate(units):
            score(row, q_refs[row // QB], row % QB, score_refs[k])
        for k, row in enumerate(units):
            top, total = soften(score_refs[k], weight_refs[k])
            if row < QB:
                finish(row, weight_refs[k], piece_refs[row], 0, top, total)
            else:
                finish(row, weight_refs[k], whole_out_ref, row % QB, top, total)


def far(where, queries, whole, x_parts):
    pay = HD + TAIL
    vmem = pl.BlockSpec(memory_space=pltpu.VMEM)
    hbm = pl.BlockSpec(memory_space=pl.ANY)
    arrays = [array for part in x_parts for array in part]
    shapes = [whole.shape[1:]] + [part[0].shape[1:] for part in x_parts]
    return pl.pallas_call(
        functools.partial(far_kernel, arrays=len(x_parts[0])),
        in_specs=[pl.BlockSpec(memory_space=pltpu.SMEM)]
        + [vmem] * 2
        + [hbm] * (1 + len(arrays)),
        out_specs=[vmem] * (QB + 1),
        out_shape=[jax.ShapeDtypeStruct((1, pay, BLK), BF16)] * QB
        + [jax.ShapeDtypeStruct((QB, pay, BLK), BF16)],
        scratch_shapes=[pltpu.VMEM((2 * QB * SEL,) + shape, BF16) for shape in shapes]
        + [pltpu.VMEM((BLK, BLK), F32)] * 2
        + [pltpu.VMEM((BLK, BLK), BF16)] * 2
        + [pltpu.SemaphoreType.DMA((2 * QB, len(shapes)))],
        compiler_params=pltpu.CompilerParams(vmem_limit_bytes=VMEM_BYTES),
        cost_estimate=pl.CostEstimate(
            flops=8 * 2 * QB * 4 * BLK * BLK * HD,
            bytes_accessed=5 << 20,
            transcendentals=2 * QB * BLK * BLK,
        ),
        name="far",
    )(where, *queries, whole, *arrays)


def merge_two_kernel(a_ref, *refs):
    b_refs, out_refs = refs[:QB], refs[QB:]
    per = QB // len(out_refs)
    for i in range(QB):
        acc_a, m_a, l_a = unpack_state(a_ref, i)
        acc_b, m_b, l_b = unpack_state(b_refs[i], 0)
        top = jnp.maximum(m_a, m_b)
        f_a = jnp.exp2(m_a - top)
        f_b = jnp.exp2(m_b - top)
        pack_state(
            out_refs[i // per], i % per, f_a * acc_a + f_b * acc_b, top, f_a * l_a + f_b * l_b
        )


def merge_two(mine, others, pieces):
    vmem = pl.BlockSpec(memory_space=pltpu.VMEM)
    shape = (QB // pieces,) + mine.shape[1:]
    return pl.pallas_call(
        merge_two_kernel,
        in_specs=[vmem] * (1 + QB),
        out_specs=[vmem] * pieces,
        out_shape=[jax.ShapeDtypeStruct(shape, BF16)] * pieces,
        name="merge_two",
    )(mine, *others)


def merge_last_kernel(a_ref, *refs):
    core_refs, refs = refs[:QB], refs[QB:]
    (acc_ref, m_ref, l_ref), chip_refs, out_ref = refs[:3], refs[3:-1], refs[-1]
    per = QB // len(chip_refs)
    for i in range(QB):
        states = [unpack_state(a_ref, i), unpack_state(core_refs[i], 0)]
        states.append(unpack_state(chip_refs[i // per], i % per))
        states.append((acc_ref[i], m_ref[i], l_ref[i]))
        top = functools.reduce(jnp.maximum, [m for _, m, _ in states])
        factors = [jnp.exp2(m - top) for _, m, _ in states]
        total = sum(f * l for f, (_, _, l) in zip(factors, states))
        factors = [f / total for f in factors]
        out = sum(f * acc for f, (acc, _, _) in zip(factors, states))
        out_ref[i * BLK : (i + 1) * BLK, :] = out.T.astype(BF16)


def merge_last(mine, core_parts, near_state, chip_parts):
    vmem = pl.BlockSpec(memory_space=pltpu.VMEM)
    arrays = [mine, *core_parts, *near_state, *chip_parts]
    return pl.pallas_call(
        merge_last_kernel,
        in_specs=[vmem] * len(arrays),
        out_specs=vmem,
        out_shape=jax.ShapeDtypeStruct((QB * BLK, HD), BF16),
        name="merge_last",
    )(*arrays)


def project_kernel(head_ref, a_ref, *refs):
    w_refs, out_ref = refs[:-1], refs[-1]
    rows = jnp.concatenate([a_ref[head_ref[0] ^ i] for i in range(len(w_refs))], axis=1)
    tile = 512
    for first in range(0, out_ref.shape[1], tile):
        weight = jnp.concatenate([w_ref[:, first : first + tile] for w_ref in w_refs], axis=0)
        out_ref[:, first : first + tile] = jnp.dot(
            rows, weight, preferred_element_type=F32
        ).astype(BF16)


def project(head, parts, weights):
    vmem = pl.BlockSpec(memory_space=pltpu.VMEM)
    return pl.pallas_call(
        project_kernel,
        in_specs=[pl.BlockSpec(memory_space=pltpu.SMEM)] + [vmem] * (1 + len(weights)),
        out_specs=vmem,
        out_shape=jax.ShapeDtypeStruct((parts.shape[1], weights[0].shape[1]), BF16),
        compiler_params=pltpu.CompilerParams(vmem_limit_bytes=24 << 20),
        name="project",
    )(head, parts, *weights)


def shift(arrays, dz, dx):
    pairs = []
    for z in range(NZ):
        for x in range(NX):
            pairs.append((z * NX + x, (z + dz) % NZ * NX + (x + dx) % NX))
    return [lax.ppermute(array, "ctx", pairs) for array in arrays]


def swap(array, bits):
    return lax.ppermute(array, "head", [(h, h ^ bits) for h in range(lax.axis_size("head"))])


def after(value, *earlier):
    return lax.optimization_barrier((value, earlier))[0]


def spread_x(array):
    half = array.shape[0] // 2
    halves = [array[:half], array[half:]]
    below, above = shift(halves, 0, 1), shift(halves, 0, -1)

    def rest(*earlier):
        low, high = after((below[0], above[1]), *earlier)
        return shift([low], 0, 1) + shift([high], 0, -1)

    return [array, *below, *above], rest


def body(queries, block_picks, span_keys, span_values, cache_keys, cache_values, out_weight):
    heads = lax.axis_size("head")
    head = lax.axis_index("head")
    ctx = lax.axis_index("ctx")
    part = head % GROUP
    kv = head // GROUP
    share = BLK // GROUP
    columns = [[z * NX + x for z in range(NZ)] for x in range(NX)]

    def cut(first, rows):
        pieces = []
        for cache in (cache_keys, cache_values):
            view = cache.reshape(BLOCKS, BLK, cache.shape[1])
            pieces.append(
                lax.dynamic_slice(view, (0, part * share + first, kv * HD), (BLOCKS, rows, HD))
            )
        return jnp.stack(pieces, axis=1)

    rows = [share * sixteenths // 16 for sixteenths in SPLIT]
    columns_0, columns_1 = [
        lax.all_gather(
            cut(first, count), "ctx", axis=0, tiled=True, axis_index_groups=columns
        )
        for first, count in ((0, rows[0]), (rows[0], rows[1]))
    ]
    whole = lax.all_gather(cut(rows[0] + rows[1], rows[2]), "ctx", axis=0, tiled=True)
    x_part_0, rest_0 = spread_x(columns_0)
    x_part_1, rest_1 = spread_x(columns_1)
    x_part_0 = x_part_0 + rest_0()

    queries_chip = swap(queries, 2)
    picks_chip = swap(block_picks, 2)
    weights = [out_weight] + [None] * (heads - 1)
    for bits in range(2, heads, 2):
        weights[bits] = swap(out_weight, bits)
    near_state = near(after(queries, columns_1), span_keys, span_values, kv[None])
    x_part_1 = x_part_1 + rest_1(*near_state)
    queries_pair, picks_pair, weights_even = after(
        ([queries, queries_chip], jnp.stack([block_picks, picks_chip]), weights[::2]), *x_part_0
    )
    group_queries = [queries, swap(queries_pair[0], 1), queries_chip, swap(queries_pair[1], 1)]
    picks_core = swap(picks_pair, 1)
    group_picks = [picks_pair[0], picks_core[0], picks_pair[1], picks_core[1]]
    for i, bits in enumerate(range(0, heads, 2)):
        weights[bits + 1] = swap(weights_even[i], 1)

    picks = jnp.stack(group_picks).reshape(GROUP, QB * SEL)
    owner, local = picks // BLOCKS, picks % BLOCKS
    dx = (owner % NX - ctx % NX) % NX
    place = owner // NX * BLOCKS + local
    half = NZ * BLOCKS // 2
    upper = (place >= half).astype(jnp.int32)
    first_array = jnp.where(dx == 3, 1, jnp.where(dx == 1, 3, 5))
    where = jnp.stack(
        [
            picks,
            jnp.where(dx == 0, 0, first_array + upper),
            jnp.where(dx == 0, place, place - half * upper),
        ],
        axis=-1,
    ).astype(jnp.int32)

    def far_of(first, second, where):
        return far(
            jnp.concatenate([where[first], where[second]], axis=0),
            [group_queries[first], group_queries[second]],
            whole,
            [x_part_0, x_part_1],
        )

    where, group_queries, weights = lax.optimization_barrier((where, group_queries, weights))
    *far_corner, far_chip = far_of(3, 2, where)
    for_chip = merge_two(far_chip, [swap(piece, 1) for piece in far_corner], 2)
    chip_parts = [swap(piece, 2) for piece in for_chip]
    *far_core, far_own = far_of(1, 0, after(where, *for_chip))
    core_parts = [swap(piece, 1) for piece in after(far_core, *chip_parts)]
    attention = merge_last(far_own, core_parts, near_state, chip_parts)

    share_rows = attention.shape[0] // heads
    parts = lax.all_to_all(
        attention.reshape(heads, share_rows, HD), "head", split_axis=0, concat_axis=0, tiled=True
    )
    return attention, project(head[None], parts, weights)


def solution(mesh):
    placed = (
        P("ctx", "head"),
        P("ctx", "head", None),
        P("ctx", None),
        P("ctx", None),
        P("ctx", None),
        P("ctx", None),
        P("head", None),
    )
    return jax.shard_map(
        body,
        mesh=mesh,
        in_specs=placed,
        out_specs=(P("ctx", "head"), P(("ctx", "head"), None)),
        check_vma=False,
    )
```

```python
import functools
import math

import jax
import jax.numpy as jnp
from jax import lax
from jax.experimental import pallas as pl
from jax.experimental.pallas import tpu as pltpu
from jax.sharding import PartitionSpec as P

HD = 128
GROUP = 4
BLK = 512
SEL = 4
QB = 4
BLOCKS = 8
TAIL = 16
SCALE = math.log2(math.e) / math.sqrt(HD)
NEG = -1e30
F32 = jnp.float32
BF16 = jnp.bfloat16
VMEM_BYTES = 56 << 20


def dot_nt(a, b):
    return lax.dot_general(a, b, (((1,), (1,)), ((), ())), preferred_element_type=F32)


def dot_tn(a, b):
    return lax.dot_general(a, b, (((0,), (0,)), ((), ())), preferred_element_type=F32)


def rounded_top(raw):
    return (raw * SCALE).astype(BF16).astype(F32)


def near_kernel(kv_ref, q_ref, k_ref, v_ref, acc_ref, m_ref, l_ref):
    scores = dot_nt(k_ref[...], q_ref[...])
    keys = lax.broadcasted_iota(jnp.int32, (BLK, BLK), 0)
    rows = lax.broadcasted_iota(jnp.int32, (BLK, BLK), 1)
    scores = jnp.where(keys <= rows, scores, NEG)
    top = rounded_top(jnp.max(scores, axis=0, keepdims=True))
    weights = jnp.exp2(scores * SCALE - top)
    m_ref[0] = top
    l_ref[0] = jnp.sum(weights, axis=0, keepdims=True)
    acc_ref[0] = dot_tn(v_ref[...], weights.astype(BF16))


def state_shapes():
    return [
        jax.ShapeDtypeStruct((QB, HD, BLK), F32),
        jax.ShapeDtypeStruct((QB, 1, BLK), F32),
        jax.ShapeDtypeStruct((QB, 1, BLK), F32),
    ]


def near(queries, span_keys, span_values, kv):
    grid_spec = pltpu.PrefetchScalarGridSpec(
        num_scalar_prefetch=1,
        grid=(QB,),
        in_specs=[
            pl.BlockSpec((BLK, HD), lambda i, kv: (i, 0)),
            pl.BlockSpec((BLK, HD), lambda i, kv: (i, kv[0])),
            pl.BlockSpec((BLK, HD), lambda i, kv: (i, kv[0])),
        ],
        out_specs=[
            pl.BlockSpec((1, HD, BLK), lambda i, kv: (i, 0, 0)),
            pl.BlockSpec((1, 1, BLK), lambda i, kv: (i, 0, 0)),
            pl.BlockSpec((1, 1, BLK), lambda i, kv: (i, 0, 0)),
        ],
    )
    return pl.pallas_call(
        near_kernel,
        grid_spec=grid_spec,
        out_shape=state_shapes(),
        cost_estimate=pl.CostEstimate(
            flops=QB * 4 * BLK * BLK * HD, bytes_accessed=4 << 20, transcendentals=QB * BLK * BLK
        ),
        name="near",
    )(kv, queries, span_keys, span_values)


def pack_state(ref, i, out, top, total):
    ref[i, :HD, :] = out.astype(BF16)
    high = total.astype(BF16)
    low = (total - high.astype(F32)).astype(BF16)
    ref[i, HD:, :] = jnp.concatenate(
        [top.astype(BF16), high, low, jnp.zeros((TAIL - 3, out.shape[1]), BF16)], axis=0
    )


def unpack_state(ref, i):
    tail = ref[i, HD:, :].astype(F32)
    return ref[i, :HD, :].astype(F32), tail[0:1], tail[1:2] + tail[2:3]


def far_kernel(picks_ref, *refs):
    q_refs, whole_ref, refs = refs[:2], refs[2], refs[3:]
    piece_refs, whole_out_ref, refs = refs[:QB], refs[QB], refs[QB + 1 :]
    buffer, score_refs, weight_refs, sems = refs[0], refs[1:3], refs[3:5], refs[5]
    for pick in range(2 * QB * SEL):
        pltpu.make_async_copy(
            whole_ref.at[picks_ref[pick]], buffer.at[pick], sems.at[pick // SEL]
        ).start()

    def joined(row, which):
        return jnp.concatenate(
            [buffer[row * SEL + j, which] for j in range(SEL)], axis=0
        )

    def score(row, q_ref, i, score_ref):
        held = buffer.at[pl.ds(row * SEL, SEL)]
        pltpu.make_async_copy(held, held, sems.at[row]).wait()
        score_ref[...] = dot_nt(joined(row, 0), q_ref[pl.ds(i * BLK, BLK), :])

    def soften(score_ref, weight_ref):
        tops, totals = [], []
        for lane in range(0, BLK, HD):
            lanes = slice(lane, lane + HD)
            top = rounded_top(jnp.max(score_ref[:, lanes], axis=0, keepdims=True))
            total = jnp.zeros((8, HD), F32)
            for row in range(0, BLK, 64):
                weights = jnp.exp2(score_ref[row : row + 64, lanes] * SCALE - top)
                weight_ref[row : row + 64, lanes] = weights.astype(BF16)
                total = total + jnp.sum(weights.reshape(8, 8, HD), axis=0)
            tops.append(top)
            totals.append(jnp.sum(total, axis=0, keepdims=True))
        return jnp.concatenate(tops, axis=1), jnp.concatenate(totals, axis=1)

    def finish(row, weight_ref, out_ref, i, top, total):
        pack_state(out_ref, i, dot_tn(joined(row, 1), weight_ref[...]), top, total)

    for first in range(0, 2 * QB, 2):
        units = [first, first + 1]
        for k, row in enumerate(units):
            score(row, q_refs[row // QB], row % QB, score_refs[k])
        for k, row in enumerate(units):
            top, total = soften(score_refs[k], weight_refs[k])
            if row < QB:
                finish(row, weight_refs[k], piece_refs[row], 0, top, total)
            else:
                finish(row, weight_refs[k], whole_out_ref, row % QB, top, total)


def far(picks, queries, whole):
    pay = HD + TAIL
    vmem = pl.BlockSpec(memory_space=pltpu.VMEM)
    return pl.pallas_call(
        far_kernel,
        in_specs=[pl.BlockSpec(memory_space=pltpu.SMEM)]
        + [vmem] * 2
        + [pl.BlockSpec(memory_space=pl.ANY)],
        out_specs=[vmem] * (QB + 1),
        out_shape=[jax.ShapeDtypeStruct((1, pay, BLK), BF16)] * QB
        + [jax.ShapeDtypeStruct((QB, pay, BLK), BF16)],
        scratch_shapes=[pltpu.VMEM((2 * QB * SEL,) + whole.shape[1:], BF16)]
        + [pltpu.VMEM((BLK, BLK), F32)] * 2
        + [pltpu.VMEM((BLK, BLK), BF16)] * 2
        + [pltpu.SemaphoreType.DMA((2 * QB,))],
        compiler_params=pltpu.CompilerParams(vmem_limit_bytes=VMEM_BYTES),
        cost_estimate=pl.CostEstimate(
            flops=8 * 2 * QB * 4 * BLK * BLK * HD,
            bytes_accessed=5 << 20,
            transcendentals=2 * QB * BLK * BLK,
        ),
        name="far",
    )(picks, *queries, whole)


def merge_two_kernel(a_ref, *refs):
    b_refs, out_refs = refs[:QB], refs[QB:]
    per = QB // len(out_refs)
    for i in range(QB):
        acc_a, m_a, l_a = unpack_state(a_ref, i)
        acc_b, m_b, l_b = unpack_state(b_refs[i], 0)
        top = jnp.maximum(m_a, m_b)
        f_a = jnp.exp2(m_a - top)
        f_b = jnp.exp2(m_b - top)
        pack_state(
            out_refs[i // per], i % per, f_a * acc_a + f_b * acc_b, top, f_a * l_a + f_b * l_b
        )


def merge_two(mine, others, pieces):
    vmem = pl.BlockSpec(memory_space=pltpu.VMEM)
    shape = (QB // pieces,) + mine.shape[1:]
    return pl.pallas_call(
        merge_two_kernel,
        in_specs=[vmem] * (1 + QB),
        out_specs=[vmem] * pieces,
        out_shape=[jax.ShapeDtypeStruct(shape, BF16)] * pieces,
        name="merge_two",
    )(mine, *others)


def merge_last_kernel(a_ref, *refs):
    core_refs, refs = refs[:QB], refs[QB:]
    (acc_ref, m_ref, l_ref), chip_refs, out_ref = refs[:3], refs[3:-1], refs[-1]
    per = QB // len(chip_refs)
    for i in range(QB):
        states = [unpack_state(a_ref, i), unpack_state(core_refs[i], 0)]
        states.append(unpack_state(chip_refs[i // per], i % per))
        states.append((acc_ref[i], m_ref[i], l_ref[i]))
        top = functools.reduce(jnp.maximum, [m for _, m, _ in states])
        factors = [jnp.exp2(m - top) for _, m, _ in states]
        total = sum(f * l for f, (_, _, l) in zip(factors, states))
        factors = [f / total for f in factors]
        out = sum(f * acc for f, (acc, _, _) in zip(factors, states))
        out_ref[i * BLK : (i + 1) * BLK, :] = out.T.astype(BF16)


def merge_last(mine, core_parts, near_state, chip_parts):
    vmem = pl.BlockSpec(memory_space=pltpu.VMEM)
    arrays = [mine, *core_parts, *near_state, *chip_parts]
    return pl.pallas_call(
        merge_last_kernel,
        in_specs=[vmem] * len(arrays),
        out_specs=vmem,
        out_shape=jax.ShapeDtypeStruct((QB * BLK, HD), BF16),
        name="merge_last",
    )(*arrays)


def project_kernel(head_ref, a_ref, *refs):
    w_refs, out_ref = refs[:-1], refs[-1]
    rows = jnp.concatenate([a_ref[head_ref[0] ^ i] for i in range(len(w_refs))], axis=1)
    tile = 512
    for first in range(0, out_ref.shape[1], tile):
        weight = jnp.concatenate([w_ref[:, first : first + tile] for w_ref in w_refs], axis=0)
        out_ref[:, first : first + tile] = jnp.dot(
            rows, weight, preferred_element_type=F32
        ).astype(BF16)


def project(head, parts, weights):
    vmem = pl.BlockSpec(memory_space=pltpu.VMEM)
    return pl.pallas_call(
        project_kernel,
        in_specs=[pl.BlockSpec(memory_space=pltpu.SMEM)] + [vmem] * (1 + len(weights)),
        out_specs=vmem,
        out_shape=jax.ShapeDtypeStruct((parts.shape[1], weights[0].shape[1]), BF16),
        compiler_params=pltpu.CompilerParams(vmem_limit_bytes=24 << 20),
        name="project",
    )(head, parts, *weights)


def swap(array, bits):
    return lax.ppermute(array, "head", [(h, h ^ bits) for h in range(lax.axis_size("head"))])


def after(value, *earlier):
    return lax.optimization_barrier((value, earlier))[0]


def body(queries, block_picks, span_keys, span_values, cache_keys, cache_values, out_weight):
    heads = lax.axis_size("head")
    head = lax.axis_index("head")
    part = head % GROUP
    kv = head // GROUP
    share = BLK // GROUP

    pieces = []
    for cache in (cache_keys, cache_values):
        view = cache.reshape(BLOCKS, BLK, cache.shape[1])
        pieces.append(lax.dynamic_slice(view, (0, part * share, kv * HD), (BLOCKS, share, HD)))
    whole = lax.all_gather(jnp.stack(pieces, axis=1), "ctx", axis=0, tiled=True)

    queries_chip = swap(queries, 2)
    picks_chip = swap(block_picks, 2)
    weights = [out_weight] + [None] * (heads - 1)
    for bits in range(2, heads, 2):
        weights[bits] = swap(out_weight, bits)
    near_state = near(queries, span_keys, span_values, kv[None])
    queries_pair = [queries, queries_chip]
    picks_pair = jnp.stack([block_picks, picks_chip])
    group_queries = [queries, swap(queries_pair[0], 1), queries_chip, swap(queries_pair[1], 1)]
    picks_core = swap(picks_pair, 1)
    group_picks = [picks_pair[0], picks_core[0], picks_pair[1], picks_core[1]]
    for bits in range(0, heads, 2):
        weights[bits + 1] = swap(weights[bits], 1)
    picks = [group_pick.reshape(QB * SEL) for group_pick in group_picks]

    picks, group_queries, weights, near_state = lax.optimization_barrier(
        (picks, group_queries, weights, near_state)
    )

    def far_of(first, second, earlier):
        return far(
            after(jnp.concatenate([picks[first], picks[second]]), *earlier),
            [group_queries[first], group_queries[second]],
            whole,
        )

    *far_corner, far_chip = far_of(3, 2, [])
    for_chip = merge_two(far_chip, [swap(piece, 1) for piece in far_corner], 2)
    chip_parts = [swap(piece, 2) for piece in for_chip]
    *far_core, far_own = far_of(1, 0, for_chip)
    core_parts = [swap(piece, 1) for piece in after(far_core, *chip_parts)]
    attention = merge_last(far_own, core_parts, near_state, chip_parts)

    share_rows = attention.shape[0] // heads
    parts = lax.all_to_all(
        attention.reshape(heads, share_rows, HD), "head", split_axis=0, concat_axis=0, tiled=True
    )
    return attention, project(head[None], parts, weights)


def solution(mesh):
    placed = (
        P("ctx", "head"),
        P("ctx", "head", None),
        P("ctx", None),
        P("ctx", None),
        P("ctx", None),
        P("ctx", None),
        P("head", None),
    )
    return jax.shard_map(
        body,
        mesh=mesh,
        in_specs=placed,
        out_specs=(P("ctx", "head"), P(("ctx", "head"), None)),
        check_vma=False,
    )
```

```python
import functools
import math

import jax
import jax.numpy as jnp
from jax import lax
from jax.experimental import pallas as pl
from jax.experimental.pallas import tpu as pltpu
from jax.sharding import PartitionSpec as P

HD = 128
GROUP = 4
BLK = 512
SEL = 4
QB = 4
BLOCKS = 8
TAIL = 16
SCALE = math.log2(math.e) / math.sqrt(HD)
NEG = -1e30
F32 = jnp.float32
BF16 = jnp.bfloat16
VMEM_BYTES = 56 << 20


def dot_nt(a, b):
    return lax.dot_general(a, b, (((1,), (1,)), ((), ())), preferred_element_type=F32)


def dot_tn(a, b):
    return lax.dot_general(a, b, (((0,), (0,)), ((), ())), preferred_element_type=F32)


def rounded_top(raw):
    return (raw * SCALE).astype(BF16).astype(F32)


def near_kernel(kv_ref, q_ref, k_ref, v_ref, acc_ref, m_ref, l_ref):
    scores = dot_nt(k_ref[...], q_ref[...])
    keys = lax.broadcasted_iota(jnp.int32, (BLK, BLK), 0)
    rows = lax.broadcasted_iota(jnp.int32, (BLK, BLK), 1)
    scores = jnp.where(keys <= rows, scores, NEG)
    top = rounded_top(jnp.max(scores, axis=0, keepdims=True))
    weights = jnp.exp2(scores * SCALE - top)
    m_ref[0] = top
    l_ref[0] = jnp.sum(weights, axis=0, keepdims=True)
    acc_ref[0] = dot_tn(v_ref[...], weights.astype(BF16))


def state_shapes():
    return [
        jax.ShapeDtypeStruct((QB, HD, BLK), F32),
        jax.ShapeDtypeStruct((QB, 1, BLK), F32),
        jax.ShapeDtypeStruct((QB, 1, BLK), F32),
    ]


def near(queries, span_keys, span_values, kv):
    grid_spec = pltpu.PrefetchScalarGridSpec(
        num_scalar_prefetch=1,
        grid=(QB,),
        in_specs=[
            pl.BlockSpec((BLK, HD), lambda i, kv: (i, 0)),
            pl.BlockSpec((BLK, HD), lambda i, kv: (i, kv[0])),
            pl.BlockSpec((BLK, HD), lambda i, kv: (i, kv[0])),
        ],
        out_specs=[
            pl.BlockSpec((1, HD, BLK), lambda i, kv: (i, 0, 0)),
            pl.BlockSpec((1, 1, BLK), lambda i, kv: (i, 0, 0)),
            pl.BlockSpec((1, 1, BLK), lambda i, kv: (i, 0, 0)),
        ],
    )
    return pl.pallas_call(
        near_kernel,
        grid_spec=grid_spec,
        out_shape=state_shapes(),
        cost_estimate=pl.CostEstimate(
            flops=QB * 4 * BLK * BLK * HD, bytes_accessed=4 << 20, transcendentals=QB * BLK * BLK
        ),
        name="near",
    )(kv, queries, span_keys, span_values)


def pack_state(ref, i, out, top, total, columns=slice(None)):
    ref[i, :HD, columns] = out.astype(BF16)
    high = total.astype(BF16)
    low = (total - high.astype(F32)).astype(BF16)
    ref[i, HD:, columns] = jnp.concatenate(
        [top.astype(BF16), high, low, jnp.zeros((TAIL - 3, out.shape[1]), BF16)], axis=0
    )


def unpack_state(ref, i):
    tail = ref[i, HD:, :].astype(F32)
    return ref[i, :HD, :].astype(F32), tail[0:1], tail[1:2] + tail[2:3]


def far_kernel(picks_ref, *refs):
    q_refs, whole_ref, out_refs, refs = refs[:2], refs[2], refs[3:5], refs[5:]
    buffer, score_refs, weight_refs, sem = refs[0], refs[1:3], refs[3:5], refs[5]
    for pick in range(2 * QB * SEL):
        pltpu.make_async_copy(whole_ref.at[picks_ref[pick]], buffer.at[pick], sem).start()
    pltpu.make_async_copy(buffer, buffer, sem).wait()
    step_columns = BLK // 2
    steps = [(row, first) for row in range(2 * QB) for first in range(0, BLK, step_columns)]
    sums = {}

    def joined(row, which):
        return jnp.concatenate([buffer[row * SEL + j, which] for j in range(SEL)], axis=0)

    def score(number):
        row, first = steps[number]
        tokens = pl.ds(row % QB * BLK + first, step_columns)
        score_refs[number % 2][...] = dot_nt(joined(row, 0), q_refs[row // QB][tokens, :])

    def soften(number):
        score_ref, weight_ref = score_refs[number % 2], weight_refs[number % 2]
        tops, totals = [], []
        for lane in range(0, step_columns, HD):
            lanes = slice(lane, lane + HD)
            top = rounded_top(jnp.max(score_ref[:, lanes], axis=0, keepdims=True))
            total = jnp.zeros((8, HD), F32)
            for row in range(0, BLK, 64):
                weights = jnp.exp2(score_ref[row : row + 64, lanes] * SCALE - top)
                weight_ref[row : row + 64, lanes] = weights.astype(BF16)
                total = total + jnp.sum(weights.reshape(8, 8, HD), axis=0)
            tops.append(top)
            totals.append(jnp.sum(total, axis=0, keepdims=True))
        sums[number] = jnp.concatenate(tops, axis=1), jnp.concatenate(totals, axis=1)

    def finish(number):
        row, first = steps[number]
        top, total = sums.pop(number)
        out = dot_tn(joined(row, 1), weight_refs[number % 2][...])
        columns = slice(first, first + step_columns)
        pack_state(out_refs[row // QB], row % QB, out, top, total, columns)

    for number in range(len(steps) + 2):
        if number < len(steps):
            score(number)
        if number >= 2:
            finish(number - 2)
        if 1 <= number <= len(steps):
            soften(number - 1)


def far(picks, queries, whole):
    pay = HD + TAIL
    vmem = pl.BlockSpec(memory_space=pltpu.VMEM)
    return pl.pallas_call(
        far_kernel,
        in_specs=[pl.BlockSpec(memory_space=pltpu.SMEM)]
        + [vmem] * 2
        + [pl.BlockSpec(memory_space=pl.ANY)],
        out_specs=[vmem] * 2,
        out_shape=[jax.ShapeDtypeStruct((QB, pay, BLK), BF16)] * 2,
        scratch_shapes=[pltpu.VMEM((2 * QB * SEL,) + whole.shape[1:], BF16)]
        + [pltpu.VMEM((BLK, BLK // 2), F32)] * 2
        + [pltpu.VMEM((BLK, BLK // 2), BF16)] * 2
        + [pltpu.SemaphoreType.DMA],
        compiler_params=pltpu.CompilerParams(vmem_limit_bytes=VMEM_BYTES),
        cost_estimate=pl.CostEstimate(
            flops=8 * 2 * QB * 4 * BLK * BLK * HD,
            bytes_accessed=5 << 20,
            transcendentals=2 * QB * BLK * BLK,
        ),
        name="far",
    )(picks, *queries, whole)


def merge_two_kernel(a_ref, b_ref, *out_refs):
    per = QB // len(out_refs)
    for i in range(QB):
        acc_a, m_a, l_a = unpack_state(a_ref, i)
        acc_b, m_b, l_b = unpack_state(b_ref, i)
        top = jnp.maximum(m_a, m_b)
        f_a = jnp.exp2(m_a - top)
        f_b = jnp.exp2(m_b - top)
        pack_state(
            out_refs[i // per], i % per, f_a * acc_a + f_b * acc_b, top, f_a * l_a + f_b * l_b
        )


def merge_two(mine, other, pieces):
    vmem = pl.BlockSpec(memory_space=pltpu.VMEM)
    shape = (QB // pieces,) + mine.shape[1:]
    return pl.pallas_call(
        merge_two_kernel,
        in_specs=[vmem] * 2,
        out_specs=[vmem] * pieces,
        out_shape=[jax.ShapeDtypeStruct(shape, BF16)] * pieces,
        name="merge_two",
    )(mine, other)


def merge_last_kernel(head_ref, a_ref, b_ref, acc_ref, m_ref, l_ref, *refs, pieces):
    chip_refs, out_ref, share_refs = refs[:pieces], refs[pieces], refs[pieces + 1 :]
    per = QB // pieces
    rows = QB * BLK // len(share_refs)
    for i in range(QB):
        states = [unpack_state(a_ref, i), unpack_state(b_ref, i)]
        states.append(unpack_state(chip_refs[i // per], i % per))
        states.append((acc_ref[i], m_ref[i], l_ref[i]))
        top = functools.reduce(jnp.maximum, [m for _, m, _ in states])
        factors = [jnp.exp2(m - top) for _, m, _ in states]
        total = sum(f * l for f, (_, _, l) in zip(factors, states))
        factors = [f / total for f in factors]
        out = sum(f * acc for f, (acc, _, _) in zip(factors, states)).T.astype(BF16)
        out_ref[i * BLK : (i + 1) * BLK, :] = out
        for first in range(0, BLK, rows):
            owner = (i * BLK + first) // rows
            for r, share_ref in enumerate(share_refs):

                def keep(share_ref=share_ref, first=first, out=out):
                    share_ref[...] = out[first : first + rows, :]

                pl.when(head_ref[0] ^ r == owner)(keep)


def merge_last(head, heads, mine, core_part, near_state, chip_parts):
    vmem = pl.BlockSpec(memory_space=pltpu.VMEM)
    arrays = [mine, core_part, *near_state, *chip_parts]
    rows = QB * BLK
    attention, *shares = pl.pallas_call(
        functools.partial(merge_last_kernel, pieces=len(chip_parts)),
        in_specs=[pl.BlockSpec(memory_space=pltpu.SMEM)] + [vmem] * len(arrays),
        out_specs=[vmem] * (1 + heads),
        out_shape=[jax.ShapeDtypeStruct((rows, HD), BF16)]
        + [jax.ShapeDtypeStruct((rows // heads, HD), BF16)] * heads,
        name="merge_last",
    )(head, *arrays)
    return attention, shares


def project_kernel(*refs):
    heads = len(refs) // 2
    a_refs, w_refs, out_ref = refs[:heads], refs[heads:-1], refs[-1]
    rows = jnp.concatenate([a_ref[...] for a_ref in a_refs], axis=1)
    tile = 512
    for first in range(0, out_ref.shape[1], tile):
        weight = jnp.concatenate([w_ref[:, first : first + tile] for w_ref in w_refs], axis=0)
        out_ref[:, first : first + tile] = jnp.dot(
            rows, weight, preferred_element_type=F32
        ).astype(BF16)


def project(parts, weights):
    vmem = pl.BlockSpec(memory_space=pltpu.VMEM)
    return pl.pallas_call(
        project_kernel,
        in_specs=[vmem] * (len(parts) + len(weights)),
        out_specs=vmem,
        out_shape=jax.ShapeDtypeStruct((parts[0].shape[0], weights[0].shape[1]), BF16),
        compiler_params=pltpu.CompilerParams(vmem_limit_bytes=24 << 20),
        name="project",
    )(*parts, *weights)


def swap(array, bits):
    return lax.ppermute(array, "head", [(h, h ^ bits) for h in range(lax.axis_size("head"))])


def after(value, *earlier):
    return lax.optimization_barrier((value, earlier))[0]


def body(queries, block_picks, span_keys, span_values, cache_keys, cache_values, out_weight):
    heads = lax.axis_size("head")
    head = lax.axis_index("head")
    part = head % GROUP
    kv = head // GROUP
    share = BLK // GROUP

    pieces = []
    for cache in (cache_keys, cache_values):
        view = cache.reshape(BLOCKS, BLK, cache.shape[1])
        pieces.append(lax.dynamic_slice(view, (0, part * share, kv * HD), (BLOCKS, share, HD)))
    whole = lax.all_gather(jnp.stack(pieces, axis=1), "ctx", axis=0, tiled=True)

    queries_chip = swap(queries, 2)
    picks_chip = swap(block_picks, 2)
    weights = [out_weight] + [None] * (heads - 1)
    for bits in range(2, heads, 2):
        weights[bits] = swap(out_weight, bits)
    near_state = near(queries, span_keys, span_values, kv[None])
    queries_pair = [queries, queries_chip]
    picks_pair = jnp.stack([block_picks, picks_chip])
    group_queries = [queries, swap(queries_pair[0], 1), queries_chip, swap(queries_pair[1], 1)]
    picks_core = swap(picks_pair, 1)
    group_picks = [picks_pair[0], picks_core[0], picks_pair[1], picks_core[1]]
    for bits in range(0, heads, 2):
        weights[bits + 1] = swap(weights[bits], 1)
    picks = [group_pick.reshape(QB * SEL) for group_pick in group_picks]

    picks, group_queries, weights, near_state = lax.optimization_barrier(
        (picks, group_queries, weights, near_state)
    )

    def far_of(first, second, earlier):
        return far(
            after(jnp.concatenate([picks[first], picks[second]]), *earlier),
            [group_queries[first], group_queries[second]],
            whole,
        )

    far_corner, far_chip = far_of(3, 2, [])
    for_chip = merge_two(far_chip, swap(far_corner, 1), 2)
    chip_parts = [swap(piece, 2) for piece in for_chip]
    far_core, far_own = far_of(1, 0, for_chip)
    core_part = swap(after(far_core, *chip_parts), 1)
    attention, shares = merge_last(
        head[None], heads, far_own, core_part, near_state, chip_parts
    )
    parts = [shares[0]] + [swap(shares[r], r) for r in range(1, heads)]
    return attention, project(parts, weights)


def solution(mesh):
    placed = (
        P("ctx", "head"),
        P("ctx", "head", None),
        P("ctx", None),
        P("ctx", None),
        P("ctx", None),
        P("ctx", None),
        P("head", None),
    )
    return jax.shard_map(
        body,
        mesh=mesh,
        in_specs=placed,
        out_specs=(P("ctx", "head"), P(("ctx", "head"), None)),
        check_vma=False,
    )
```

```python
import functools
import math

import jax
import jax.numpy as jnp
from jax import lax
from jax.experimental import pallas as pl
from jax.experimental.pallas import tpu as pltpu
from jax.sharding import PartitionSpec as P

HD = 128
GROUP = 4
BLK = 512
SEL = 4
QB = 4
BLOCKS = 8
TAIL = 16
SCALE = math.log2(math.e) / math.sqrt(HD)
NEG = -1e30
F32 = jnp.float32
BF16 = jnp.bfloat16
NX = 4
NZ = 8
RING_ROWS = 32
VMEM_BYTES = 56 << 20


def dot_nt(a, b):
    return lax.dot_general(a, b, (((1,), (1,)), ((), ())), preferred_element_type=F32)


def dot_tn(a, b):
    return lax.dot_general(a, b, (((0,), (0,)), ((), ())), preferred_element_type=F32)


def rounded_top(raw):
    return (raw * SCALE).astype(BF16).astype(F32)


def near_kernel(kv_ref, q_ref, k_ref, v_ref, acc_ref, m_ref, l_ref):
    scores = dot_nt(k_ref[...], q_ref[...])
    keys = lax.broadcasted_iota(jnp.int32, (BLK, BLK), 0)
    rows = lax.broadcasted_iota(jnp.int32, (BLK, BLK), 1)
    scores = jnp.where(keys <= rows, scores, NEG)
    top = rounded_top(jnp.max(scores, axis=0, keepdims=True))
    weights = jnp.exp2(scores * SCALE - top)
    m_ref[0] = top
    l_ref[0] = jnp.sum(weights, axis=0, keepdims=True)
    acc_ref[0] = dot_tn(v_ref[...], weights.astype(BF16))


def state_shapes():
    return [
        jax.ShapeDtypeStruct((QB, HD, BLK), F32),
        jax.ShapeDtypeStruct((QB, 1, BLK), F32),
        jax.ShapeDtypeStruct((QB, 1, BLK), F32),
    ]


def near(queries, span_keys, span_values, kv):
    grid_spec = pltpu.PrefetchScalarGridSpec(
        num_scalar_prefetch=1,
        grid=(QB,),
        in_specs=[
            pl.BlockSpec((BLK, HD), lambda i, kv: (i, 0)),
            pl.BlockSpec((BLK, HD), lambda i, kv: (i, kv[0])),
            pl.BlockSpec((BLK, HD), lambda i, kv: (i, kv[0])),
        ],
        out_specs=[
            pl.BlockSpec((1, HD, BLK), lambda i, kv: (i, 0, 0)),
            pl.BlockSpec((1, 1, BLK), lambda i, kv: (i, 0, 0)),
            pl.BlockSpec((1, 1, BLK), lambda i, kv: (i, 0, 0)),
        ],
    )
    return pl.pallas_call(
        near_kernel,
        grid_spec=grid_spec,
        out_shape=state_shapes(),
        cost_estimate=pl.CostEstimate(
            flops=QB * 4 * BLK * BLK * HD, bytes_accessed=4 << 20, transcendentals=QB * BLK * BLK
        ),
        name="near",
    )(kv, queries, span_keys, span_values)


def pack_state(ref, i, out, top, total, columns=slice(None)):
    ref[i, :HD, columns] = out.astype(BF16)
    high = total.astype(BF16)
    low = (total - high.astype(F32)).astype(BF16)
    ref[i, HD:, columns] = jnp.concatenate(
        [top.astype(BF16), high, low, jnp.zeros((TAIL - 3, out.shape[1]), BF16)], axis=0
    )


def unpack_state(ref, i):
    tail = ref[i, HD:, :].astype(F32)
    return ref[i, :HD, :].astype(F32), tail[0:1], tail[1:2] + tail[2:3]


def far_kernel(picks_ref, *refs, half):
    q_refs, whole_ref, early_ref, refs = refs[:2], refs[2], refs[3], refs[4:]
    out_refs, (buffer, early), refs = refs[:2], refs[2:4], refs[4:]
    score_refs, weight_refs, sems = refs[:2], refs[2:4], refs[4]
    picks = 2 * QB * SEL
    early_copy = pltpu.make_async_copy(
        early_ref.at[pl.ds(half * picks, picks)], early, sems.at[0]
    )
    early_copy.start()
    for pick in range(picks):
        pltpu.make_async_copy(whole_ref.at[picks_ref[pick]], buffer.at[pick], sems.at[1]).start()
    early_copy.wait()
    pltpu.make_async_copy(buffer, buffer, sems.at[1]).wait()
    step_columns = BLK // 2
    steps = [(row, first) for row in range(2 * QB) for first in range(0, BLK, step_columns)]
    sums = {}

    def joined(row, which):
        return jnp.concatenate(
            [held[row * SEL + j, which] for held in (buffer, early) for j in range(SEL)], axis=0
        )

    def score(number):
        row, first = steps[number]
        tokens = pl.ds(row % QB * BLK + first, step_columns)
        score_refs[number % 2][...] = dot_nt(joined(row, 0), q_refs[row // QB][tokens, :])

    def soften(number):
        score_ref, weight_ref = score_refs[number % 2], weight_refs[number % 2]
        tops, totals = [], []
        for lane in range(0, step_columns, HD):
            lanes = slice(lane, lane + HD)
            top = rounded_top(jnp.max(score_ref[:, lanes], axis=0, keepdims=True))
            total = jnp.zeros((8, HD), F32)
            for row in range(0, BLK, 64):
                weights = jnp.exp2(score_ref[row : row + 64, lanes] * SCALE - top)
                weight_ref[row : row + 64, lanes] = weights.astype(BF16)
                total = total + jnp.sum(weights.reshape(8, 8, HD), axis=0)
            tops.append(top)
            totals.append(jnp.sum(total, axis=0, keepdims=True))
        sums[number] = jnp.concatenate(tops, axis=1), jnp.concatenate(totals, axis=1)

    def finish(number):
        row, first = steps[number]
        top, total = sums.pop(number)
        out = dot_tn(joined(row, 1), weight_refs[number % 2][...])
        columns = slice(first, first + step_columns)
        pack_state(out_refs[row // QB], row % QB, out, top, total, columns)

    for number in range(len(steps) + 2):
        if number < len(steps):
            score(number)
        if number >= 2:
            finish(number - 2)
        if 1 <= number <= len(steps):
            soften(number - 1)


def far(picks, queries, whole, early, half):
    pay = HD + TAIL
    vmem = pl.BlockSpec(memory_space=pltpu.VMEM)
    return pl.pallas_call(
        functools.partial(far_kernel, half=half),
        in_specs=[pl.BlockSpec(memory_space=pltpu.SMEM)]
        + [vmem] * 2
        + [pl.BlockSpec(memory_space=pl.ANY)] * 2,
        out_specs=[vmem] * 2,
        out_shape=[jax.ShapeDtypeStruct((QB, pay, BLK), BF16)] * 2,
        scratch_shapes=[
            pltpu.VMEM((2 * QB * SEL,) + array.shape[1:], BF16) for array in (whole, early)
        ]
        + [pltpu.VMEM((BLK, BLK // 2), F32)] * 2
        + [pltpu.VMEM((BLK, BLK // 2), BF16)] * 2
        + [pltpu.SemaphoreType.DMA((2,))],
        compiler_params=pltpu.CompilerParams(vmem_limit_bytes=VMEM_BYTES),
        cost_estimate=pl.CostEstimate(
            flops=8 * 2 * QB * 4 * BLK * BLK * HD,
            bytes_accessed=5 << 20,
            transcendentals=2 * QB * BLK * BLK,
        ),
        name="far",
    )(picks, *queries, whole, early)


def collect_kernel(where_ref, *refs):
    sources, out_ref, sem = refs[:-2], refs[-2], refs[-1]

    def fetch(pick, carry):
        array, index = where_ref[pick, 0], where_ref[pick, 1]
        for number, source in enumerate(sources):

            def start(source=source):
                pltpu.make_async_copy(source.at[index], out_ref.at[pick], sem).start()

            pl.when(array == number)(start)
        return carry

    lax.fori_loop(0, out_ref.shape[0], fetch, 0)
    pltpu.make_async_copy(out_ref, out_ref, sem).wait()


def collect(where, arrays):
    return pl.pallas_call(
        collect_kernel,
        in_specs=[pl.BlockSpec(memory_space=pltpu.SMEM)]
        + [pl.BlockSpec(memory_space=pl.ANY)] * len(arrays),
        out_specs=pl.BlockSpec(memory_space=pltpu.VMEM),
        out_shape=jax.ShapeDtypeStruct((where.shape[0],) + arrays[0].shape[1:], BF16),
        scratch_shapes=[pltpu.SemaphoreType.DMA],
        compiler_params=pltpu.CompilerParams(vmem_limit_bytes=VMEM_BYTES),
        name="collect",
    )(where, *arrays)


def merge_two_kernel(a_ref, b_ref, *out_refs):
    per = QB // len(out_refs)
    for i in range(QB):
        acc_a, m_a, l_a = unpack_state(a_ref, i)
        acc_b, m_b, l_b = unpack_state(b_ref, i)
        top = jnp.maximum(m_a, m_b)
        f_a = jnp.exp2(m_a - top)
        f_b = jnp.exp2(m_b - top)
        pack_state(
            out_refs[i // per], i % per, f_a * acc_a + f_b * acc_b, top, f_a * l_a + f_b * l_b
        )


def merge_two(mine, other, pieces):
    vmem = pl.BlockSpec(memory_space=pltpu.VMEM)
    shape = (QB // pieces,) + mine.shape[1:]
    return pl.pallas_call(
        merge_two_kernel,
        in_specs=[vmem] * 2,
        out_specs=[vmem] * pieces,
        out_shape=[jax.ShapeDtypeStruct(shape, BF16)] * pieces,
        name="merge_two",
    )(mine, other)


def merge_last_kernel(head_ref, a_ref, b_ref, acc_ref, m_ref, l_ref, *refs, pieces):
    chip_refs, out_ref, share_refs = refs[:pieces], refs[pieces], refs[pieces + 1 :]
    per = QB // pieces
    rows = QB * BLK // len(share_refs)
    for i in range(QB):
        states = [unpack_state(a_ref, i), unpack_state(b_ref, i)]
        states.append(unpack_state(chip_refs[i // per], i % per))
        states.append((acc_ref[i], m_ref[i], l_ref[i]))
        top = functools.reduce(jnp.maximum, [m for _, m, _ in states])
        factors = [jnp.exp2(m - top) for _, m, _ in states]
        total = sum(f * l for f, (_, _, l) in zip(factors, states))
        factors = [f / total for f in factors]
        out = sum(f * acc for f, (acc, _, _) in zip(factors, states)).T.astype(BF16)
        out_ref[i * BLK : (i + 1) * BLK, :] = out
        for first in range(0, BLK, rows):
            owner = (i * BLK + first) // rows
            for r, share_ref in enumerate(share_refs):

                def keep(share_ref=share_ref, first=first, out=out):
                    share_ref[...] = out[first : first + rows, :]

                pl.when(head_ref[0] ^ r == owner)(keep)


def merge_last(head, heads, mine, core_part, near_state, chip_parts):
    vmem = pl.BlockSpec(memory_space=pltpu.VMEM)
    arrays = [mine, core_part, *near_state, *chip_parts]
    rows = QB * BLK
    attention, *shares = pl.pallas_call(
        functools.partial(merge_last_kernel, pieces=len(chip_parts)),
        in_specs=[pl.BlockSpec(memory_space=pltpu.SMEM)] + [vmem] * len(arrays),
        out_specs=[vmem] * (1 + heads),
        out_shape=[jax.ShapeDtypeStruct((rows, HD), BF16)]
        + [jax.ShapeDtypeStruct((rows // heads, HD), BF16)] * heads,
        name="merge_last",
    )(head, *arrays)
    return attention, shares


def project_kernel(*refs):
    heads = len(refs) // 2
    a_refs, w_refs, out_ref = refs[:heads], refs[heads:-1], refs[-1]
    rows = jnp.concatenate([a_ref[...] for a_ref in a_refs], axis=1)
    tile = 512
    for first in range(0, out_ref.shape[1], tile):
        weight = jnp.concatenate([w_ref[:, first : first + tile] for w_ref in w_refs], axis=0)
        out_ref[:, first : first + tile] = jnp.dot(
            rows, weight, preferred_element_type=F32
        ).astype(BF16)


def project(parts, weights):
    vmem = pl.BlockSpec(memory_space=pltpu.VMEM)
    return pl.pallas_call(
        project_kernel,
        in_specs=[vmem] * (len(parts) + len(weights)),
        out_specs=vmem,
        out_shape=jax.ShapeDtypeStruct((parts[0].shape[0], weights[0].shape[1]), BF16),
        compiler_params=pltpu.CompilerParams(vmem_limit_bytes=24 << 20),
        name="project",
    )(*parts, *weights)


def shift(array, dz, dx):
    pairs = []
    for z in range(NZ):
        for x in range(NX):
            pairs.append((z * NX + x, (z + dz) % NZ * NX + (x + dx) % NX))
    return lax.ppermute(array, "ctx", pairs)


def swap(array, bits):
    return lax.ppermute(array, "head", [(h, h ^ bits) for h in range(lax.axis_size("head"))])


def after(value, *earlier):
    return lax.optimization_barrier((value, earlier))[0]


def body(queries, block_picks, span_keys, span_values, cache_keys, cache_values, out_weight):
    heads = lax.axis_size("head")
    head = lax.axis_index("head")
    part = head % GROUP
    kv = head // GROUP
    share = BLK // GROUP

    def cut(first, rows):
        pieces = []
        for cache in (cache_keys, cache_values):
            view = cache.reshape(BLOCKS, BLK, cache.shape[1])
            pieces.append(
                lax.dynamic_slice(view, (0, part * share + first, kv * HD), (BLOCKS, rows, HD))
            )
        return jnp.stack(pieces, axis=1)

    whole = lax.all_gather(cut(0, share - RING_ROWS), "ctx", axis=0, tiled=True)

    ring = cut(share - RING_ROWS, RING_ROWS)
    z1, z2 = shift(ring, 1, 0), shift(ring, -1, 0)
    z3, z4 = shift(z1, 1, 0), shift(z2, -1, 0)
    low = jnp.concatenate([ring, z1, z2, z3], axis=0)
    x1_low, x2_low = shift(low, 0, 1), shift(low, 0, -1)
    z5, z6 = shift(z3, 1, 0), shift(z4, -1, 0)
    half = BLOCKS // 2
    z7, z8 = shift(z5[:half], 1, 0), shift(z6[half:], -1, 0)
    high = jnp.concatenate([z4, z5, z6, z7, z8], axis=0)
    x1_high, x2_high = shift(high, 0, 1), shift(high, 0, -1)
    x3_low, x3_high = shift(x1_low, 0, 1), shift(x2_high, 0, -1)
    ring_arrays = [low, high, x1_low, x1_high, x2_low, x2_high, x3_low, x3_high]

    queries_early, picks_early, weight_early = after(
        (queries, block_picks, out_weight), *ring_arrays[:6]
    )
    queries_pair = [queries, swap(queries_early, 2)]
    picks_pair = jnp.stack([block_picks, swap(picks_early, 2)])
    weights = [out_weight] + [None] * (heads - 1)
    for bits in range(2, heads, 2):
        weights[bits] = swap(weight_early, bits)
    near_state = near(queries_early, span_keys, span_values, kv[None])
    queries_pair, picks_pair, weights[::2] = after(
        (queries_pair, picks_pair, weights[::2]), *ring_arrays
    )
    group_queries = [queries, swap(queries_pair[0], 1), queries_pair[1], swap(queries_pair[1], 1)]
    picks_core = swap(picks_pair, 1)
    group_picks = [picks_pair[0], picks_core[0], picks_pair[1], picks_core[1]]
    for bits in range(0, heads, 2):
        weights[bits + 1] = swap(weights[bits], 1)
    picks = [group_pick.reshape(QB * SEL) for group_pick in group_picks]

    every_pick = jnp.concatenate(picks[::-1])
    owner, local = every_pick // BLOCKS, every_pick % BLOCKS
    ctx = lax.axis_index("ctx")
    dz = (owner // NX - ctx // NX) % NZ
    dx = (owner % NX - ctx % NX) % NX
    order_x = jnp.where(dx == 0, 0, jnp.where(dx == 3, 1, jnp.where(dx == 1, 2, 3)))
    order_z = jnp.where(dz == 0, 0, jnp.where(dz > NZ // 2, 2 * (NZ - dz) - 1, 2 * dz))
    place = jnp.where(dz == NZ // 2, NZ - 1, order_z) * BLOCKS + local
    upper = (place >= low.shape[0]).astype(jnp.int32)
    where = jnp.stack([2 * order_x + upper, place - low.shape[0] * upper], axis=-1)
    early = collect(where.astype(jnp.int32), ring_arrays)

    picks, group_queries, weights, near_state, early = lax.optimization_barrier(
        (picks, group_queries, weights, near_state, early)
    )

    def far_of(first, second, earlier, half):
        return far(
            after(jnp.concatenate([picks[first], picks[second]]), *earlier),
            [group_queries[first], group_queries[second]],
            whole,
            early,
            half,
        )

    far_corner, far_chip = far_of(3, 2, [], 0)
    for_chip = merge_two(far_chip, swap(far_corner, 1), 2)
    chip_parts = [swap(piece, 2) for piece in for_chip]
    far_core, far_own = far_of(1, 0, for_chip, 1)
    core_part = swap(after(far_core, *chip_parts), 1)
    attention, shares = merge_last(
        head[None], heads, far_own, core_part, near_state, chip_parts
    )
    parts = [shares[0]] + [swap(shares[r], r) for r in range(1, heads)]
    return attention, project(parts, weights)


def solution(mesh):
    placed = (
        P("ctx", "head"),
        P("ctx", "head", None),
        P("ctx", None),
        P("ctx", None),
        P("ctx", None),
        P("ctx", None),
        P("head", None),
    )
    return jax.shard_map(
        body,
        mesh=mesh,
        in_specs=placed,
        out_specs=(P("ctx", "head"), P(("ctx", "head"), None)),
        check_vma=False,
    )
```

```python
import functools
import math

import jax
import jax.numpy as jnp
from jax import lax
from jax.experimental import pallas as pl
from jax.experimental.pallas import tpu as pltpu
from jax.sharding import PartitionSpec as P

HD = 128
GROUP = 4
BLK = 512
HALF = BLK // 2
SEL = 4
QB = 4
BLOCKS = 8
TAIL = 16
SCALE = math.log2(math.e) / math.sqrt(HD)
NEG = -1e30
F32 = jnp.float32
BF16 = jnp.bfloat16
NX = 4
NZ = 8
RING_ROWS = 48
VMEM_BYTES = 56 << 20


def dot_nt(a, b):
    return lax.dot_general(a, b, (((1,), (1,)), ((), ())), preferred_element_type=F32)


def dot_tn(a, b):
    return lax.dot_general(a, b, (((0,), (0,)), ((), ())), preferred_element_type=F32)


def rounded_top(raw):
    return (raw * SCALE).astype(BF16).astype(F32)


def near_kernel(place_ref, *refs):
    q_refs, (k_ref, v_ref, acc_ref, m_ref, l_ref) = refs[:2], refs[2:]
    keys = lax.broadcasted_iota(jnp.int32, (BLK, HALF), 0)
    rows = lax.broadcasted_iota(jnp.int32, (BLK, HALF), 1) + place_ref[1] * HALF
    for r, q_ref in enumerate(q_refs):
        scores = jnp.where(keys <= rows, dot_nt(k_ref[...], q_ref[...]), NEG)
        top = rounded_top(jnp.max(scores, axis=0, keepdims=True))
        weights = jnp.exp2(scores * SCALE - top)
        m_ref[0, r] = top
        l_ref[0, r] = jnp.sum(weights, axis=0, keepdims=True)
        acc_ref[0, r] = dot_tn(v_ref[...], weights.astype(BF16))


def near(place, queries, span_keys, span_values):
    grid_spec = pltpu.PrefetchScalarGridSpec(
        num_scalar_prefetch=1,
        grid=(QB,),
        in_specs=[pl.BlockSpec((HALF, HD), lambda i, place: (2 * i + place[1], 0))] * 2
        + [pl.BlockSpec((BLK, HD), lambda i, place: (i, place[0]))] * 2,
        out_specs=[
            pl.BlockSpec((1, 2, HD, HALF), lambda i, place: (i, 0, 0, 0)),
            pl.BlockSpec((1, 2, 1, HALF), lambda i, place: (i, 0, 0, 0)),
            pl.BlockSpec((1, 2, 1, HALF), lambda i, place: (i, 0, 0, 0)),
        ],
    )
    return pl.pallas_call(
        near_kernel,
        grid_spec=grid_spec,
        out_shape=[
            jax.ShapeDtypeStruct((QB, 2, HD, HALF), F32),
            jax.ShapeDtypeStruct((QB, 2, 1, HALF), F32),
            jax.ShapeDtypeStruct((QB, 2, 1, HALF), F32),
        ],
        cost_estimate=pl.CostEstimate(
            flops=QB * 4 * BLK * BLK * HD, bytes_accessed=4 << 20, transcendentals=QB * BLK * BLK
        ),
        name="near",
    )(place, *queries, span_keys, span_values)


def pack_state(ref, i, out, top, total):
    ref[i, :HD, :] = out.astype(BF16)
    high = total.astype(BF16)
    low = (total - high.astype(F32)).astype(BF16)
    ref[i, HD:, :] = jnp.concatenate(
        [top.astype(BF16), high, low, jnp.zeros((TAIL - 3, out.shape[1]), BF16)], axis=0
    )


def unpack_state(ref, i):
    tail = ref[i, HD:, :].astype(F32)
    return ref[i, :HD, :].astype(F32), tail[0:1], tail[1:2] + tail[2:3]


def far_kernel(picks_ref, *refs, half):
    q_refs, whole_ref, early_ref, refs = refs[:2], refs[2], refs[3], refs[4:]
    out_refs, (buffer, early), refs = refs[:2], refs[2:4], refs[4:]
    score_refs, weight_refs, sems = refs[:2], refs[2:4], refs[4]
    picks = 2 * QB * SEL
    early_copy = pltpu.make_async_copy(
        early_ref.at[pl.ds(half * picks, picks)], early, sems.at[0]
    )
    early_copy.start()
    for pick in range(picks):
        sem = sems.at[1 if pick < SEL else 2]
        pltpu.make_async_copy(whole_ref.at[picks_ref[pick]], buffer.at[pick], sem).start()
    early_copy.wait()
    steps = [(row, k) for row in range(2 * QB) for k in range(2)]
    sums = {}

    def fetched(first, count, sem):
        held = buffer.at[pl.ds(first, count)]
        pltpu.make_async_copy(held, held, sem).wait()

    def joined(row, which):
        return jnp.concatenate(
            [held[row * SEL + j, which] for held in (buffer, early) for j in range(SEL)], axis=0
        )

    def score(number):
        row, k = steps[number]
        if number == 0:
            fetched(0, SEL, sems.at[1])
        if number == 2:
            fetched(SEL, picks - SEL, sems.at[2])
        first = row % QB * BLK + (picks_ref[picks] ^ k) * HALF
        tokens = pl.ds(pl.multiple_of(first, HALF), HALF)
        score_refs[number % 2][...] = dot_nt(joined(row, 0), q_refs[row // QB][tokens, :])

    def soften(number):
        score_ref, weight_ref = score_refs[number % 2], weight_refs[number % 2]
        tops, totals = [], []
        for lane in range(0, HALF, HD):
            lanes = slice(lane, lane + HD)
            top = rounded_top(jnp.max(score_ref[:, lanes], axis=0, keepdims=True))
            total = jnp.zeros((8, HD), F32)
            for row in range(0, BLK, 64):
                weights = jnp.exp2(score_ref[row : row + 64, lanes] * SCALE - top)
                weight_ref[row : row + 64, lanes] = weights.astype(BF16)
                total = total + jnp.sum(weights.reshape(8, 8, HD), axis=0)
            tops.append(top)
            totals.append(jnp.sum(total, axis=0, keepdims=True))
        sums[number] = jnp.concatenate(tops, axis=1), jnp.concatenate(totals, axis=1)

    def finish(number):
        row, k = steps[number]
        top, total = sums.pop(number)
        out = dot_tn(joined(row, 1), weight_refs[number % 2][...])
        pack_state(out_refs[k], row, out, top, total)

    for number in range(len(steps) + 2):
        if number < len(steps):
            score(number)
        if number >= 2:
            finish(number - 2)
        if 1 <= number <= len(steps):
            soften(number - 1)


def far(picks, queries, whole, early, half):
    pay = HD + TAIL
    vmem = pl.BlockSpec(memory_space=pltpu.VMEM)
    return pl.pallas_call(
        functools.partial(far_kernel, half=half),
        in_specs=[pl.BlockSpec(memory_space=pltpu.SMEM)]
        + [vmem] * 2
        + [pl.BlockSpec(memory_space=pl.ANY)] * 2,
        out_specs=[vmem] * 2,
        out_shape=[jax.ShapeDtypeStruct((2 * QB, pay, HALF), BF16)] * 2,
        scratch_shapes=[
            pltpu.VMEM((2 * QB * SEL,) + array.shape[1:], BF16) for array in (whole, early)
        ]
        + [pltpu.VMEM((BLK, HALF), F32)] * 2
        + [pltpu.VMEM((BLK, HALF), BF16)] * 2
        + [pltpu.SemaphoreType.DMA((3,))],
        compiler_params=pltpu.CompilerParams(vmem_limit_bytes=VMEM_BYTES),
        cost_estimate=pl.CostEstimate(
            flops=8 * 2 * QB * 4 * BLK * BLK * HD,
            bytes_accessed=5 << 20,
            transcendentals=2 * QB * BLK * BLK,
        ),
        name="far",
    )(picks, *queries, whole, early)


def collect_kernel(where_ref, *refs):
    sources, out_ref, sem = refs[:-2], refs[-2], refs[-1]

    def fetch(pick, carry):
        array, index = where_ref[pick, 0], where_ref[pick, 1]
        for number, source in enumerate(sources):

            def start(source=source):
                pltpu.make_async_copy(source.at[index], out_ref.at[pick], sem).start()

            pl.when(array == number)(start)
        return carry

    lax.fori_loop(0, out_ref.shape[0], fetch, 0)
    pltpu.make_async_copy(out_ref, out_ref, sem).wait()


def collect(where, arrays):
    return pl.pallas_call(
        collect_kernel,
        in_specs=[pl.BlockSpec(memory_space=pltpu.SMEM)]
        + [pl.BlockSpec(memory_space=pl.ANY)] * len(arrays),
        out_specs=pl.BlockSpec(memory_space=pltpu.VMEM),
        out_shape=jax.ShapeDtypeStruct((where.shape[0],) + arrays[0].shape[1:], BF16),
        scratch_shapes=[pltpu.SemaphoreType.DMA],
        compiler_params=pltpu.CompilerParams(vmem_limit_bytes=VMEM_BYTES),
        name="collect",
    )(where, *arrays)


def crossed(row):
    return (row + QB) % (2 * QB)


def merge_two_kernel(a_ref, b_ref, *out_refs):
    for row in range(2 * QB):
        acc_a, m_a, l_a = unpack_state(a_ref, row)
        acc_b, m_b, l_b = unpack_state(b_ref, crossed(row))
        top = jnp.maximum(m_a, m_b)
        f_a = jnp.exp2(m_a - top)
        f_b = jnp.exp2(m_b - top)
        out = f_a * acc_a + f_b * acc_b
        pack_state(out_refs[row // QB], row % QB, out, top, f_a * l_a + f_b * l_b)


def merge_two(mine, other):
    vmem = pl.BlockSpec(memory_space=pltpu.VMEM)
    return pl.pallas_call(
        merge_two_kernel,
        in_specs=[vmem] * 2,
        out_specs=[vmem] * 2,
        out_shape=[jax.ShapeDtypeStruct((QB,) + mine.shape[1:], BF16)] * 2,
        name="merge_two",
    )(mine, other)


def merge_last_kernel(chip_ref, a_ref, b_ref, acc_ref, m_ref, l_ref, *refs):
    chip_refs, half_refs, share_refs = refs[:2], refs[2:4], refs[4:]
    for row in range(2 * QB):
        r, i = row // QB, row % QB
        states = [unpack_state(a_ref, row), unpack_state(b_ref, crossed(row))]
        states.append(unpack_state(chip_refs[r], i))
        states.append((acc_ref[i, r], m_ref[i, r], l_ref[i, r]))
        top = functools.reduce(jnp.maximum, [m for _, m, _ in states])
        factors = [jnp.exp2(m - top) for _, m, _ in states]
        total = sum(f * l for f, (_, _, l) in zip(factors, states))
        factors = [f / total for f in factors]
        out = sum(f * acc for f, (acc, _, _) in zip(factors, states)).T.astype(BF16)
        half_refs[r][i] = out
        for n, share_ref in enumerate(share_refs):

            def keep(share_ref=share_ref, r=r, out=out):
                share_ref[r] = out

            pl.when(chip_ref[0] ^ n == i)(keep)


def merge_last(chip, mine, core_part, near_state, chip_parts):
    vmem = pl.BlockSpec(memory_space=pltpu.VMEM)
    arrays = [mine, core_part, *near_state, *chip_parts]
    own, other, *shares = pl.pallas_call(
        merge_last_kernel,
        in_specs=[pl.BlockSpec(memory_space=pltpu.SMEM)] + [vmem] * len(arrays),
        out_specs=[vmem] * (2 + QB),
        out_shape=[jax.ShapeDtypeStruct((QB, HALF, HD), BF16)] * 2
        + [jax.ShapeDtypeStruct((2, HALF, HD), BF16)] * QB,
        name="merge_last",
    )(chip, *arrays)
    return own, other, shares


def assemble_kernel(core_ref, own_ref, other_ref, out_ref):
    for i in range(QB):
        for k, ref in enumerate((own_ref, other_ref)):
            first = pl.multiple_of(i * BLK + (core_ref[0] ^ k) * HALF, HALF)
            out_ref[pl.ds(first, HALF), :] = ref[i]


def assemble(core, own, other):
    vmem = pl.BlockSpec(memory_space=pltpu.VMEM)
    return pl.pallas_call(
        assemble_kernel,
        in_specs=[pl.BlockSpec(memory_space=pltpu.SMEM)] + [vmem] * 2,
        out_specs=vmem,
        out_shape=jax.ShapeDtypeStruct((QB * BLK, HD), BF16),
        name="assemble",
    )(core, own, other)


def project_kernel(*refs):
    a_refs, w_refs, out_ref = refs[:QB], refs[QB:-1], refs[-1]
    rows = jnp.concatenate([a_ref[r] for a_ref in a_refs for r in range(2)], axis=1)
    tile = 512
    for first in range(0, out_ref.shape[1], tile):
        weight = jnp.concatenate([w_ref[:, first : first + tile] for w_ref in w_refs], axis=0)
        out_ref[:, first : first + tile] = jnp.dot(
            rows, weight, preferred_element_type=F32
        ).astype(BF16)


def project(parts, weights):
    vmem = pl.BlockSpec(memory_space=pltpu.VMEM)
    return pl.pallas_call(
        project_kernel,
        in_specs=[vmem] * (len(parts) + len(weights)),
        out_specs=vmem,
        out_shape=jax.ShapeDtypeStruct((parts[0].shape[1], weights[0].shape[1]), BF16),
        compiler_params=pltpu.CompilerParams(vmem_limit_bytes=24 << 20),
        name="project",
    )(*parts, *weights)


def shift(array, dz, dx):
    pairs = []
    for z in range(NZ):
        for x in range(NX):
            pairs.append((z * NX + x, (z + dz) % NZ * NX + (x + dx) % NX))
    return lax.ppermute(array, "ctx", pairs)


def swap(array, bits):
    return lax.ppermute(array, "head", [(h, h ^ bits) for h in range(lax.axis_size("head"))])


def after(value, *earlier):
    return lax.optimization_barrier((value, earlier))[0]


def body(queries, block_picks, span_keys, span_values, cache_keys, cache_values, out_weight):
    heads = lax.axis_size("head")
    head = lax.axis_index("head")
    part = head % GROUP
    kv = head // GROUP
    share = BLK // GROUP

    def cut(first, rows):
        pieces = []
        for cache in (cache_keys, cache_values):
            view = cache.reshape(BLOCKS, BLK, cache.shape[1])
            pieces.append(
                lax.dynamic_slice(view, (0, part * share + first, kv * HD), (BLOCKS, rows, HD))
            )
        return jnp.stack(pieces, axis=1)

    whole = lax.all_gather(cut(0, share - RING_ROWS), "ctx", axis=0, tiled=True)

    ring = cut(share - RING_ROWS, RING_ROWS)
    z1, z2 = shift(ring, 1, 0), shift(ring, -1, 0)
    z3, z4 = shift(z1, 1, 0), shift(z2, -1, 0)
    low = jnp.concatenate([ring, z1, z2, z3], axis=0)
    x1_low, x2_low = shift(low, 0, 1), shift(low, 0, -1)
    z5, z6 = shift(z3, 1, 0), shift(z4, -1, 0)
    half = BLOCKS // 2
    z7, z8 = shift(z5[:half], 1, 0), shift(z6[half:], -1, 0)
    high = jnp.concatenate([z4, z5, z6, z7, z8], axis=0)
    x1_high, x2_high = shift(high, 0, 1), shift(high, 0, -1)
    x3_low, x3_high = shift(x1_low, 0, 1), shift(x2_high, 0, -1)
    ring_arrays = [low, high, x1_low, x1_high, x2_low, x2_high, x3_low, x3_high]

    queries_early, picks_early, weight_early = after(
        (queries, block_picks, out_weight), x1_low, x2_low
    )
    queries_pair = [queries, swap(queries_early, 2)]
    picks_pair = jnp.stack([block_picks, swap(picks_early, 2)])
    weights = [out_weight] + [None] * (heads - 1)
    for bits in range(2, heads, 2):
        weights[bits] = swap(weight_early, bits)
    queries_pair, picks_pair, weights[::2] = after(
        (queries_pair, picks_pair, weights[::2]), *ring_arrays
    )
    group_queries = [queries, swap(queries_pair[0], 1), queries_pair[1], swap(queries_pair[1], 1)]
    core, chip = head % 2, head // 2
    near_state = near(
        jnp.stack([kv, core]).astype(jnp.int32), group_queries[:2], span_keys, span_values
    )
    picks_core = swap(picks_pair, 1)
    group_picks = [picks_pair[0], picks_core[0], picks_pair[1], picks_core[1]]
    for bits in range(0, heads, 2):
        weights[bits + 1] = swap(weights[bits], 1)
    picks = [group_pick.reshape(QB * SEL) for group_pick in group_picks]

    every_pick = jnp.concatenate([picks[r] for r in (2, 3, 0, 1)])
    owner, local = every_pick // BLOCKS, every_pick % BLOCKS
    ctx = lax.axis_index("ctx")
    dz = (owner // NX - ctx // NX) % NZ
    dx = (owner % NX - ctx % NX) % NX
    order_x = jnp.where(dx == 0, 0, jnp.where(dx == 3, 1, jnp.where(dx == 1, 2, 3)))
    order_z = jnp.where(dz == 0, 0, jnp.where(dz > NZ // 2, 2 * (NZ - dz) - 1, 2 * dz))
    place = jnp.where(dz == NZ // 2, NZ - 1, order_z) * BLOCKS + local
    upper = (place >= low.shape[0]).astype(jnp.int32)
    where = jnp.stack([2 * order_x + upper, place - low.shape[0] * upper], axis=-1)
    early = collect(where.astype(jnp.int32), ring_arrays)

    picks, group_queries, weights, near_state, early = lax.optimization_barrier(
        (picks, group_queries, weights, near_state, early)
    )

    def far_of(first, second, earlier, half):
        return far(
            after(jnp.concatenate([picks[first], picks[second], core[None]]), *earlier),
            [group_queries[first], group_queries[second]],
            whole,
            early,
            half,
        )

    chip_here, chip_there = far_of(2, 3, [], 0)
    for_chip = merge_two(chip_here, swap(chip_there, 1))
    chip_parts = [swap(piece, 2) for piece in for_chip]
    own_here, own_there = far_of(0, 1, for_chip, 1)
    core_part = swap(after(own_there, *chip_parts), 1)
    own, other, shares = merge_last(chip[None], own_here, core_part, near_state, chip_parts)
    parts = [shares[0]] + [swap(shares[n], 2 * n) for n in range(1, QB)]
    attention = assemble(core[None], own, swap(other, 1))
    return attention, project(after(parts, attention), weights)


def solution(mesh):
    placed = (
        P("ctx", "head"),
        P("ctx", "head", None),
        P("ctx", None),
        P("ctx", None),
        P("ctx", None),
        P("ctx", None),
        P("head", None),
    )
    return jax.shard_map(
        body,
        mesh=mesh,
        in_specs=placed,
        out_specs=(P("ctx", "head"), P(("ctx", "head"), None)),
        check_vma=False,
    )
```

```python
import functools
import math

import jax
import jax.numpy as jnp
from jax import lax
from jax.experimental import pallas as pl
from jax.experimental.pallas import tpu as pltpu
from jax.sharding import PartitionSpec as P

HD = 128
GROUP = 4
BLK = 512
HALF = BLK // 2
SEL = 4
QB = 4
BLOCKS = 8
TAIL = 16
SCALE = math.log2(math.e) / math.sqrt(HD)
NEG = -1e30
F32 = jnp.float32
BF16 = jnp.bfloat16
NX = 4
NZ = 8
ROWS_ZX = 32
ROWS_XZ = 16
VMEM_BYTES = 56 << 20


def dot_nt(a, b):
    return lax.dot_general(a, b, (((1,), (1,)), ((), ())), preferred_element_type=F32)


def dot_tn(a, b):
    return lax.dot_general(a, b, (((0,), (0,)), ((), ())), preferred_element_type=F32)


def rounded_top(raw):
    return (raw * SCALE).astype(BF16).astype(F32)


def near_kernel(place_ref, *refs):
    q_refs, (k_ref, v_ref, acc_ref, m_ref, l_ref) = refs[:2], refs[2:]
    keys = lax.broadcasted_iota(jnp.int32, (BLK, HALF), 0)
    rows = lax.broadcasted_iota(jnp.int32, (BLK, HALF), 1) + place_ref[1] * HALF
    for r, q_ref in enumerate(q_refs):
        scores = jnp.where(keys <= rows, dot_nt(k_ref[...], q_ref[...]), NEG)
        top = rounded_top(jnp.max(scores, axis=0, keepdims=True))
        weights = jnp.exp2(scores * SCALE - top)
        m_ref[0, r] = top
        l_ref[0, r] = jnp.sum(weights, axis=0, keepdims=True)
        acc_ref[0, r] = dot_tn(v_ref[...], weights.astype(BF16))


def near(place, queries, span_keys, span_values):
    grid_spec = pltpu.PrefetchScalarGridSpec(
        num_scalar_prefetch=1,
        grid=(QB,),
        in_specs=[pl.BlockSpec((HALF, HD), lambda i, place: (2 * i + place[1], 0))] * 2
        + [pl.BlockSpec((BLK, HD), lambda i, place: (i, place[0]))] * 2,
        out_specs=[
            pl.BlockSpec((1, 2, HD, HALF), lambda i, place: (i, 0, 0, 0)),
            pl.BlockSpec((1, 2, 1, HALF), lambda i, place: (i, 0, 0, 0)),
            pl.BlockSpec((1, 2, 1, HALF), lambda i, place: (i, 0, 0, 0)),
        ],
    )
    return pl.pallas_call(
        near_kernel,
        grid_spec=grid_spec,
        out_shape=[
            jax.ShapeDtypeStruct((QB, 2, HD, HALF), F32),
            jax.ShapeDtypeStruct((QB, 2, 1, HALF), F32),
            jax.ShapeDtypeStruct((QB, 2, 1, HALF), F32),
        ],
        cost_estimate=pl.CostEstimate(
            flops=QB * 4 * BLK * BLK * HD, bytes_accessed=4 << 20, transcendentals=QB * BLK * BLK
        ),
        name="near",
    )(place, *queries, span_keys, span_values)


def pack_state(ref, i, out, top, total):
    ref[i, :HD, :] = out.astype(BF16)
    high = total.astype(BF16)
    low = (total - high.astype(F32)).astype(BF16)
    ref[i, HD:, :] = jnp.concatenate(
        [top.astype(BF16), high, low, jnp.zeros((TAIL - 3, out.shape[1]), BF16)], axis=0
    )


def unpack_state(ref, i):
    tail = ref[i, HD:, :].astype(F32)
    return ref[i, :HD, :].astype(F32), tail[0:1], tail[1:2] + tail[2:3]


def far_kernel(picks_ref, *refs, half):
    q_refs, whole_ref, early_refs, refs = refs[:2], refs[2], refs[3:5], refs[5:]
    out_refs, buffer, early, refs = refs[:2], refs[2], refs[3:5], refs[5:]
    score_refs, weight_refs, sems = refs[:2], refs[2:4], refs[4]
    picks = 2 * QB * SEL
    early_copies = [
        pltpu.make_async_copy(source.at[pl.ds(half * picks, picks)], target, sems.at[2 + n])
        for n, (source, target) in enumerate(zip(early_refs, early))
    ]
    for copy in early_copies:
        copy.start()
    for pick in range(picks):
        sem = sems.at[0 if pick < SEL else 1]
        pltpu.make_async_copy(whole_ref.at[picks_ref[pick]], buffer.at[pick], sem).start()
    for copy in early_copies:
        copy.wait()
    steps = [(row, k) for row in range(2 * QB) for k in range(2)]
    sums = {}

    def fetched(first, count, sem):
        held = buffer.at[pl.ds(first, count)]
        pltpu.make_async_copy(held, held, sem).wait()

    def joined(row, which):
        return jnp.concatenate(
            [held[row * SEL + j, which] for held in (buffer, *early) for j in range(SEL)], axis=0
        )

    def score(number):
        row, k = steps[number]
        if number == 0:
            fetched(0, SEL, sems.at[0])
        if number == 2:
            fetched(SEL, picks - SEL, sems.at[1])
        first = row % QB * BLK + (picks_ref[picks] ^ k) * HALF
        tokens = pl.ds(pl.multiple_of(first, HALF), HALF)
        score_refs[number % 2][...] = dot_nt(joined(row, 0), q_refs[row // QB][tokens, :])

    def soften(number):
        score_ref, weight_ref = score_refs[number % 2], weight_refs[number % 2]
        tops, totals = [], []
        for lane in range(0, HALF, HD):
            lanes = slice(lane, lane + HD)
            top = rounded_top(jnp.max(score_ref[:, lanes], axis=0, keepdims=True))
            total = jnp.zeros((8, HD), F32)
            for row in range(0, BLK, 64):
                weights = jnp.exp2(score_ref[row : row + 64, lanes] * SCALE - top)
                weight_ref[row : row + 64, lanes] = weights.astype(BF16)
                total = total + jnp.sum(weights.reshape(8, 8, HD), axis=0)
            tops.append(top)
            totals.append(jnp.sum(total, axis=0, keepdims=True))
        sums[number] = jnp.concatenate(tops, axis=1), jnp.concatenate(totals, axis=1)

    def finish(number):
        row, k = steps[number]
        top, total = sums.pop(number)
        out = dot_tn(joined(row, 1), weight_refs[number % 2][...])
        pack_state(out_refs[k], row, out, top, total)

    for number in range(len(steps) + 2):
        if number < len(steps):
            score(number)
        if number >= 2:
            finish(number - 2)
        if 1 <= number <= len(steps):
            soften(number - 1)


def far(picks, queries, whole, early, half):
    pay = HD + TAIL
    vmem = pl.BlockSpec(memory_space=pltpu.VMEM)
    return pl.pallas_call(
        functools.partial(far_kernel, half=half),
        in_specs=[pl.BlockSpec(memory_space=pltpu.SMEM)]
        + [vmem] * 2
        + [pl.BlockSpec(memory_space=pl.ANY)] * 3,
        out_specs=[vmem] * 2,
        out_shape=[jax.ShapeDtypeStruct((2 * QB, pay, HALF), BF16)] * 2,
        scratch_shapes=[
            pltpu.VMEM((2 * QB * SEL,) + array.shape[1:], BF16) for array in (whole, *early)
        ]
        + [pltpu.VMEM((BLK, HALF), F32)] * 2
        + [pltpu.VMEM((BLK, HALF), BF16)] * 2
        + [pltpu.SemaphoreType.DMA((4,))],
        compiler_params=pltpu.CompilerParams(vmem_limit_bytes=VMEM_BYTES),
        cost_estimate=pl.CostEstimate(
            flops=8 * 2 * QB * 4 * BLK * BLK * HD,
            bytes_accessed=5 << 20,
            transcendentals=2 * QB * BLK * BLK,
        ),
        name="far",
    )(picks, *queries, whole, *early)


def collect_kernel(where_ref, *refs, counts):
    sources, refs = [refs[: counts[0]], refs[counts[0] : sum(counts)]], refs[sum(counts) :]
    out_refs, sems = refs[:2], refs[2]

    def fetch(pick, carry):
        for part, arrays in enumerate(sources):
            array, index = where_ref[pick, 2 * part], where_ref[pick, 2 * part + 1]
            for number, source in enumerate(arrays):

                def start(source=source, part=part, index=index):
                    pltpu.make_async_copy(
                        source.at[index], out_refs[part].at[pick], sems.at[part]
                    ).start()

                pl.when(array == number)(start)
        return carry

    lax.fori_loop(0, where_ref.shape[0], fetch, 0)
    for part, out_ref in enumerate(out_refs):
        pltpu.make_async_copy(out_ref, out_ref, sems.at[part]).wait()


def collect(where, parts):
    arrays = [array for part in parts for array in part]
    return pl.pallas_call(
        functools.partial(collect_kernel, counts=tuple(len(part) for part in parts)),
        in_specs=[pl.BlockSpec(memory_space=pltpu.SMEM)]
        + [pl.BlockSpec(memory_space=pl.ANY)] * len(arrays),
        out_specs=[pl.BlockSpec(memory_space=pltpu.VMEM)] * 2,
        out_shape=[
            jax.ShapeDtypeStruct((where.shape[0],) + part[0].shape[1:], BF16) for part in parts
        ],
        scratch_shapes=[pltpu.SemaphoreType.DMA((2,))],
        compiler_params=pltpu.CompilerParams(vmem_limit_bytes=VMEM_BYTES),
        name="collect",
    )(where, *arrays)


def crossed(row):
    return (row + QB) % (2 * QB)


def merge_two_kernel(a_ref, b_ref, *out_refs):
    for row in range(2 * QB):
        acc_a, m_a, l_a = unpack_state(a_ref, row)
        acc_b, m_b, l_b = unpack_state(b_ref, crossed(row))
        top = jnp.maximum(m_a, m_b)
        f_a = jnp.exp2(m_a - top)
        f_b = jnp.exp2(m_b - top)
        out = f_a * acc_a + f_b * acc_b
        pack_state(out_refs[row // QB], row % QB, out, top, f_a * l_a + f_b * l_b)


def merge_two(mine, other):
    vmem = pl.BlockSpec(memory_space=pltpu.VMEM)
    return pl.pallas_call(
        merge_two_kernel,
        in_specs=[vmem] * 2,
        out_specs=[vmem] * 2,
        out_shape=[jax.ShapeDtypeStruct((QB,) + mine.shape[1:], BF16)] * 2,
        name="merge_two",
    )(mine, other)


def merge_last_kernel(chip_ref, a_ref, b_ref, acc_ref, m_ref, l_ref, *refs):
    chip_refs, half_refs, share_refs = refs[:2], refs[2:4], refs[4:]
    for row in range(2 * QB):
        r, i = row // QB, row % QB
        states = [unpack_state(a_ref, row), unpack_state(b_ref, crossed(row))]
        states.append(unpack_state(chip_refs[r], i))
        states.append((acc_ref[i, r], m_ref[i, r], l_ref[i, r]))
        top = functools.reduce(jnp.maximum, [m for _, m, _ in states])
        factors = [jnp.exp2(m - top) for _, m, _ in states]
        total = sum(f * l for f, (_, _, l) in zip(factors, states))
        factors = [f / total for f in factors]
        out = sum(f * acc for f, (acc, _, _) in zip(factors, states)).T.astype(BF16)
        half_refs[r][i] = out
        for n, share_ref in enumerate(share_refs):

            def keep(share_ref=share_ref, r=r, out=out):
                share_ref[r] = out

            pl.when(chip_ref[0] ^ n == i)(keep)


def merge_last(chip, mine, core_part, near_state, chip_parts):
    vmem = pl.BlockSpec(memory_space=pltpu.VMEM)
    arrays = [mine, core_part, *near_state, *chip_parts]
    own, other, *shares = pl.pallas_call(
        merge_last_kernel,
        in_specs=[pl.BlockSpec(memory_space=pltpu.SMEM)] + [vmem] * len(arrays),
        out_specs=[vmem] * (2 + QB),
        out_shape=[jax.ShapeDtypeStruct((QB, HALF, HD), BF16)] * 2
        + [jax.ShapeDtypeStruct((2, HALF, HD), BF16)] * QB,
        name="merge_last",
    )(chip, *arrays)
    return own, other, shares


def assemble_kernel(core_ref, own_ref, other_ref, out_ref):
    for i in range(QB):
        for k, ref in enumerate((own_ref, other_ref)):
            first = pl.multiple_of(i * BLK + (core_ref[0] ^ k) * HALF, HALF)
            out_ref[pl.ds(first, HALF), :] = ref[i]


def assemble(core, own, other):
    vmem = pl.BlockSpec(memory_space=pltpu.VMEM)
    return pl.pallas_call(
        assemble_kernel,
        in_specs=[pl.BlockSpec(memory_space=pltpu.SMEM)] + [vmem] * 2,
        out_specs=vmem,
        out_shape=jax.ShapeDtypeStruct((QB * BLK, HD), BF16),
        name="assemble",
    )(core, own, other)


def project_kernel(*refs):
    a_refs, w_refs, out_ref = refs[:QB], refs[QB:-1], refs[-1]
    rows = jnp.concatenate([a_ref[r] for a_ref in a_refs for r in range(2)], axis=1)
    tile = 512
    for first in range(0, out_ref.shape[1], tile):
        weight = jnp.concatenate([w_ref[:, first : first + tile] for w_ref in w_refs], axis=0)
        out_ref[:, first : first + tile] = jnp.dot(
            rows, weight, preferred_element_type=F32
        ).astype(BF16)


def project(parts, weights):
    vmem = pl.BlockSpec(memory_space=pltpu.VMEM)
    return pl.pallas_call(
        project_kernel,
        in_specs=[vmem] * (len(parts) + len(weights)),
        out_specs=vmem,
        out_shape=jax.ShapeDtypeStruct((parts[0].shape[1], weights[0].shape[1]), BF16),
        compiler_params=pltpu.CompilerParams(vmem_limit_bytes=24 << 20),
        name="project",
    )(*parts, *weights)


def shift(array, dz, dx):
    pairs = []
    for z in range(NZ):
        for x in range(NX):
            pairs.append((z * NX + x, (z + dz) % NZ * NX + (x + dx) % NX))
    return lax.ppermute(array, "ctx", pairs)


def swap(array, bits):
    return lax.ppermute(array, "head", [(h, h ^ bits) for h in range(lax.axis_size("head"))])


def after(value, *earlier):
    return lax.optimization_barrier((value, earlier))[0]


def body(queries, block_picks, span_keys, span_values, cache_keys, cache_values, out_weight):
    heads = lax.axis_size("head")
    head = lax.axis_index("head")
    part = head % GROUP
    kv = head // GROUP
    share = BLK // GROUP

    def cut(first, rows):
        pieces = []
        for cache in (cache_keys, cache_values):
            view = cache.reshape(BLOCKS, BLK, cache.shape[1])
            pieces.append(
                lax.dynamic_slice(view, (0, part * share + first, kv * HD), (BLOCKS, rows, HD))
            )
        return jnp.stack(pieces, axis=1)

    rows = share - ROWS_ZX - ROWS_XZ
    whole = lax.all_gather(cut(0, rows), "ctx", axis=0, tiled=True)

    half = BLOCKS // 2
    ring = cut(rows, ROWS_ZX)
    ring_xz = cut(rows + ROWS_ZX, ROWS_XZ)
    z1, z2 = shift(ring, 1, 0), shift(ring, -1, 0)
    a1, a2 = shift(ring_xz, 0, 1), shift(ring_xz, 0, -1)
    z3, z4 = shift(z1, 1, 0), shift(z2, -1, 0)
    a3, a4 = shift(a1[:half], 0, 1), shift(a2[half:], 0, -1)
    wide = after(jnp.concatenate([ring_xz, a1, a2, a3, a4], axis=0), z1, z2)
    c1, c2 = shift(wide, 1, 0), shift(wide, -1, 0)
    low = jnp.concatenate([ring, z1, z2, z3], axis=0)
    x1_low, x2_low = shift(low, 0, 1), shift(low, 0, -1)
    z5, z6 = shift(z3, 1, 0), shift(z4, -1, 0)
    z7, z8 = shift(z5[:half], 1, 0), shift(z6[half:], -1, 0)
    high = jnp.concatenate([z4, z5, z6, z7, z8], axis=0)
    x1_high, x2_high = shift(high, 0, 1), shift(high, 0, -1)
    c1, c2 = after((c1, c2), z5, z6)
    c3, c4 = shift(c1, 1, 0), shift(c2, -1, 0)
    c3, c4 = after((c3, c4), high)
    c5, c6 = shift(c3, 1, 0), shift(c4, -1, 0)
    x3_low = shift(after(x1_low, x2_low), 0, 1)
    x3_high = shift(after(x2_high, x1_high), 0, -1)
    half_a = wide.shape[0] // 2
    c7, c8 = shift(c5[:half_a], 1, 0), shift(c6[half_a:], -1, 0)
    arrays_zx = [low, high, x1_low, x1_high, x2_low, x2_high, x3_low, x3_high]
    arrays_xz = [wide, c1, c2, c3, c4, c5, c6, c7, c8]

    core, chip = head % 2, head // 2
    queries_core = swap(after(queries, high), 1)
    near_queries = after([queries, queries_core], x1_high, x2_high)
    near_state = near(
        jnp.stack([kv, core]).astype(jnp.int32), near_queries, span_keys, span_values
    )
    queries_early, picks_early, weight_early = after(
        (queries, block_picks, out_weight), x1_high, x2_high, x3_low, c5, c6
    )
    queries_chip = swap(queries_early, 2)
    picks_pair = jnp.stack([block_picks, swap(picks_early, 2)])
    weights = [out_weight] + [None] * (heads - 1)
    for bits in range(2, heads, 2):
        weights[bits] = swap(weight_early, bits)
    queries_chip, picks_pair, weights[::2] = after(
        (queries_chip, picks_pair, weights[::2]), *arrays_zx, *arrays_xz
    )
    group_queries = [queries, queries_core, queries_chip, swap(queries_chip, 1)]
    picks_core = swap(picks_pair, 1)
    group_picks = [picks_pair[0], picks_core[0], picks_pair[1], picks_core[1]]
    for bits in range(0, heads, 2):
        weights[bits + 1] = swap(weights[bits], 1)
    picks = [group_pick.reshape(QB * SEL) for group_pick in group_picks]

    every_pick = jnp.concatenate([picks[r] for r in (2, 3, 0, 1)])
    owner, local = every_pick // BLOCKS, every_pick % BLOCKS
    ctx = lax.axis_index("ctx")
    dz = (owner // NX - ctx // NX) % NZ
    dx = (owner % NX - ctx % NX) % NX
    order_x = jnp.where(dx == 0, 0, jnp.where(dx == 3, 1, jnp.where(dx == 1, 2, 3)))
    order_z = jnp.where(dz == 0, 0, jnp.where(dz > NZ // 2, 2 * (NZ - dz) - 1, 2 * dz))
    order_z = jnp.where(dz == NZ // 2, NZ - 1, order_z)
    place = order_z * BLOCKS + local
    upper = (place >= low.shape[0]).astype(jnp.int32)
    place_a = order_x * BLOCKS + local
    upper_a = ((place_a >= half_a) & (order_z == NZ - 1)).astype(jnp.int32)
    where = jnp.stack(
        [
            2 * order_x + upper,
            place - low.shape[0] * upper,
            order_z + upper_a,
            place_a - half_a * upper_a,
        ],
        axis=-1,
    )
    early = collect(where.astype(jnp.int32), [arrays_zx, arrays_xz])

    picks, group_queries, weights, near_state, early = lax.optimization_barrier(
        (picks, group_queries, weights, near_state, early)
    )

    def far_of(first, second, earlier, half):
        return far(
            after(jnp.concatenate([picks[first], picks[second], core[None]]), *earlier),
            [group_queries[first], group_queries[second]],
            whole,
            early,
            half,
        )

    chip_here, chip_there = far_of(2, 3, [], 0)
    for_chip = merge_two(chip_here, swap(chip_there, 1))
    chip_parts = [swap(piece, 2) for piece in for_chip]
    own_here, own_there = far_of(0, 1, for_chip, 1)
    core_part = swap(after(own_there, *chip_parts), 1)
    own, other, shares = merge_last(chip[None], own_here, core_part, near_state, chip_parts)
    parts = [shares[0]] + [swap(shares[n], 2 * n) for n in range(1, QB)]
    attention = assemble(core[None], own, swap(other, 1))
    return attention, project(after(parts, attention), weights)


def solution(mesh):
    placed = (
        P("ctx", "head"),
        P("ctx", "head", None),
        P("ctx", None),
        P("ctx", None),
        P("ctx", None),
        P("ctx", None),
        P("head", None),
    )
    return jax.shard_map(
        body,
        mesh=mesh,
        in_specs=placed,
        out_specs=(P("ctx", "head"), P(("ctx", "head"), None)),
        check_vma=False,
    )
```

```python
import functools
import math

import jax
import jax.numpy as jnp
from jax import lax
from jax.experimental import pallas as pl
from jax.experimental.pallas import tpu as pltpu
from jax.sharding import PartitionSpec as P

HD = 128
GROUP = 4
BLK = 512
HALF = BLK // 2
SEL = 4
QB = 4
BLOCKS = 8
TAIL = 16
SCALE = math.log2(math.e) / math.sqrt(HD)
NEG = -1e30
F32 = jnp.float32
BF16 = jnp.bfloat16
NX = 4
NZ = 8
RING_ROWS = 32
VMEM_BYTES = 56 << 20


def dot_nt(a, b):
    return lax.dot_general(a, b, (((1,), (1,)), ((), ())), preferred_element_type=F32)


def dot_tn(a, b):
    return lax.dot_general(a, b, (((0,), (0,)), ((), ())), preferred_element_type=F32)


def rounded_top(raw):
    return (raw * SCALE).astype(BF16).astype(F32)


def near_kernel(place_ref, *refs):
    q_refs, (k_ref, v_ref, acc_ref, m_ref, l_ref) = refs[:2], refs[2:]
    keys = lax.broadcasted_iota(jnp.int32, (BLK, HALF), 0)
    rows = lax.broadcasted_iota(jnp.int32, (BLK, HALF), 1) + place_ref[1] * HALF
    for r, q_ref in enumerate(q_refs):
        scores = jnp.where(keys <= rows, dot_nt(k_ref[...], q_ref[...]), NEG)
        top = rounded_top(jnp.max(scores, axis=0, keepdims=True))
        weights = jnp.exp2(scores * SCALE - top)
        m_ref[0, r] = top
        l_ref[0, r] = jnp.sum(weights, axis=0, keepdims=True)
        acc_ref[0, r] = dot_tn(v_ref[...], weights.astype(BF16))


def near(place, queries, span_keys, span_values):
    grid_spec = pltpu.PrefetchScalarGridSpec(
        num_scalar_prefetch=1,
        grid=(QB,),
        in_specs=[pl.BlockSpec((HALF, HD), lambda i, place: (2 * i + place[1], 0))] * 2
        + [pl.BlockSpec((BLK, HD), lambda i, place: (i, place[0]))] * 2,
        out_specs=[
            pl.BlockSpec((1, 2, HD, HALF), lambda i, place: (i, 0, 0, 0)),
            pl.BlockSpec((1, 2, 1, HALF), lambda i, place: (i, 0, 0, 0)),
            pl.BlockSpec((1, 2, 1, HALF), lambda i, place: (i, 0, 0, 0)),
        ],
    )
    return pl.pallas_call(
        near_kernel,
        grid_spec=grid_spec,
        out_shape=[
            jax.ShapeDtypeStruct((QB, 2, HD, HALF), F32),
            jax.ShapeDtypeStruct((QB, 2, 1, HALF), F32),
            jax.ShapeDtypeStruct((QB, 2, 1, HALF), F32),
        ],
        cost_estimate=pl.CostEstimate(
            flops=QB * 4 * BLK * BLK * HD, bytes_accessed=4 << 20, transcendentals=QB * BLK * BLK
        ),
        name="near",
    )(place, *queries, span_keys, span_values)


def pack_state(ref, i, out, top, total):
    ref[i, :HD, :] = out.astype(BF16)
    high = total.astype(BF16)
    low = (total - high.astype(F32)).astype(BF16)
    ref[i, HD:, :] = jnp.concatenate(
        [top.astype(BF16), high, low, jnp.zeros((TAIL - 3, out.shape[1]), BF16)], axis=0
    )


def unpack_state(ref, i):
    tail = ref[i, HD:, :].astype(F32)
    return ref[i, :HD, :].astype(F32), tail[0:1], tail[1:2] + tail[2:3]


def far_kernel(picks_ref, *refs, half):
    q_refs, whole_ref, early_ref, refs = refs[:2], refs[2], refs[3], refs[4:]
    out_refs, (buffer, early), refs = refs[:2], refs[2:4], refs[4:]
    score_refs, weight_refs, sems = refs[:2], refs[2:4], refs[4]
    picks = 2 * QB * SEL
    early_copy = pltpu.make_async_copy(
        early_ref.at[pl.ds(half * picks, picks)], early, sems.at[0]
    )
    early_copy.start()
    for pick in range(picks):
        sem = sems.at[1 if pick < SEL else 2]
        pltpu.make_async_copy(whole_ref.at[picks_ref[pick]], buffer.at[pick], sem).start()
    early_copy.wait()
    steps = [(row, k) for row in range(2 * QB) for k in range(2)]
    sums = {}

    def fetched(first, count, sem):
        held = buffer.at[pl.ds(first, count)]
        pltpu.make_async_copy(held, held, sem).wait()

    def joined(row, which):
        return jnp.concatenate(
            [held[row * SEL + j, which] for held in (buffer, early) for j in range(SEL)], axis=0
        )

    def score(number):
        row, k = steps[number]
        if number == 0:
            fetched(0, SEL, sems.at[1])
        if number == 2:
            fetched(SEL, picks - SEL, sems.at[2])
        first = row % QB * BLK + (picks_ref[picks] ^ k) * HALF
        tokens = pl.ds(pl.multiple_of(first, HALF), HALF)
        score_refs[number % 2][...] = dot_nt(joined(row, 0), q_refs[row // QB][tokens, :])

    def soften(number):
        score_ref, weight_ref = score_refs[number % 2], weight_refs[number % 2]
        tops, totals = [], []
        for lane in range(0, HALF, HD):
            lanes = slice(lane, lane + HD)
            top = rounded_top(jnp.max(score_ref[:, lanes], axis=0, keepdims=True))
            total = jnp.zeros((8, HD), F32)
            for row in range(0, BLK, 64):
                weights = jnp.exp2((score_ref[row : row + 64, lanes] * SCALE - top).astype(BF16))
                weight_ref[row : row + 64, lanes] = weights
                total = total + jnp.sum(weights.astype(F32).reshape(8, 8, HD), axis=0)
            tops.append(top)
            totals.append(jnp.sum(total, axis=0, keepdims=True))
        sums[number] = jnp.concatenate(tops, axis=1), jnp.concatenate(totals, axis=1)

    def finish(number):
        row, k = steps[number]
        top, total = sums.pop(number)
        out = dot_tn(joined(row, 1), weight_refs[number % 2][...])
        pack_state(out_refs[k], row, out, top, total)

    for number in range(len(steps) + 2):
        if number < len(steps):
            score(number)
        if number >= 2:
            finish(number - 2)
        if 1 <= number <= len(steps):
            soften(number - 1)


def far(picks, queries, whole, early, half):
    pay = HD + TAIL
    vmem = pl.BlockSpec(memory_space=pltpu.VMEM)
    return pl.pallas_call(
        functools.partial(far_kernel, half=half),
        in_specs=[pl.BlockSpec(memory_space=pltpu.SMEM)]
        + [vmem] * 2
        + [pl.BlockSpec(memory_space=pl.ANY)] * 2,
        out_specs=[vmem] * 2,
        out_shape=[jax.ShapeDtypeStruct((2 * QB, pay, HALF), BF16)] * 2,
        scratch_shapes=[
            pltpu.VMEM((2 * QB * SEL,) + array.shape[1:], BF16) for array in (whole, early)
        ]
        + [pltpu.VMEM((BLK, HALF), F32)] * 2
        + [pltpu.VMEM((BLK, HALF), BF16)] * 2
        + [pltpu.SemaphoreType.DMA((3,))],
        compiler_params=pltpu.CompilerParams(vmem_limit_bytes=VMEM_BYTES),
        cost_estimate=pl.CostEstimate(
            flops=8 * 2 * QB * 4 * BLK * BLK * HD,
            bytes_accessed=5 << 20,
            transcendentals=2 * QB * BLK * BLK,
        ),
        name="far",
    )(picks, *queries, whole, early)


def collect_kernel(where_ref, *refs):
    sources, out_ref, sem = refs[:-2], refs[-2], refs[-1]

    def fetch(pick, carry):
        array, index = where_ref[pick, 0], where_ref[pick, 1]
        for number, source in enumerate(sources):

            def start(source=source):
                pltpu.make_async_copy(source.at[index], out_ref.at[pick], sem).start()

            pl.when(array == number)(start)
        return carry

    lax.fori_loop(0, out_ref.shape[0], fetch, 0)
    pltpu.make_async_copy(out_ref, out_ref, sem).wait()


def collect(where, arrays):
    return pl.pallas_call(
        collect_kernel,
        in_specs=[pl.BlockSpec(memory_space=pltpu.SMEM)]
        + [pl.BlockSpec(memory_space=pl.ANY)] * len(arrays),
        out_specs=pl.BlockSpec(memory_space=pltpu.VMEM),
        out_shape=jax.ShapeDtypeStruct((where.shape[0],) + arrays[0].shape[1:], BF16),
        scratch_shapes=[pltpu.SemaphoreType.DMA],
        compiler_params=pltpu.CompilerParams(vmem_limit_bytes=VMEM_BYTES),
        name="collect",
    )(where, *arrays)


def crossed(row):
    return (row + QB) % (2 * QB)


def merge_two_kernel(a_ref, b_ref, *out_refs):
    for row in range(2 * QB):
        acc_a, m_a, l_a = unpack_state(a_ref, row)
        acc_b, m_b, l_b = unpack_state(b_ref, crossed(row))
        top = jnp.maximum(m_a, m_b)
        f_a = jnp.exp2(m_a - top)
        f_b = jnp.exp2(m_b - top)
        out = f_a * acc_a + f_b * acc_b
        pack_state(out_refs[row // QB], row % QB, out, top, f_a * l_a + f_b * l_b)


def merge_two(mine, other):
    vmem = pl.BlockSpec(memory_space=pltpu.VMEM)
    return pl.pallas_call(
        merge_two_kernel,
        in_specs=[vmem] * 2,
        out_specs=[vmem] * 2,
        out_shape=[jax.ShapeDtypeStruct((QB,) + mine.shape[1:], BF16)] * 2,
        name="merge_two",
    )(mine, other)


def merge_last_kernel(chip_ref, a_ref, b_ref, acc_ref, m_ref, l_ref, *refs):
    chip_refs, half_refs, share_refs = refs[:2], refs[2:4], refs[4:]
    for row in range(2 * QB):
        r, i = row // QB, row % QB
        states = [unpack_state(a_ref, row), unpack_state(b_ref, crossed(row))]
        states.append(unpack_state(chip_refs[r], i))
        states.append((acc_ref[i, r], m_ref[i, r], l_ref[i, r]))
        top = functools.reduce(jnp.maximum, [m for _, m, _ in states])
        factors = [jnp.exp2(m - top) for _, m, _ in states]
        total = sum(f * l for f, (_, _, l) in zip(factors, states))
        factors = [f / total for f in factors]
        out = sum(f * acc for f, (acc, _, _) in zip(factors, states)).T.astype(BF16)
        half_refs[r][i] = out
        for n, share_ref in enumerate(share_refs):

            def keep(share_ref=share_ref, r=r, out=out):
                share_ref[r] = out

            pl.when(chip_ref[0] ^ n == i)(keep)


def merge_last(chip, mine, core_part, near_state, chip_parts):
    vmem = pl.BlockSpec(memory_space=pltpu.VMEM)
    arrays = [mine, core_part, *near_state, *chip_parts]
    own, other, *shares = pl.pallas_call(
        merge_last_kernel,
        in_specs=[pl.BlockSpec(memory_space=pltpu.SMEM)] + [vmem] * len(arrays),
        out_specs=[vmem] * (2 + QB),
        out_shape=[jax.ShapeDtypeStruct((QB, HALF, HD), BF16)] * 2
        + [jax.ShapeDtypeStruct((2, HALF, HD), BF16)] * QB,
        name="merge_last",
    )(chip, *arrays)
    return own, other, shares


def assemble_kernel(core_ref, own_ref, other_ref, out_ref):
    for i in range(QB):
        for k, ref in enumerate((own_ref, other_ref)):
            first = pl.multiple_of(i * BLK + (core_ref[0] ^ k) * HALF, HALF)
            out_ref[pl.ds(first, HALF), :] = ref[i]


def assemble(core, own, other):
    vmem = pl.BlockSpec(memory_space=pltpu.VMEM)
    return pl.pallas_call(
        assemble_kernel,
        in_specs=[pl.BlockSpec(memory_space=pltpu.SMEM)] + [vmem] * 2,
        out_specs=vmem,
        out_shape=jax.ShapeDtypeStruct((QB * BLK, HD), BF16),
        name="assemble",
    )(core, own, other)


def project_kernel(*refs):
    a_refs, w_refs, out_ref = refs[:QB], refs[QB:-1], refs[-1]
    rows = jnp.concatenate([a_ref[r] for a_ref in a_refs for r in range(2)], axis=1)
    tile = 512
    for first in range(0, out_ref.shape[1], tile):
        weight = jnp.concatenate([w_ref[:, first : first + tile] for w_ref in w_refs], axis=0)
        out_ref[:, first : first + tile] = jnp.dot(
            rows, weight, preferred_element_type=F32
        ).astype(BF16)


def project(parts, weights):
    vmem = pl.BlockSpec(memory_space=pltpu.VMEM)
    return pl.pallas_call(
        project_kernel,
        in_specs=[vmem] * (len(parts) + len(weights)),
        out_specs=vmem,
        out_shape=jax.ShapeDtypeStruct((parts[0].shape[1], weights[0].shape[1]), BF16),
        compiler_params=pltpu.CompilerParams(vmem_limit_bytes=VMEM_BYTES),
        name="project",
    )(*parts, *weights)


def shift(array, dz, dx):
    pairs = []
    for z in range(NZ):
        for x in range(NX):
            pairs.append((z * NX + x, (z + dz) % NZ * NX + (x + dx) % NX))
    return lax.ppermute(array, "ctx", pairs)


def swap(array, bits):
    return lax.ppermute(array, "head", [(h, h ^ bits) for h in range(lax.axis_size("head"))])


def after(value, *earlier):
    return lax.optimization_barrier((value, earlier))[0]


def body(queries, block_picks, span_keys, span_values, cache_keys, cache_values, out_weight):
    heads = lax.axis_size("head")
    head = lax.axis_index("head")
    part = head % GROUP
    kv = head // GROUP
    share = BLK // GROUP

    def cut(first, rows):
        pieces = []
        for cache in (cache_keys, cache_values):
            view = cache.reshape(BLOCKS, BLK, cache.shape[1])
            pieces.append(
                lax.dynamic_slice(view, (0, part * share + first, kv * HD), (BLOCKS, rows, HD))
            )
        return jnp.stack(pieces, axis=1)

    whole = lax.all_gather(cut(0, share - RING_ROWS), "ctx", axis=0, tiled=True)

    ring = cut(share - RING_ROWS, RING_ROWS)
    z1, z2 = shift(ring, 1, 0), shift(ring, -1, 0)
    z3, z4 = shift(z1, 1, 0), shift(z2, -1, 0)
    low = jnp.concatenate([ring, z1, z2, z3], axis=0)
    x1_low, x2_low = shift(low, 0, 1), shift(low, 0, -1)
    z5, z6 = shift(z3, 1, 0), shift(z4, -1, 0)
    half = BLOCKS // 2
    z7, z8 = shift(z5[:half], 1, 0), shift(z6[half:], -1, 0)
    high = jnp.concatenate([z4, z5, z6, z7, z8], axis=0)
    x1_high, x2_high = shift(high, 0, 1), shift(high, 0, -1)
    x3_low, x3_high = shift(x1_low, 0, 1), shift(x2_high, 0, -1)
    ring_arrays = [low, high, x1_low, x1_high, x2_low, x2_high, x3_low, x3_high]

    core, chip = head % 2, head // 2
    queries_core = swap(after(queries, low), 1)
    near_queries = after([queries, queries_core], *ring_arrays[2:6])
    near_state = near(
        jnp.stack([kv, core]).astype(jnp.int32), near_queries, span_keys, span_values
    )
    queries_early, picks_early, weight_early = after(
        (queries, block_picks, out_weight), *ring_arrays[2:6]
    )
    queries_chip = swap(queries_early, 2)
    picks_pair = jnp.stack([block_picks, swap(picks_early, 2)])
    weights = [out_weight] + [None] * (heads - 1)
    for bits in range(2, heads, 2):
        weights[bits] = swap(weight_early, bits)
    queries_chip, picks_pair, weights[::2] = after(
        (queries_chip, picks_pair, weights[::2]), *ring_arrays
    )
    group_queries = [queries, queries_core, queries_chip, swap(queries_chip, 1)]
    picks_core = swap(picks_pair, 1)
    group_picks = [picks_pair[0], picks_core[0], picks_pair[1], picks_core[1]]
    for bits in range(0, heads, 2):
        weights[bits + 1] = swap(weights[bits], 1)
    picks = [group_pick.reshape(QB * SEL) for group_pick in group_picks]

    every_pick = jnp.concatenate([picks[r] for r in (2, 3, 0, 1)])
    owner, local = every_pick // BLOCKS, every_pick % BLOCKS
    ctx = lax.axis_index("ctx")
    dz = (owner // NX - ctx // NX) % NZ
    dx = (owner % NX - ctx % NX) % NX
    order_x = jnp.where(dx == 0, 0, jnp.where(dx == 3, 1, jnp.where(dx == 1, 2, 3)))
    order_z = jnp.where(dz == 0, 0, jnp.where(dz > NZ // 2, 2 * (NZ - dz) - 1, 2 * dz))
    place = jnp.where(dz == NZ // 2, NZ - 1, order_z) * BLOCKS + local
    upper = (place >= low.shape[0]).astype(jnp.int32)
    where = jnp.stack([2 * order_x + upper, place - low.shape[0] * upper], axis=-1)
    early = collect(where.astype(jnp.int32), ring_arrays)

    picks, group_queries, weights, near_state, early = lax.optimization_barrier(
        (picks, group_queries, weights, near_state, early)
    )

    def far_of(first, second, earlier, half):
        return far(
            after(jnp.concatenate([picks[first], picks[second], core[None]]), *earlier),
            [group_queries[first], group_queries[second]],
            whole,
            early,
            half,
        )

    chip_here, chip_there = far_of(2, 3, [], 0)
    for_chip = merge_two(chip_here, swap(chip_there, 1))
    chip_parts = [swap(piece, 2) for piece in for_chip]
    own_here, own_there = far_of(0, 1, for_chip, 1)
    core_part = swap(after(own_there, *chip_parts), 1)
    own, other, shares = merge_last(chip[None], own_here, core_part, near_state, chip_parts)
    parts = [shares[0]] + [swap(shares[n], 2 * n) for n in range(1, QB)]
    attention = assemble(core[None], own, swap(other, 1))
    return attention, project(after(parts, attention), weights)


def solution(mesh):
    placed = (
        P("ctx", "head"),
        P("ctx", "head", None),
        P("ctx", None),
        P("ctx", None),
        P("ctx", None),
        P("ctx", None),
        P("head", None),
    )
    return jax.shard_map(
        body,
        mesh=mesh,
        in_specs=placed,
        out_specs=(P("ctx", "head"), P(("ctx", "head"), None)),
        check_vma=False,
    )
```

```python
import functools
import math

import jax
import jax.numpy as jnp
from jax import lax
from jax.experimental import pallas as pl
from jax.experimental.pallas import tpu as pltpu
from jax.sharding import PartitionSpec as P

HD = 128
GROUP = 4
BLK = 512
HALF = BLK // 2
SEL = 4
QB = 4
BLOCKS = 8
TAIL = 16
SCALE = math.log2(math.e) / math.sqrt(HD)
NEG = -1e30
F32 = jnp.float32
BF16 = jnp.bfloat16
NX = 4
NZ = 8
RING_ROWS = 32
VMEM_BYTES = 56 << 20


def dot_nt(a, b):
    return lax.dot_general(a, b, (((1,), (1,)), ((), ())), preferred_element_type=F32)


def dot_tn(a, b):
    return lax.dot_general(a, b, (((0,), (0,)), ((), ())), preferred_element_type=F32)


def rounded_top(raw):
    return (raw * SCALE).astype(BF16).astype(F32)


def near_kernel(place_ref, *refs):
    q_refs, (k_ref, v_ref, acc_ref, m_ref, l_ref) = refs[:2], refs[2:]
    keys = lax.broadcasted_iota(jnp.int32, (BLK, HALF), 0)
    rows = lax.broadcasted_iota(jnp.int32, (BLK, HALF), 1) + place_ref[1] * HALF
    for r, q_ref in enumerate(q_refs):
        scores = jnp.where(keys <= rows, dot_nt(k_ref[...], q_ref[...]), NEG)
        top = rounded_top(jnp.max(scores, axis=0, keepdims=True))
        weights = jnp.exp2(scores * SCALE - top)
        m_ref[0, r] = top
        l_ref[0, r] = jnp.sum(weights, axis=0, keepdims=True)
        acc_ref[0, r] = dot_tn(v_ref[...], weights.astype(BF16))


def near(place, queries, span_keys, span_values):
    grid_spec = pltpu.PrefetchScalarGridSpec(
        num_scalar_prefetch=1,
        grid=(QB,),
        in_specs=[pl.BlockSpec((HALF, HD), lambda i, place: (2 * i + place[1], 0))] * 2
        + [pl.BlockSpec((BLK, HD), lambda i, place: (i, place[0]))] * 2,
        out_specs=[
            pl.BlockSpec((1, 2, HD, HALF), lambda i, place: (i, 0, 0, 0)),
            pl.BlockSpec((1, 2, 1, HALF), lambda i, place: (i, 0, 0, 0)),
            pl.BlockSpec((1, 2, 1, HALF), lambda i, place: (i, 0, 0, 0)),
        ],
    )
    return pl.pallas_call(
        near_kernel,
        grid_spec=grid_spec,
        out_shape=[
            jax.ShapeDtypeStruct((QB, 2, HD, HALF), F32),
            jax.ShapeDtypeStruct((QB, 2, 1, HALF), F32),
            jax.ShapeDtypeStruct((QB, 2, 1, HALF), F32),
        ],
        cost_estimate=pl.CostEstimate(
            flops=QB * 4 * BLK * BLK * HD, bytes_accessed=4 << 20, transcendentals=QB * BLK * BLK
        ),
        name="near",
    )(place, *queries, span_keys, span_values)


def pack_state(ref, i, out, top, total):
    ref[i, :HD, :] = out.astype(BF16)
    high = total.astype(BF16)
    low = (total - high.astype(F32)).astype(BF16)
    ref[i, HD:, :] = jnp.concatenate(
        [top.astype(BF16), high, low, jnp.zeros((TAIL - 3, out.shape[1]), BF16)], axis=0
    )


def unpack_state(ref, i):
    tail = ref[i, HD:, :].astype(F32)
    return ref[i, :HD, :].astype(F32), tail[0:1], tail[1:2] + tail[2:3]


def scale_kernel(*refs):
    count = len(refs) // 2
    for q_ref, out_ref in zip(refs[:count], refs[count:]):
        scaled = q_ref[...].astype(F32) * SCALE
        high = scaled.astype(BF16)
        out_ref[:, :HD] = high
        out_ref[:, HD:] = (scaled - high.astype(F32)).astype(BF16)


def scale(queries):
    count = len(queries)
    return pl.pallas_call(
        scale_kernel,
        grid=(QB,),
        in_specs=[pl.BlockSpec((BLK, HD), lambda i: (i, 0))] * count,
        out_specs=[pl.BlockSpec((BLK, 2 * HD), lambda i: (i, 0))] * count,
        out_shape=[jax.ShapeDtypeStruct((QB * BLK, 2 * HD), BF16)] * count,
        name="scale",
    )(*queries)


def far_kernel(picks_ref, *refs, half):
    q_refs, whole_ref, early_ref, refs = refs[:2], refs[2], refs[3], refs[4:]
    out_refs, (buffer, early), refs = refs[:2], refs[2:4], refs[4:]
    score_refs, weight_refs, sems = refs[:2], refs[2:4], refs[4]
    picks = 2 * QB * SEL
    early_copy = pltpu.make_async_copy(
        early_ref.at[pl.ds(half * picks, picks)], early, sems.at[0]
    )
    early_copy.start()
    for pick in range(picks):
        sem = sems.at[1 if pick < SEL else 2]
        pltpu.make_async_copy(whole_ref.at[picks_ref[pick]], buffer.at[pick], sem).start()
    early_copy.wait()
    steps = [(row, k) for row in range(2 * QB) for k in range(2)]
    sums = {}

    def fetched(first, count, sem):
        held = buffer.at[pl.ds(first, count)]
        pltpu.make_async_copy(held, held, sem).wait()

    def joined(row, which):
        return jnp.concatenate(
            [held[row * SEL + j, which] for held in (buffer, early) for j in range(SEL)], axis=0
        )

    def score(number):
        row, k = steps[number]
        if number == 0:
            fetched(0, SEL, sems.at[1])
        if number == 2:
            fetched(SEL, picks - SEL, sems.at[2])
        first = row % QB * BLK + (picks_ref[picks] ^ k) * HALF
        tokens = pl.ds(pl.multiple_of(first, HALF), HALF)
        keys = joined(row, 0)
        twice = jnp.concatenate([keys, keys], axis=1)
        score_refs[number % 2][...] = dot_nt(twice, q_refs[row // QB][tokens, :])

    def soften(number):
        score_ref, weight_ref = score_refs[number % 2], weight_refs[number % 2]
        tops, totals = [], []
        for lane in range(0, HALF, HD):
            lanes = slice(lane, lane + HD)
            top = jnp.max(score_ref[:, lanes], axis=0, keepdims=True).astype(BF16).astype(F32)
            total = jnp.zeros((8, HD), F32)
            for row in range(0, BLK, 64):
                weights = jnp.exp2(score_ref[row : row + 64, lanes] - top)
                weight_ref[row : row + 64, lanes] = weights.astype(BF16)
                total = total + jnp.sum(weights.reshape(8, 8, HD), axis=0)
            tops.append(top)
            totals.append(jnp.sum(total, axis=0, keepdims=True))
        sums[number] = jnp.concatenate(tops, axis=1), jnp.concatenate(totals, axis=1)

    def finish(number):
        row, k = steps[number]
        top, total = sums.pop(number)
        out = dot_tn(joined(row, 1), weight_refs[number % 2][...])
        pack_state(out_refs[k], row, out, top, total)

    for number in range(len(steps) + 2):
        if number < len(steps):
            score(number)
        if number >= 2:
            finish(number - 2)
        if 1 <= number <= len(steps):
            soften(number - 1)


def far(picks, queries, whole, early, half):
    pay = HD + TAIL
    vmem = pl.BlockSpec(memory_space=pltpu.VMEM)
    return pl.pallas_call(
        functools.partial(far_kernel, half=half),
        in_specs=[pl.BlockSpec(memory_space=pltpu.SMEM)]
        + [vmem] * 2
        + [pl.BlockSpec(memory_space=pl.ANY)] * 2,
        out_specs=[vmem] * 2,
        out_shape=[jax.ShapeDtypeStruct((2 * QB, pay, HALF), BF16)] * 2,
        scratch_shapes=[
            pltpu.VMEM((2 * QB * SEL,) + array.shape[1:], BF16) for array in (whole, early)
        ]
        + [pltpu.VMEM((BLK, HALF), F32)] * 2
        + [pltpu.VMEM((BLK, HALF), BF16)] * 2
        + [pltpu.SemaphoreType.DMA((3,))],
        compiler_params=pltpu.CompilerParams(vmem_limit_bytes=VMEM_BYTES),
        cost_estimate=pl.CostEstimate(
            flops=8 * 2 * QB * 4 * BLK * BLK * HD,
            bytes_accessed=5 << 20,
            transcendentals=2 * QB * BLK * BLK,
        ),
        name="far",
    )(picks, *queries, whole, early)


def collect_kernel(where_ref, *refs):
    sources, out_ref, sem = refs[:-2], refs[-2], refs[-1]

    def fetch(pick, carry):
        array, index = where_ref[pick, 0], where_ref[pick, 1]
        for number, source in enumerate(sources):

            def start(source=source):
                pltpu.make_async_copy(source.at[index], out_ref.at[pick], sem).start()

            pl.when(array == number)(start)
        return carry

    lax.fori_loop(0, out_ref.shape[0], fetch, 0)
    pltpu.make_async_copy(out_ref, out_ref, sem).wait()


def collect(where, arrays):
    return pl.pallas_call(
        collect_kernel,
        in_specs=[pl.BlockSpec(memory_space=pltpu.SMEM)]
        + [pl.BlockSpec(memory_space=pl.ANY)] * len(arrays),
        out_specs=pl.BlockSpec(memory_space=pltpu.VMEM),
        out_shape=jax.ShapeDtypeStruct((where.shape[0],) + arrays[0].shape[1:], BF16),
        scratch_shapes=[pltpu.SemaphoreType.DMA],
        compiler_params=pltpu.CompilerParams(vmem_limit_bytes=VMEM_BYTES),
        name="collect",
    )(where, *arrays)


def crossed(row):
    return (row + QB) % (2 * QB)


def merge_two_kernel(a_ref, b_ref, *out_refs):
    for row in range(2 * QB):
        acc_a, m_a, l_a = unpack_state(a_ref, row)
        acc_b, m_b, l_b = unpack_state(b_ref, crossed(row))
        top = jnp.maximum(m_a, m_b)
        f_a = jnp.exp2(m_a - top)
        f_b = jnp.exp2(m_b - top)
        out = f_a * acc_a + f_b * acc_b
        pack_state(out_refs[row // QB], row % QB, out, top, f_a * l_a + f_b * l_b)


def merge_two(mine, other):
    vmem = pl.BlockSpec(memory_space=pltpu.VMEM)
    return pl.pallas_call(
        merge_two_kernel,
        in_specs=[vmem] * 2,
        out_specs=[vmem] * 2,
        out_shape=[jax.ShapeDtypeStruct((QB,) + mine.shape[1:], BF16)] * 2,
        name="merge_two",
    )(mine, other)


def merge_chip_kernel(acc_ref, m_ref, l_ref, *refs):
    chip_refs, (acc_out, m_out, l_out) = refs[:2], refs[2:]
    for row in range(2 * QB):
        r, i = row // QB, row % QB
        acc, m, l = unpack_state(chip_refs[r], i)
        top = jnp.maximum(m, m_ref[i, r])
        f_chip = jnp.exp2(m - top)
        f_near = jnp.exp2(m_ref[i, r] - top)
        m_out[i, r] = top
        l_out[i, r] = f_chip * l + f_near * l_ref[i, r]
        acc_out[i, r] = f_chip * acc + f_near * acc_ref[i, r]


def merge_chip(near_state, chip_parts):
    vmem = pl.BlockSpec(memory_space=pltpu.VMEM)
    return pl.pallas_call(
        merge_chip_kernel,
        in_specs=[vmem] * 5,
        out_specs=[vmem] * 3,
        out_shape=[jax.ShapeDtypeStruct(array.shape, F32) for array in near_state],
        cost_estimate=pl.CostEstimate(
            flops=8 * QB * 4 * BLK * BLK * HD, bytes_accessed=4 << 20, transcendentals=8 * BLK
        ),
        name="merge_chip",
    )(*near_state, *chip_parts)


def merge_last_kernel(chip_ref, a_ref, b_ref, acc_ref, m_ref, l_ref, *refs):
    half_refs, share_refs = refs[:2], refs[2:]
    for row in range(2 * QB):
        r, i = row // QB, row % QB
        states = [unpack_state(a_ref, row), unpack_state(b_ref, crossed(row))]
        states.append((acc_ref[i, r], m_ref[i, r], l_ref[i, r]))
        top = functools.reduce(jnp.maximum, [m for _, m, _ in states])
        factors = [jnp.exp2(m - top) for _, m, _ in states]
        total = sum(f * l for f, (_, _, l) in zip(factors, states))
        factors = [f / total for f in factors]
        out = sum(f * acc for f, (acc, _, _) in zip(factors, states)).T.astype(BF16)
        half_refs[r][i] = out
        for n, share_ref in enumerate(share_refs):

            def keep(share_ref=share_ref, r=r, out=out):
                share_ref[r] = out

            pl.when(chip_ref[0] ^ n == i)(keep)


def merge_last(chip, mine, core_part, other_state):
    vmem = pl.BlockSpec(memory_space=pltpu.VMEM)
    arrays = [mine, core_part, *other_state]
    own, other, *shares = pl.pallas_call(
        merge_last_kernel,
        in_specs=[pl.BlockSpec(memory_space=pltpu.SMEM)] + [vmem] * len(arrays),
        out_specs=[vmem] * (2 + QB),
        out_shape=[jax.ShapeDtypeStruct((QB, HALF, HD), BF16)] * 2
        + [jax.ShapeDtypeStruct((2, HALF, HD), BF16)] * QB,
        name="merge_last",
    )(chip, *arrays)
    return own, other, shares


def assemble_kernel(core_ref, own_ref, other_ref, out_ref):
    for i in range(QB):
        for k, ref in enumerate((own_ref, other_ref)):
            first = pl.multiple_of(i * BLK + (core_ref[0] ^ k) * HALF, HALF)
            out_ref[pl.ds(first, HALF), :] = ref[i]


def assemble(core, own, other):
    vmem = pl.BlockSpec(memory_space=pltpu.VMEM)
    return pl.pallas_call(
        assemble_kernel,
        in_specs=[pl.BlockSpec(memory_space=pltpu.SMEM)] + [vmem] * 2,
        out_specs=vmem,
        out_shape=jax.ShapeDtypeStruct((QB * BLK, HD), BF16),
        name="assemble",
    )(core, own, other)


def project_kernel(*refs):
    a_refs, w_refs, out_ref = refs[:QB], refs[QB:-1], refs[-1]
    rows = jnp.concatenate([a_ref[r] for a_ref in a_refs for r in range(2)], axis=1)
    tile = 512
    for first in range(0, out_ref.shape[1], tile):
        weight = jnp.concatenate([w_ref[:, first : first + tile] for w_ref in w_refs], axis=0)
        out_ref[:, first : first + tile] = jnp.dot(
            rows, weight, preferred_element_type=F32
        ).astype(BF16)


def project(parts, weights):
    vmem = pl.BlockSpec(memory_space=pltpu.VMEM)
    return pl.pallas_call(
        project_kernel,
        in_specs=[vmem] * (len(parts) + len(weights)),
        out_specs=vmem,
        out_shape=jax.ShapeDtypeStruct((parts[0].shape[1], weights[0].shape[1]), BF16),
        compiler_params=pltpu.CompilerParams(vmem_limit_bytes=24 << 20),
        name="project",
    )(*parts, *weights)


def shift(array, dz, dx):
    pairs = []
    for z in range(NZ):
        for x in range(NX):
            pairs.append((z * NX + x, (z + dz) % NZ * NX + (x + dx) % NX))
    return lax.ppermute(array, "ctx", pairs)


def swap(array, bits):
    return lax.ppermute(array, "head", [(h, h ^ bits) for h in range(lax.axis_size("head"))])


def after(value, *earlier):
    return lax.optimization_barrier((value, earlier))[0]


def body(queries, block_picks, span_keys, span_values, cache_keys, cache_values, out_weight):
    heads = lax.axis_size("head")
    head = lax.axis_index("head")
    part = head % GROUP
    kv = head // GROUP
    share = BLK // GROUP

    def cut(first, rows):
        pieces = []
        for cache in (cache_keys, cache_values):
            view = cache.reshape(BLOCKS, BLK, cache.shape[1])
            pieces.append(
                lax.dynamic_slice(view, (0, part * share + first, kv * HD), (BLOCKS, rows, HD))
            )
        return jnp.stack(pieces, axis=1)

    whole = lax.all_gather(cut(0, share - RING_ROWS), "ctx", axis=0, tiled=True)

    ring = cut(share - RING_ROWS, RING_ROWS)
    z1, z2 = shift(ring, 1, 0), shift(ring, -1, 0)
    z3, z4 = shift(z1, 1, 0), shift(z2, -1, 0)
    low = jnp.concatenate([ring, z1, z2, z3], axis=0)
    x1_low, x2_low = shift(low, 0, 1), shift(low, 0, -1)
    z5, z6 = shift(z3, 1, 0), shift(z4, -1, 0)
    half = BLOCKS // 2
    z7, z8 = shift(z5[:half], 1, 0), shift(z6[half:], -1, 0)
    high = jnp.concatenate([z4, z5, z6, z7, z8], axis=0)
    x1_high, x2_high = shift(high, 0, 1), shift(high, 0, -1)
    x3_low, x3_high = shift(x1_low, 0, 1), shift(x2_high, 0, -1)
    ring_arrays = [low, high, x1_low, x1_high, x2_low, x2_high, x3_low, x3_high]

    core, chip = head % 2, head // 2
    queries_core = swap(after(queries, low), 1)
    near_queries = after([queries, queries_core], *ring_arrays[2:6])
    near_state = near(
        jnp.stack([kv, core]).astype(jnp.int32), near_queries, span_keys, span_values
    )
    queries_early, picks_early, weight_early = after(
        (queries, block_picks, out_weight), *ring_arrays[2:6]
    )
    queries_chip = swap(queries_early, 2)
    picks_pair = jnp.stack([block_picks, swap(picks_early, 2)])
    weights = [out_weight] + [None] * (heads - 1)
    for bits in range(2, heads, 2):
        weights[bits] = swap(weight_early, bits)
    queries_chip, picks_pair, weights[::2] = after(
        (queries_chip, picks_pair, weights[::2]), *ring_arrays
    )
    group_queries = [queries, queries_core, queries_chip, swap(queries_chip, 1)]
    picks_core = swap(picks_pair, 1)
    group_picks = [picks_pair[0], picks_core[0], picks_pair[1], picks_core[1]]
    for bits in range(0, heads, 2):
        weights[bits + 1] = swap(weights[bits], 1)
    picks = [group_pick.reshape(QB * SEL) for group_pick in group_picks]

    every_pick = jnp.concatenate([picks[r] for r in (2, 3, 0, 1)])
    owner, local = every_pick // BLOCKS, every_pick % BLOCKS
    ctx = lax.axis_index("ctx")
    dz = (owner // NX - ctx // NX) % NZ
    dx = (owner % NX - ctx % NX) % NX
    order_x = jnp.where(dx == 0, 0, jnp.where(dx == 3, 1, jnp.where(dx == 1, 2, 3)))
    order_z = jnp.where(dz == 0, 0, jnp.where(dz > NZ // 2, 2 * (NZ - dz) - 1, 2 * dz))
    place = jnp.where(dz == NZ // 2, NZ - 1, order_z) * BLOCKS + local
    upper = (place >= low.shape[0]).astype(jnp.int32)
    where = jnp.stack([2 * order_x + upper, place - low.shape[0] * upper], axis=-1)
    early = collect(where.astype(jnp.int32), ring_arrays)

    picks, group_queries, weights, near_state, early = lax.optimization_barrier(
        (picks, scale(group_queries), weights, near_state, early)
    )

    def far_of(first, second, earlier, half):
        return far(
            after(jnp.concatenate([picks[first], picks[second], core[None]]), *earlier),
            [group_queries[first], group_queries[second]],
            whole,
            early,
            half,
        )

    chip_here, chip_there = far_of(2, 3, [], 0)
    for_chip = merge_two(chip_here, swap(chip_there, 1))
    chip_parts = [swap(piece, 2) for piece in for_chip]
    own_here, own_there = far_of(0, 1, for_chip, 1)
    core_part = swap(own_there, 1)
    other_state = merge_chip(near_state, chip_parts)
    own, other, shares = merge_last(chip[None], own_here, core_part, other_state)
    parts = [shares[0]] + [swap(shares[n], 2 * n) for n in range(1, QB)]
    attention = assemble(core[None], own, swap(other, 1))
    return attention, project(after(parts, attention), weights)


def solution(mesh):
    placed = (
        P("ctx", "head"),
        P("ctx", "head", None),
        P("ctx", None),
        P("ctx", None),
        P("ctx", None),
        P("ctx", None),
        P("head", None),
    )
    return jax.shard_map(
        body,
        mesh=mesh,
        in_specs=placed,
        out_specs=(P("ctx", "head"), P(("ctx", "head"), None)),
        check_vma=False,
    )
```

```python
import functools
import math

import jax
import jax.numpy as jnp
from jax import lax
from jax.experimental import pallas as pl
from jax.experimental.pallas import tpu as pltpu
from jax.sharding import PartitionSpec as P

HD = 128
GROUP = 4
BLK = 512
HALF = BLK // 2
SEL = 4
QB = 4
BLOCKS = 8
TAIL = 16
SCALE = math.log2(math.e) / math.sqrt(HD)
NEG = -1e30
F32 = jnp.float32
BF16 = jnp.bfloat16
NX = 4
NZ = 8
RING_ROWS = 32
VMEM_BYTES = 56 << 20


def dot_nt(a, b):
    return lax.dot_general(a, b, (((1,), (1,)), ((), ())), preferred_element_type=F32)


def dot_tn(a, b):
    return lax.dot_general(a, b, (((0,), (0,)), ((), ())), preferred_element_type=F32)


def rounded_top(raw):
    return (raw * SCALE).astype(BF16).astype(F32)


def near_kernel(place_ref, *refs):
    q_refs, (k_ref, v_ref, acc_ref, m_ref, l_ref) = refs[:2], refs[2:]
    keys = lax.broadcasted_iota(jnp.int32, (BLK, HALF), 0)
    rows = lax.broadcasted_iota(jnp.int32, (BLK, HALF), 1) + place_ref[1] * HALF
    for r, q_ref in enumerate(q_refs):
        scores = jnp.where(keys <= rows, dot_nt(k_ref[...], q_ref[...]), NEG)
        top = rounded_top(jnp.max(scores, axis=0, keepdims=True))
        weights = jnp.exp2(scores * SCALE - top)
        m_ref[0, r] = top
        l_ref[0, r] = jnp.sum(weights, axis=0, keepdims=True)
        acc_ref[0, r] = dot_tn(v_ref[...], weights.astype(BF16))


def near(place, queries, span_keys, span_values):
    grid_spec = pltpu.PrefetchScalarGridSpec(
        num_scalar_prefetch=1,
        grid=(QB,),
        in_specs=[pl.BlockSpec((HALF, HD), lambda i, place: (2 * i + place[1], 0))] * 2
        + [pl.BlockSpec((BLK, HD), lambda i, place: (i, place[0]))] * 2,
        out_specs=[
            pl.BlockSpec((1, 2, HD, HALF), lambda i, place: (i, 0, 0, 0)),
            pl.BlockSpec((1, 2, 1, HALF), lambda i, place: (i, 0, 0, 0)),
            pl.BlockSpec((1, 2, 1, HALF), lambda i, place: (i, 0, 0, 0)),
        ],
    )
    return pl.pallas_call(
        near_kernel,
        grid_spec=grid_spec,
        out_shape=[
            jax.ShapeDtypeStruct((QB, 2, HD, HALF), F32),
            jax.ShapeDtypeStruct((QB, 2, 1, HALF), F32),
            jax.ShapeDtypeStruct((QB, 2, 1, HALF), F32),
        ],
        cost_estimate=pl.CostEstimate(
            flops=QB * 4 * BLK * BLK * HD, bytes_accessed=4 << 20, transcendentals=QB * BLK * BLK
        ),
        name="near",
    )(place, *queries, span_keys, span_values)


def pack_state(ref, i, out, top, total):
    ref[i, :HD, :] = out.astype(BF16)
    high = total.astype(BF16)
    low = (total - high.astype(F32)).astype(BF16)
    ref[i, HD:, :] = jnp.concatenate(
        [top.astype(BF16), high, low, jnp.zeros((TAIL - 3, out.shape[1]), BF16)], axis=0
    )


def unpack_state(ref, i):
    tail = ref[i, HD:, :].astype(F32)
    return ref[i, :HD, :].astype(F32), tail[0:1], tail[1:2] + tail[2:3]


def far_kernel(picks_ref, *refs, half):
    q_refs, whole_ref, early_ref, refs = refs[:2], refs[2], refs[3], refs[4:]
    out_refs, (buffer, early), refs = refs[:2], refs[2:4], refs[4:]
    score_refs, weight_refs, sems = refs[:2], refs[2:4], refs[4]
    picks = 2 * QB * SEL
    early_copy = pltpu.make_async_copy(
        early_ref.at[pl.ds(half * picks, picks)], early, sems.at[0]
    )
    early_copy.start()
    for pick in range(picks):
        sem = sems.at[1 if pick < SEL else 2]
        pltpu.make_async_copy(whole_ref.at[picks_ref[pick]], buffer.at[pick], sem).start()
    early_copy.wait()
    steps = [(row, k) for row in range(2 * QB) for k in range(2)]
    sums = {}

    def fetched(first, count, sem):
        held = buffer.at[pl.ds(first, count)]
        pltpu.make_async_copy(held, held, sem).wait()

    def joined(row, which):
        return jnp.concatenate(
            [held[row * SEL + j, which] for held in (buffer, early) for j in range(SEL)], axis=0
        )

    def score(number):
        row, k = steps[number]
        if number == 0:
            fetched(0, SEL, sems.at[1])
        if number == 2:
            fetched(SEL, picks - SEL, sems.at[2])
        first = row % QB * BLK + (picks_ref[picks] ^ k) * HALF
        tokens = pl.ds(pl.multiple_of(first, HALF), HALF)
        score_refs[number % 2][...] = dot_nt(joined(row, 0), q_refs[row // QB][tokens, :])

    def soften(number):
        score_ref, weight_ref = score_refs[number % 2], weight_refs[number % 2]
        tops, totals = [], []
        for lane in range(0, HALF, HD):
            lanes = slice(lane, lane + HD)
            top = rounded_top(jnp.max(score_ref[:, lanes], axis=0, keepdims=True))
            total = jnp.zeros((8, HD), F32)
            for row in range(0, BLK, 64):
                weights = jnp.exp2(score_ref[row : row + 64, lanes] * SCALE - top)
                weight_ref[row : row + 64, lanes] = weights.astype(BF16)
                total = total + jnp.sum(weights.reshape(8, 8, HD), axis=0)
            tops.append(top)
            totals.append(jnp.sum(total, axis=0, keepdims=True))
        sums[number] = jnp.concatenate(tops, axis=1), jnp.concatenate(totals, axis=1)

    def finish(number):
        row, k = steps[number]
        top, total = sums.pop(number)
        out = dot_tn(joined(row, 1), weight_refs[number % 2][...])
        pack_state(out_refs[k], row, out, top, total)

    for number in range(len(steps) + 2):
        if number < len(steps):
            score(number)
        if number >= 2:
            finish(number - 2)
        if 1 <= number <= len(steps):
            soften(number - 1)


def far(picks, queries, whole, early, half):
    pay = HD + TAIL
    vmem = pl.BlockSpec(memory_space=pltpu.VMEM)
    return pl.pallas_call(
        functools.partial(far_kernel, half=half),
        in_specs=[pl.BlockSpec(memory_space=pltpu.SMEM)]
        + [vmem] * 2
        + [pl.BlockSpec(memory_space=pl.ANY)] * 2,
        out_specs=[vmem] * 2,
        out_shape=[jax.ShapeDtypeStruct((2 * QB, pay, HALF), BF16)] * 2,
        scratch_shapes=[
            pltpu.VMEM((2 * QB * SEL,) + array.shape[1:], BF16) for array in (whole, early)
        ]
        + [pltpu.VMEM((BLK, HALF), F32)] * 2
        + [pltpu.VMEM((BLK, HALF), BF16)] * 2
        + [pltpu.SemaphoreType.DMA((3,))],
        compiler_params=pltpu.CompilerParams(vmem_limit_bytes=VMEM_BYTES),
        cost_estimate=pl.CostEstimate(
            flops=8 * 2 * QB * 4 * BLK * BLK * HD,
            bytes_accessed=5 << 20,
            transcendentals=2 * QB * BLK * BLK,
        ),
        name="far",
    )(picks, *queries, whole, early)


def collect_kernel(where_ref, *refs):
    sources, out_ref, sem = refs[:-2], refs[-2], refs[-1]

    def fetch(pick, carry):
        array, index = where_ref[pick, 0], where_ref[pick, 1]
        for number, source in enumerate(sources):

            def start(source=source):
                pltpu.make_async_copy(source.at[index], out_ref.at[pick], sem).start()

            pl.when(array == number)(start)
        return carry

    lax.fori_loop(0, out_ref.shape[0], fetch, 0)
    pltpu.make_async_copy(out_ref, out_ref, sem).wait()


def collect(where, arrays):
    return pl.pallas_call(
        collect_kernel,
        in_specs=[pl.BlockSpec(memory_space=pltpu.SMEM)]
        + [pl.BlockSpec(memory_space=pl.ANY)] * len(arrays),
        out_specs=pl.BlockSpec(memory_space=pltpu.VMEM),
        out_shape=jax.ShapeDtypeStruct((where.shape[0],) + arrays[0].shape[1:], BF16),
        scratch_shapes=[pltpu.SemaphoreType.DMA],
        compiler_params=pltpu.CompilerParams(vmem_limit_bytes=VMEM_BYTES),
        name="collect",
    )(where, *arrays)


def crossed(row):
    return (row + QB) % (2 * QB)


def merge_two_kernel(a_ref, b_ref, *out_refs):
    for row in range(2 * QB):
        acc_a, m_a, l_a = unpack_state(a_ref, row)
        acc_b, m_b, l_b = unpack_state(b_ref, crossed(row))
        top = jnp.maximum(m_a, m_b)
        f_a = jnp.exp2(m_a - top)
        f_b = jnp.exp2(m_b - top)
        out = f_a * acc_a + f_b * acc_b
        pack_state(out_refs[row // QB], row % QB, out, top, f_a * l_a + f_b * l_b)


def merge_two(mine, other):
    vmem = pl.BlockSpec(memory_space=pltpu.VMEM)
    return pl.pallas_call(
        merge_two_kernel,
        in_specs=[vmem] * 2,
        out_specs=[vmem] * 2,
        out_shape=[jax.ShapeDtypeStruct((QB,) + mine.shape[1:], BF16)] * 2,
        name="merge_two",
    )(mine, other)


def hold(arrays):
    hbm = pl.BlockSpec(memory_space=pl.ANY)
    return pl.pallas_call(
        lambda *refs: None,
        in_specs=[hbm] * len(arrays),
        out_specs=[hbm] * len(arrays),
        out_shape=[jax.ShapeDtypeStruct(array.shape, array.dtype) for array in arrays],
        input_output_aliases={n: n for n in range(len(arrays))},
        cost_estimate=pl.CostEstimate(
            flops=8 * QB * 4 * BLK * BLK * HD, bytes_accessed=4 << 20, transcendentals=8 * BLK
        ),
        name="hold",
    )(*arrays)


def merge_last_kernel(chip_ref, a_ref, b_ref, acc_ref, m_ref, l_ref, *refs):
    chip_refs, half_refs, share_refs = refs[:2], refs[2:4], refs[4:]
    for row in range(2 * QB):
        r, i = row // QB, row % QB
        states = [unpack_state(a_ref, row), unpack_state(b_ref, crossed(row))]
        states.append(unpack_state(chip_refs[r], i))
        states.append((acc_ref[i, r], m_ref[i, r], l_ref[i, r]))
        top = functools.reduce(jnp.maximum, [m for _, m, _ in states])
        factors = [jnp.exp2(m - top) for _, m, _ in states]
        total = sum(f * l for f, (_, _, l) in zip(factors, states))
        factors = [f / total for f in factors]
        out = sum(f * acc for f, (acc, _, _) in zip(factors, states)).T.astype(BF16)
        half_refs[r][i] = out
        for n, share_ref in enumerate(share_refs):

            def keep(share_ref=share_ref, r=r, out=out):
                share_ref[r] = out

            pl.when(chip_ref[0] ^ n == i)(keep)


def merge_last(chip, mine, core_part, near_state, chip_parts):
    vmem = pl.BlockSpec(memory_space=pltpu.VMEM)
    arrays = [mine, core_part, *near_state, *chip_parts]
    own, other, *shares = pl.pallas_call(
        merge_last_kernel,
        in_specs=[pl.BlockSpec(memory_space=pltpu.SMEM)] + [vmem] * len(arrays),
        out_specs=[vmem] * (2 + QB),
        out_shape=[jax.ShapeDtypeStruct((QB, HALF, HD), BF16)] * 2
        + [jax.ShapeDtypeStruct((2, HALF, HD), BF16)] * QB,
        name="merge_last",
    )(chip, *arrays)
    return own, other, shares


def assemble_kernel(core_ref, own_ref, other_ref, out_ref):
    for i in range(QB):
        for k, ref in enumerate((own_ref, other_ref)):
            first = pl.multiple_of(i * BLK + (core_ref[0] ^ k) * HALF, HALF)
            out_ref[pl.ds(first, HALF), :] = ref[i]


def assemble(core, own, other):
    vmem = pl.BlockSpec(memory_space=pltpu.VMEM)
    return pl.pallas_call(
        assemble_kernel,
        in_specs=[pl.BlockSpec(memory_space=pltpu.SMEM)] + [vmem] * 2,
        out_specs=vmem,
        out_shape=jax.ShapeDtypeStruct((QB * BLK, HD), BF16),
        name="assemble",
    )(core, own, other)


def project_kernel(*refs):
    a_refs, w_refs, out_ref = refs[:QB], refs[QB:-1], refs[-1]
    rows = jnp.concatenate([a_ref[r] for a_ref in a_refs for r in range(2)], axis=1)
    tile = 512
    for first in range(0, out_ref.shape[1], tile):
        weight = jnp.concatenate([w_ref[:, first : first + tile] for w_ref in w_refs], axis=0)
        out_ref[:, first : first + tile] = jnp.dot(
            rows, weight, preferred_element_type=F32
        ).astype(BF16)


def project(parts, weights):
    vmem = pl.BlockSpec(memory_space=pltpu.VMEM)
    return pl.pallas_call(
        project_kernel,
        in_specs=[vmem] * (len(parts) + len(weights)),
        out_specs=vmem,
        out_shape=jax.ShapeDtypeStruct((parts[0].shape[1], weights[0].shape[1]), BF16),
        compiler_params=pltpu.CompilerParams(vmem_limit_bytes=24 << 20),
        name="project",
    )(*parts, *weights)


def shift(array, dz, dx):
    pairs = []
    for z in range(NZ):
        for x in range(NX):
            pairs.append((z * NX + x, (z + dz) % NZ * NX + (x + dx) % NX))
    return lax.ppermute(array, "ctx", pairs)


def swap(array, bits):
    return lax.ppermute(array, "head", [(h, h ^ bits) for h in range(lax.axis_size("head"))])


def after(value, *earlier):
    return lax.optimization_barrier((value, earlier))[0]


def body(queries, block_picks, span_keys, span_values, cache_keys, cache_values, out_weight):
    heads = lax.axis_size("head")
    head = lax.axis_index("head")
    part = head % GROUP
    kv = head // GROUP
    share = BLK // GROUP

    def cut(first, rows):
        pieces = []
        for cache in (cache_keys, cache_values):
            view = cache.reshape(BLOCKS, BLK, cache.shape[1])
            pieces.append(
                lax.dynamic_slice(view, (0, part * share + first, kv * HD), (BLOCKS, rows, HD))
            )
        return jnp.stack(pieces, axis=1)

    whole = lax.all_gather(cut(0, share - RING_ROWS), "ctx", axis=0, tiled=True)

    ring = cut(share - RING_ROWS, RING_ROWS)
    z1, z2 = shift(ring, 1, 0), shift(ring, -1, 0)
    z3, z4 = shift(z1, 1, 0), shift(z2, -1, 0)
    low = jnp.concatenate([ring, z1, z2, z3], axis=0)
    x1_low, x2_low = shift(low, 0, 1), shift(low, 0, -1)
    z5, z6 = shift(z3, 1, 0), shift(z4, -1, 0)
    half = BLOCKS // 2
    z7, z8 = shift(z5[:half], 1, 0), shift(z6[half:], -1, 0)
    high = jnp.concatenate([z4, z5, z6, z7, z8], axis=0)
    x1_high, x2_high = shift(high, 0, 1), shift(high, 0, -1)
    x3_low, x3_high = shift(x1_low, 0, 1), shift(x2_high, 0, -1)
    ring_arrays = [low, high, x1_low, x1_high, x2_low, x2_high, x3_low, x3_high]

    core, chip = head % 2, head // 2
    queries_core = swap(after(queries, low), 1)
    near_queries = after([queries, queries_core], *ring_arrays[2:6])
    near_state = near(
        jnp.stack([kv, core]).astype(jnp.int32), near_queries, span_keys, span_values
    )
    picks_chip = swap(after(block_picks, x1_low, x2_low), 2)
    queries_early, weight_early = after((queries, out_weight), x3_low, picks_chip)
    queries_chip = swap(queries_early, 2)
    picks_pair = jnp.stack([block_picks, picks_chip])
    weights = [out_weight] + [None] * (heads - 1)
    for bits in range(2, heads, 2):
        weights[bits] = swap(weight_early, bits)
    queries_chip, picks_pair, weights[::2] = after(
        (queries_chip, picks_pair, weights[::2]), *ring_arrays
    )
    group_queries = [queries, queries_core, queries_chip, swap(queries_chip, 1)]
    picks_core = swap(picks_pair, 1)
    group_picks = [picks_pair[0], picks_core[0], picks_pair[1], picks_core[1]]
    for bits in range(0, heads, 2):
        weights[bits + 1] = swap(weights[bits], 1)
    picks = [group_pick.reshape(QB * SEL) for group_pick in group_picks]

    every_pick = jnp.concatenate([picks[r] for r in (2, 3, 0, 1)])
    owner, local = every_pick // BLOCKS, every_pick % BLOCKS
    ctx = lax.axis_index("ctx")
    dz = (owner // NX - ctx // NX) % NZ
    dx = (owner % NX - ctx % NX) % NX
    order_x = jnp.where(dx == 0, 0, jnp.where(dx == 3, 1, jnp.where(dx == 1, 2, 3)))
    order_z = jnp.where(dz == 0, 0, jnp.where(dz > NZ // 2, 2 * (NZ - dz) - 1, 2 * dz))
    place = jnp.where(dz == NZ // 2, NZ - 1, order_z) * BLOCKS + local
    upper = (place >= low.shape[0]).astype(jnp.int32)
    where = jnp.stack([2 * order_x + upper, place - low.shape[0] * upper], axis=-1)
    early = collect(where.astype(jnp.int32), ring_arrays)

    picks, group_queries, weights, near_state, early = lax.optimization_barrier(
        (picks, group_queries, weights, near_state, early)
    )

    def far_of(first, second, earlier, half):
        return far(
            after(jnp.concatenate([picks[first], picks[second], core[None]]), *earlier),
            [group_queries[first], group_queries[second]],
            whole,
            early,
            half,
        )

    chip_here, chip_there = far_of(2, 3, [], 0)
    for_chip = merge_two(chip_here, swap(chip_there, 1))
    chip_parts = [swap(piece, 2) for piece in for_chip]
    own_here, own_there = far_of(0, 1, for_chip, 1)
    core_part = swap(own_there, 1)
    chip_parts = hold(chip_parts)
    own, other, shares = merge_last(chip[None], own_here, core_part, near_state, chip_parts)
    parts = [shares[0]] + [swap(shares[n], 2 * n) for n in range(1, QB)]
    attention = assemble(core[None], own, swap(other, 1))
    return attention, project(after(parts, attention), weights)


def solution(mesh):
    placed = (
        P("ctx", "head"),
        P("ctx", "head", None),
        P("ctx", None),
        P("ctx", None),
        P("ctx", None),
        P("ctx", None),
        P("head", None),
    )
    return jax.shard_map(
        body,
        mesh=mesh,
        in_specs=placed,
        out_specs=(P("ctx", "head"), P(("ctx", "head"), None)),
        check_vma=False,
    )
```

```python
import functools
import math

import jax
import jax.numpy as jnp
from jax import lax
from jax.experimental import pallas as pl
from jax.experimental.pallas import tpu as pltpu
from jax.sharding import PartitionSpec as P

HD = 128
GROUP = 4
BLK = 512
HALF = BLK // 2
SEL = 4
QB = 4
BLOCKS = 8
TAIL = 16
SCALE = math.log2(math.e) / math.sqrt(HD)
NEG = -1e30
F32 = jnp.float32
BF16 = jnp.bfloat16
NX = 4
NZ = 8
RING_ROWS = 48
VMEM_BYTES = 56 << 20


def dot_nt(a, b):
    return lax.dot_general(a, b, (((1,), (1,)), ((), ())), preferred_element_type=F32)


def dot_tn(a, b):
    return lax.dot_general(a, b, (((0,), (0,)), ((), ())), preferred_element_type=F32)


def rounded_top(raw):
    return (raw * SCALE).astype(BF16).astype(F32)


def near_kernel(place_ref, *refs):
    q_refs, (k_ref, v_ref, acc_ref, m_ref, l_ref) = refs[:2], refs[2:]
    keys = lax.broadcasted_iota(jnp.int32, (BLK, HALF), 0)
    rows = lax.broadcasted_iota(jnp.int32, (BLK, HALF), 1) + place_ref[1] * HALF
    for r, q_ref in enumerate(q_refs):
        scores = jnp.where(keys <= rows, dot_nt(k_ref[...], q_ref[...]), NEG)
        top = rounded_top(jnp.max(scores, axis=0, keepdims=True))
        weights = jnp.exp2(scores * SCALE - top)
        m_ref[0, r] = top
        l_ref[0, r] = jnp.sum(weights, axis=0, keepdims=True)
        acc_ref[0, r] = dot_tn(v_ref[...], weights.astype(BF16))


def near(place, queries, span_keys, span_values):
    grid_spec = pltpu.PrefetchScalarGridSpec(
        num_scalar_prefetch=1,
        grid=(QB,),
        in_specs=[pl.BlockSpec((HALF, HD), lambda i, place: (2 * i + place[1], 0))] * 2
        + [pl.BlockSpec((BLK, HD), lambda i, place: (i, place[0]))] * 2,
        out_specs=[
            pl.BlockSpec((1, 2, HD, HALF), lambda i, place: (i, 0, 0, 0)),
            pl.BlockSpec((1, 2, 1, HALF), lambda i, place: (i, 0, 0, 0)),
            pl.BlockSpec((1, 2, 1, HALF), lambda i, place: (i, 0, 0, 0)),
        ],
    )
    return pl.pallas_call(
        near_kernel,
        grid_spec=grid_spec,
        out_shape=[
            jax.ShapeDtypeStruct((QB, 2, HD, HALF), F32),
            jax.ShapeDtypeStruct((QB, 2, 1, HALF), F32),
            jax.ShapeDtypeStruct((QB, 2, 1, HALF), F32),
        ],
        cost_estimate=pl.CostEstimate(
            flops=QB * 4 * BLK * BLK * HD, bytes_accessed=4 << 20, transcendentals=QB * BLK * BLK
        ),
        name="near",
    )(place, *queries, span_keys, span_values)


def pack_state(ref, i, out, top, total):
    ref[i, :HD, :] = out.astype(BF16)
    high = total.astype(BF16)
    low = (total - high.astype(F32)).astype(BF16)
    ref[i, HD:, :] = jnp.concatenate(
        [top.astype(BF16), high, low, jnp.zeros((TAIL - 3, out.shape[1]), BF16)], axis=0
    )


def unpack_state(ref, i):
    tail = ref[i, HD:, :].astype(F32)
    return ref[i, :HD, :].astype(F32), tail[0:1], tail[1:2] + tail[2:3]


def far_kernel(picks_ref, *refs, half):
    q_refs, whole_ref, early_ref, refs = refs[:2], refs[2], refs[3], refs[4:]
    out_refs, (buffer, early), refs = refs[:2], refs[2:4], refs[4:]
    score_refs, weight_refs, sems = refs[:2], refs[2:4], refs[4]
    picks = 2 * QB * SEL
    early_copy = pltpu.make_async_copy(
        early_ref.at[pl.ds(half * picks, picks)], early, sems.at[0]
    )
    early_copy.start()
    for pick in range(picks):
        sem = sems.at[1 if pick < SEL else 2]
        pltpu.make_async_copy(whole_ref.at[picks_ref[pick]], buffer.at[pick], sem).start()
    early_copy.wait()
    steps = [(row, k) for row in range(2 * QB) for k in range(2)]
    sums = {}

    def fetched(first, count, sem):
        held = buffer.at[pl.ds(first, count)]
        pltpu.make_async_copy(held, held, sem).wait()

    def joined(row, which):
        return jnp.concatenate(
            [held[row * SEL + j, which] for held in (buffer, early) for j in range(SEL)], axis=0
        )

    def score(number):
        row, k = steps[number]
        if number == 0:
            fetched(0, SEL, sems.at[1])
        if number == 2:
            fetched(SEL, picks - SEL, sems.at[2])
        first = row % QB * BLK + (picks_ref[picks] ^ k) * HALF
        tokens = pl.ds(pl.multiple_of(first, HALF), HALF)
        score_refs[number % 2][...] = dot_nt(joined(row, 0), q_refs[row // QB][tokens, :])

    def soften(number):
        score_ref, weight_ref = score_refs[number % 2], weight_refs[number % 2]
        tops, totals = [], []
        for lane in range(0, HALF, HD):
            lanes = slice(lane, lane + HD)
            top = rounded_top(jnp.max(score_ref[:, lanes], axis=0, keepdims=True))
            total = jnp.zeros((8, HD), F32)
            for row in range(0, BLK, 64):
                weights = jnp.exp2(score_ref[row : row + 64, lanes] * SCALE - top)
                weight_ref[row : row + 64, lanes] = weights.astype(BF16)
                total = total + jnp.sum(weights.reshape(8, 8, HD), axis=0)
            tops.append(top)
            totals.append(jnp.sum(total, axis=0, keepdims=True))
        sums[number] = jnp.concatenate(tops, axis=1), jnp.concatenate(totals, axis=1)

    def finish(number):
        row, k = steps[number]
        top, total = sums.pop(number)
        out = dot_tn(joined(row, 1), weight_refs[number % 2][...])
        pack_state(out_refs[k], row, out, top, total)

    for number in range(len(steps) + 2):
        if number < len(steps):
            score(number)
        if number >= 2:
            finish(number - 2)
        if 1 <= number <= len(steps):
            soften(number - 1)


def far(picks, queries, whole, early, half):
    pay = HD + TAIL
    vmem = pl.BlockSpec(memory_space=pltpu.VMEM)
    return pl.pallas_call(
        functools.partial(far_kernel, half=half),
        in_specs=[pl.BlockSpec(memory_space=pltpu.SMEM)]
        + [vmem] * 2
        + [pl.BlockSpec(memory_space=pl.ANY)] * 2,
        out_specs=[vmem] * 2,
        out_shape=[jax.ShapeDtypeStruct((2 * QB, pay, HALF), BF16)] * 2,
        scratch_shapes=[
            pltpu.VMEM((2 * QB * SEL,) + array.shape[1:], BF16) for array in (whole, early)
        ]
        + [pltpu.VMEM((BLK, HALF), F32)] * 2
        + [pltpu.VMEM((BLK, HALF), BF16)] * 2
        + [pltpu.SemaphoreType.DMA((3,))],
        compiler_params=pltpu.CompilerParams(vmem_limit_bytes=VMEM_BYTES),
        cost_estimate=pl.CostEstimate(
            flops=8 * 2 * QB * 4 * BLK * BLK * HD,
            bytes_accessed=5 << 20,
            transcendentals=2 * QB * BLK * BLK,
        ),
        name="far",
    )(picks, *queries, whole, early)


def collect_kernel(where_ref, *refs):
    sources, out_ref, sem = refs[:-2], refs[-2], refs[-1]

    def fetch(pick, carry):
        array, index = where_ref[pick, 0], where_ref[pick, 1]
        for number, source in enumerate(sources):

            def start(source=source):
                pltpu.make_async_copy(source.at[index], out_ref.at[pick], sem).start()

            pl.when(array == number)(start)
        return carry

    lax.fori_loop(0, out_ref.shape[0], fetch, 0)
    pltpu.make_async_copy(out_ref, out_ref, sem).wait()


def collect(where, arrays):
    return pl.pallas_call(
        collect_kernel,
        in_specs=[pl.BlockSpec(memory_space=pltpu.SMEM)]
        + [pl.BlockSpec(memory_space=pl.ANY)] * len(arrays),
        out_specs=pl.BlockSpec(memory_space=pltpu.VMEM),
        out_shape=jax.ShapeDtypeStruct((where.shape[0],) + arrays[0].shape[1:], BF16),
        scratch_shapes=[pltpu.SemaphoreType.DMA],
        compiler_params=pltpu.CompilerParams(vmem_limit_bytes=VMEM_BYTES),
        name="collect",
    )(where, *arrays)


def crossed(row):
    return (row + QB) % (2 * QB)


def merge_two_kernel(a_ref, b_ref, *out_refs):
    for row in range(2 * QB):
        acc_a, m_a, l_a = unpack_state(a_ref, row)
        acc_b, m_b, l_b = unpack_state(b_ref, crossed(row))
        top = jnp.maximum(m_a, m_b)
        f_a = jnp.exp2(m_a - top)
        f_b = jnp.exp2(m_b - top)
        out = f_a * acc_a + f_b * acc_b
        pack_state(out_refs[row // QB], row % QB, out, top, f_a * l_a + f_b * l_b)


def merge_two(mine, other):
    vmem = pl.BlockSpec(memory_space=pltpu.VMEM)
    return pl.pallas_call(
        merge_two_kernel,
        in_specs=[vmem] * 2,
        out_specs=[vmem] * 2,
        out_shape=[jax.ShapeDtypeStruct((QB,) + mine.shape[1:], BF16)] * 2,
        name="merge_two",
    )(mine, other)


def hold(arrays):
    hbm = pl.BlockSpec(memory_space=pl.ANY)
    return pl.pallas_call(
        lambda *refs: None,
        in_specs=[hbm] * len(arrays),
        out_specs=[hbm] * len(arrays),
        out_shape=[jax.ShapeDtypeStruct(array.shape, array.dtype) for array in arrays],
        input_output_aliases={n: n for n in range(len(arrays))},
        cost_estimate=pl.CostEstimate(
            flops=8 * QB * 4 * BLK * BLK * HD, bytes_accessed=4 << 20, transcendentals=8 * BLK
        ),
        name="hold",
    )(*arrays)


def merge_last_kernel(chip_ref, a_ref, b_ref, acc_ref, m_ref, l_ref, *refs):
    chip_refs, half_refs, share_refs = refs[:2], refs[2:4], refs[4:]
    for row in range(2 * QB):
        r, i = row // QB, row % QB
        states = [unpack_state(a_ref, row), unpack_state(b_ref, crossed(row))]
        states.append(unpack_state(chip_refs[r], i))
        states.append((acc_ref[i, r], m_ref[i, r], l_ref[i, r]))
        top = functools.reduce(jnp.maximum, [m for _, m, _ in states])
        factors = [jnp.exp2(m - top) for _, m, _ in states]
        total = sum(f * l for f, (_, _, l) in zip(factors, states))
        factors = [f / total for f in factors]
        out = sum(f * acc for f, (acc, _, _) in zip(factors, states)).T.astype(BF16)
        half_refs[r][i] = out
        for n, share_ref in enumerate(share_refs):

            def keep(share_ref=share_ref, r=r, out=out):
                share_ref[r] = out

            pl.when(chip_ref[0] ^ n == i)(keep)


def merge_last(chip, mine, core_part, near_state, chip_parts):
    vmem = pl.BlockSpec(memory_space=pltpu.VMEM)
    arrays = [mine, core_part, *near_state, *chip_parts]
    own, other, *shares = pl.pallas_call(
        merge_last_kernel,
        in_specs=[pl.BlockSpec(memory_space=pltpu.SMEM)] + [vmem] * len(arrays),
        out_specs=[vmem] * (2 + QB),
        out_shape=[jax.ShapeDtypeStruct((QB, HALF, HD), BF16)] * 2
        + [jax.ShapeDtypeStruct((2, HALF, HD), BF16)] * QB,
        name="merge_last",
    )(chip, *arrays)
    return own, other, shares


def assemble_kernel(core_ref, own_ref, other_ref, out_ref):
    for i in range(QB):
        for k, ref in enumerate((own_ref, other_ref)):
            first = pl.multiple_of(i * BLK + (core_ref[0] ^ k) * HALF, HALF)
            out_ref[pl.ds(first, HALF), :] = ref[i]


def assemble(core, own, other):
    vmem = pl.BlockSpec(memory_space=pltpu.VMEM)
    return pl.pallas_call(
        assemble_kernel,
        in_specs=[pl.BlockSpec(memory_space=pltpu.SMEM)] + [vmem] * 2,
        out_specs=vmem,
        out_shape=jax.ShapeDtypeStruct((QB * BLK, HD), BF16),
        name="assemble",
    )(core, own, other)


def project_kernel(*refs):
    a_refs, w_refs, out_ref = refs[:QB], refs[QB:-1], refs[-1]
    rows = jnp.concatenate([a_ref[r] for a_ref in a_refs for r in range(2)], axis=1)
    tile = 512
    for first in range(0, out_ref.shape[1], tile):
        weight = jnp.concatenate([w_ref[:, first : first + tile] for w_ref in w_refs], axis=0)
        out_ref[:, first : first + tile] = jnp.dot(
            rows, weight, preferred_element_type=F32
        ).astype(BF16)


def project(parts, weights):
    vmem = pl.BlockSpec(memory_space=pltpu.VMEM)
    return pl.pallas_call(
        project_kernel,
        in_specs=[vmem] * (len(parts) + len(weights)),
        out_specs=vmem,
        out_shape=jax.ShapeDtypeStruct((parts[0].shape[1], weights[0].shape[1]), BF16),
        compiler_params=pltpu.CompilerParams(vmem_limit_bytes=24 << 20),
        name="project",
    )(*parts, *weights)


def shift(array, dz, dx):
    pairs = []
    for z in range(NZ):
        for x in range(NX):
            pairs.append((z * NX + x, (z + dz) % NZ * NX + (x + dx) % NX))
    return lax.ppermute(array, "ctx", pairs)


def swap(array, bits):
    return lax.ppermute(array, "head", [(h, h ^ bits) for h in range(lax.axis_size("head"))])


def after(value, *earlier):
    return lax.optimization_barrier((value, earlier))[0]


def body(queries, block_picks, span_keys, span_values, cache_keys, cache_values, out_weight):
    heads = lax.axis_size("head")
    head = lax.axis_index("head")
    part = head % GROUP
    kv = head // GROUP
    share = BLK // GROUP

    def cut(first, rows):
        pieces = []
        for cache in (cache_keys, cache_values):
            view = cache.reshape(BLOCKS, BLK, cache.shape[1])
            pieces.append(
                lax.dynamic_slice(view, (0, part * share + first, kv * HD), (BLOCKS, rows, HD))
            )
        return jnp.stack(pieces, axis=1)

    whole = lax.all_gather(cut(0, share - RING_ROWS), "ctx", axis=0, tiled=True)

    ring = cut(share - RING_ROWS, RING_ROWS)
    z1, z2 = shift(ring, 1, 0), shift(ring, -1, 0)
    z3, z4 = shift(z1, 1, 0), shift(z2, -1, 0)
    groups = [jnp.concatenate([ring, z1], axis=0), jnp.concatenate([z2, z3], axis=0)]
    z5, z6 = shift(z3, 1, 0), shift(z4, -1, 0)
    half = BLOCKS // 2
    z7, z8 = shift(z5[:half], 1, 0), shift(z6[half:], -1, 0)
    groups += [jnp.concatenate([z4, z5], axis=0), jnp.concatenate([z6, z7, z8], axis=0)]
    from_below = [shift(group, 0, 1) for group in groups]
    from_above = [shift(group, 0, -1) for group in groups]
    farthest = [shift(group, 0, 1) for group in from_below[:2]]
    farthest += [shift(group, 0, -1) for group in from_above[2:]]
    ring_arrays = groups + from_below + from_above + farthest

    core, chip = head % 2, head // 2
    queries_core = swap(after(queries, groups[3]), 1)
    near_queries = after([queries, queries_core], *from_below, *from_above)
    near_state = near(
        jnp.stack([kv, core]).astype(jnp.int32), near_queries, span_keys, span_values
    )
    picks_chip = swap(after(block_picks, from_below[1], from_above[1]), 2)
    queries_early, weight_early = after(
        (queries, out_weight), *from_below, *from_above, *farthest[:3], picks_chip
    )
    queries_chip = swap(queries_early, 2)
    picks_pair = jnp.stack([block_picks, picks_chip])
    weights = [out_weight] + [None] * (heads - 1)
    for bits in range(2, heads, 2):
        weights[bits] = swap(weight_early, bits)
    queries_chip, picks_pair, weights[::2] = after(
        (queries_chip, picks_pair, weights[::2]), *ring_arrays
    )
    group_queries = [queries, queries_core, queries_chip, swap(queries_chip, 1)]
    picks_core = swap(picks_pair, 1)
    group_picks = [picks_pair[0], picks_core[0], picks_pair[1], picks_core[1]]
    for bits in range(0, heads, 2):
        weights[bits + 1] = swap(weights[bits], 1)
    picks = [group_pick.reshape(QB * SEL) for group_pick in group_picks]

    every_pick = jnp.concatenate([picks[r] for r in (2, 3, 0, 1)])
    owner, local = every_pick // BLOCKS, every_pick % BLOCKS
    ctx = lax.axis_index("ctx")
    dz = (owner // NX - ctx // NX) % NZ
    dx = (owner % NX - ctx % NX) % NX
    order_x = jnp.where(dx == 0, 0, jnp.where(dx == 3, 1, jnp.where(dx == 1, 2, 3)))
    order_z = jnp.where(dz == 0, 0, jnp.where(dz > NZ // 2, 2 * (NZ - dz) - 1, 2 * dz))
    order_z = jnp.where(dz == NZ // 2, NZ - 1, order_z)
    where = jnp.stack(
        [len(groups) * order_x + order_z // 2, order_z % 2 * BLOCKS + local], axis=-1
    )
    early = collect(where.astype(jnp.int32), ring_arrays)

    picks, group_queries, weights, near_state, early = lax.optimization_barrier(
        (picks, group_queries, weights, near_state, early)
    )

    def far_of(first, second, earlier, half):
        return far(
            after(jnp.concatenate([picks[first], picks[second], core[None]]), *earlier),
            [group_queries[first], group_queries[second]],
            whole,
            early,
            half,
        )

    chip_here, chip_there = far_of(2, 3, [], 0)
    for_chip = merge_two(chip_here, swap(chip_there, 1))
    chip_parts = [swap(piece, 2) for piece in for_chip]
    own_here, own_there = far_of(0, 1, for_chip, 1)
    core_part = swap(own_there, 1)
    chip_parts = hold(chip_parts)
    own, other, shares = merge_last(chip[None], own_here, core_part, near_state, chip_parts)
    parts = [shares[0]] + [swap(shares[n], 2 * n) for n in range(1, QB)]
    attention = assemble(core[None], own, swap(other, 1))
    return attention, project(after(parts, attention), weights)


def solution(mesh):
    placed = (
        P("ctx", "head"),
        P("ctx", "head", None),
        P("ctx", None),
        P("ctx", None),
        P("ctx", None),
        P("ctx", None),
        P("head", None),
    )
    return jax.shard_map(
        body,
        mesh=mesh,
        in_specs=placed,
        out_specs=(P("ctx", "head"), P(("ctx", "head"), None)),
        check_vma=False,
    )
```

```python
import functools
import math

import jax
import jax.numpy as jnp
from jax import lax
from jax.experimental import pallas as pl
from jax.experimental.pallas import tpu as pltpu
from jax.sharding import PartitionSpec as P

HD = 128
GROUP = 4
BLK = 512
HALF = BLK // 2
SEL = 4
QB = 4
BLOCKS = 8
TAIL = 16
SCALE = math.log2(math.e) / math.sqrt(HD)
NEG = -1e30
F32 = jnp.float32
BF16 = jnp.bfloat16
NX = 4
NZ = 8
RING_ROWS = 32
VMEM_BYTES = 56 << 20


def dot_nt(a, b):
    return lax.dot_general(a, b, (((1,), (1,)), ((), ())), preferred_element_type=F32)


def dot_tn(a, b):
    return lax.dot_general(a, b, (((0,), (0,)), ((), ())), preferred_element_type=F32)


def rounded_top(raw):
    return (raw * SCALE).astype(BF16).astype(F32)


def near_kernel(place_ref, *refs):
    q_refs, (k_ref, v_ref, acc_ref, m_ref, l_ref) = refs[:2], refs[2:]
    keys = lax.broadcasted_iota(jnp.int32, (BLK, HALF), 0)
    rows = lax.broadcasted_iota(jnp.int32, (BLK, HALF), 1) + place_ref[1] * HALF
    for r, q_ref in enumerate(q_refs):
        scores = jnp.where(keys <= rows, dot_nt(k_ref[...], q_ref[...]), NEG)
        top = rounded_top(jnp.max(scores, axis=0, keepdims=True))
        weights = jnp.exp2(scores * SCALE - top)
        m_ref[0, r] = top
        l_ref[0, r] = jnp.sum(weights, axis=0, keepdims=True)
        acc_ref[0, r] = dot_tn(v_ref[...], weights.astype(BF16))


def near(place, queries, span_keys, span_values):
    grid_spec = pltpu.PrefetchScalarGridSpec(
        num_scalar_prefetch=1,
        grid=(QB,),
        in_specs=[pl.BlockSpec((HALF, HD), lambda i, place: (2 * i + place[1], 0))] * 2
        + [pl.BlockSpec((BLK, HD), lambda i, place: (i, place[0]))] * 2,
        out_specs=[
            pl.BlockSpec((1, 2, HD, HALF), lambda i, place: (i, 0, 0, 0)),
            pl.BlockSpec((1, 2, 1, HALF), lambda i, place: (i, 0, 0, 0)),
            pl.BlockSpec((1, 2, 1, HALF), lambda i, place: (i, 0, 0, 0)),
        ],
    )
    return pl.pallas_call(
        near_kernel,
        grid_spec=grid_spec,
        out_shape=[
            jax.ShapeDtypeStruct((QB, 2, HD, HALF), F32),
            jax.ShapeDtypeStruct((QB, 2, 1, HALF), F32),
            jax.ShapeDtypeStruct((QB, 2, 1, HALF), F32),
        ],
        cost_estimate=pl.CostEstimate(
            flops=QB * 4 * BLK * BLK * HD, bytes_accessed=4 << 20, transcendentals=QB * BLK * BLK
        ),
        name="near",
    )(place, *queries, span_keys, span_values)


def pack_state(ref, i, out, top, total):
    ref[i, :HD, :] = out.astype(BF16)
    high = total.astype(BF16)
    low = (total - high.astype(F32)).astype(BF16)
    ref[i, HD:, :] = jnp.concatenate(
        [top.astype(BF16), high, low, jnp.zeros((TAIL - 3, out.shape[1]), BF16)], axis=0
    )


def unpack_state(ref, i):
    tail = ref[i, HD:, :].astype(F32)
    return ref[i, :HD, :].astype(F32), tail[0:1], tail[1:2] + tail[2:3]


def far_kernel(picks_ref, *refs, half):
    q_refs, whole_ref, early_ref, refs = refs[:2], refs[2], refs[3], refs[4:]
    out_refs, (buffer, early), refs = refs[:2], refs[2:4], refs[4:]
    score_refs, weight_refs, sems = refs[:2], refs[2:4], refs[4]
    picks = 2 * QB * SEL
    early_copy = pltpu.make_async_copy(
        early_ref.at[pl.ds(half * picks, picks)], early, sems.at[0]
    )
    early_copy.start()
    for pick in range(picks):
        sem = sems.at[1 if pick < SEL else 2]
        pltpu.make_async_copy(whole_ref.at[picks_ref[pick]], buffer.at[pick], sem).start()
    early_copy.wait()
    steps = [(row, k) for row in range(2 * QB) for k in range(2)]
    sums = {}

    def fetched(first, count, sem):
        held = buffer.at[pl.ds(first, count)]
        pltpu.make_async_copy(held, held, sem).wait()

    def joined(row, which):
        return jnp.concatenate(
            [held[row * SEL + j, which] for held in (buffer, early) for j in range(SEL)], axis=0
        )

    def score(number):
        row, k = steps[number]
        if number == 0:
            fetched(0, SEL, sems.at[1])
        if number == 2:
            fetched(SEL, picks - SEL, sems.at[2])
        first = row % QB * BLK + (picks_ref[picks] ^ k) * HALF
        tokens = pl.ds(pl.multiple_of(first, HALF), HALF)
        score_refs[number % 2][...] = dot_nt(joined(row, 0), q_refs[row // QB][tokens, :])

    def soften(number):
        score_ref, weight_ref = score_refs[number % 2], weight_refs[number % 2]
        tops, totals = [], []
        for lane in range(0, HALF, HD):
            lanes = slice(lane, lane + HD)
            top = rounded_top(jnp.max(score_ref[:, lanes], axis=0, keepdims=True))
            total = jnp.zeros((8, HD), F32)
            for row in range(0, BLK, 64):
                weights = jnp.exp2(score_ref[row : row + 64, lanes] * SCALE - top)
                weight_ref[row : row + 64, lanes] = weights.astype(BF16)
                total = total + jnp.sum(weights.reshape(8, 8, HD), axis=0)
            tops.append(top)
            totals.append(jnp.sum(total, axis=0, keepdims=True))
        sums[number] = jnp.concatenate(tops, axis=1), jnp.concatenate(totals, axis=1)

    def finish(number):
        row, k = steps[number]
        top, total = sums.pop(number)
        out = dot_tn(joined(row, 1), weight_refs[number % 2][...])
        pack_state(out_refs[k], row, out, top, total)

    for number in range(len(steps) + 2):
        if number < len(steps):
            score(number)
        if number >= 2:
            finish(number - 2)
        if 1 <= number <= len(steps):
            soften(number - 1)


def far(picks, queries, whole, early, half):
    pay = HD + TAIL
    vmem = pl.BlockSpec(memory_space=pltpu.VMEM)
    return pl.pallas_call(
        functools.partial(far_kernel, half=half),
        in_specs=[pl.BlockSpec(memory_space=pltpu.SMEM)]
        + [vmem] * 2
        + [pl.BlockSpec(memory_space=pl.ANY)] * 2,
        out_specs=[vmem] * 2,
        out_shape=[jax.ShapeDtypeStruct((2 * QB, pay, HALF), BF16)] * 2,
        scratch_shapes=[
            pltpu.VMEM((2 * QB * SEL,) + array.shape[1:], BF16) for array in (whole, early)
        ]
        + [pltpu.VMEM((BLK, HALF), F32)] * 2
        + [pltpu.VMEM((BLK, HALF), BF16)] * 2
        + [pltpu.SemaphoreType.DMA((3,))],
        compiler_params=pltpu.CompilerParams(vmem_limit_bytes=VMEM_BYTES),
        cost_estimate=pl.CostEstimate(
            flops=8 * 2 * QB * 4 * BLK * BLK * HD,
            bytes_accessed=5 << 20,
            transcendentals=2 * QB * BLK * BLK,
        ),
        name="far",
    )(picks, *queries, whole, early)


def collect_kernel(where_ref, *refs):
    sources, out_ref, sem = refs[:-2], refs[-2], refs[-1]

    def fetch(pick, carry):
        array, index = where_ref[pick, 0], where_ref[pick, 1]
        for number, source in enumerate(sources):

            def start(source=source):
                pltpu.make_async_copy(source.at[index], out_ref.at[pick], sem).start()

            pl.when(array == number)(start)
        return carry

    lax.fori_loop(0, out_ref.shape[0], fetch, 0)
    pltpu.make_async_copy(out_ref, out_ref, sem).wait()


def collect(where, arrays):
    return pl.pallas_call(
        collect_kernel,
        in_specs=[pl.BlockSpec(memory_space=pltpu.SMEM)]
        + [pl.BlockSpec(memory_space=pl.ANY)] * len(arrays),
        out_specs=pl.BlockSpec(memory_space=pltpu.VMEM),
        out_shape=jax.ShapeDtypeStruct((where.shape[0],) + arrays[0].shape[1:], BF16),
        scratch_shapes=[pltpu.SemaphoreType.DMA],
        compiler_params=pltpu.CompilerParams(vmem_limit_bytes=VMEM_BYTES),
        name="collect",
    )(where, *arrays)


def crossed(row):
    return (row + QB) % (2 * QB)


def merge_two_kernel(a_ref, b_ref, *out_refs):
    for row in range(2 * QB):
        acc_a, m_a, l_a = unpack_state(a_ref, row)
        acc_b, m_b, l_b = unpack_state(b_ref, crossed(row))
        top = jnp.maximum(m_a, m_b)
        f_a = jnp.exp2(m_a - top)
        f_b = jnp.exp2(m_b - top)
        out = f_a * acc_a + f_b * acc_b
        pack_state(out_refs[row // QB], row % QB, out, top, f_a * l_a + f_b * l_b)


def merge_two(mine, other):
    vmem = pl.BlockSpec(memory_space=pltpu.VMEM)
    return pl.pallas_call(
        merge_two_kernel,
        in_specs=[vmem] * 2,
        out_specs=[vmem] * 2,
        out_shape=[jax.ShapeDtypeStruct((QB,) + mine.shape[1:], BF16)] * 2,
        name="merge_two",
    )(mine, other)


def hold(arrays):
    hbm = pl.BlockSpec(memory_space=pl.ANY)
    return pl.pallas_call(
        lambda *refs: None,
        in_specs=[hbm] * len(arrays),
        out_specs=[hbm] * len(arrays),
        out_shape=[jax.ShapeDtypeStruct(array.shape, array.dtype) for array in arrays],
        input_output_aliases={n: n for n in range(len(arrays))},
        cost_estimate=pl.CostEstimate(
            flops=8 * QB * 4 * BLK * BLK * HD, bytes_accessed=4 << 20, transcendentals=8 * BLK
        ),
        name="hold",
    )(*arrays)


def merge_last_kernel(chip_ref, a_ref, b_ref, acc_ref, m_ref, l_ref, *refs):
    chip_refs, half_refs, share_refs = refs[:2], refs[2:4], refs[4:]
    for row in range(2 * QB):
        r, i = row // QB, row % QB
        states = [unpack_state(a_ref, row), unpack_state(b_ref, crossed(row))]
        states.append(unpack_state(chip_refs[r], i))
        states.append((acc_ref[i, r], m_ref[i, r], l_ref[i, r]))
        top = functools.reduce(jnp.maximum, [m for _, m, _ in states])
        factors = [jnp.exp2(m - top) for _, m, _ in states]
        total = sum(f * l for f, (_, _, l) in zip(factors, states))
        factors = [f / total for f in factors]
        out = sum(f * acc for f, (acc, _, _) in zip(factors, states)).T.astype(BF16)
        half_refs[r][i] = out
        for n, share_ref in enumerate(share_refs):

            def keep(share_ref=share_ref, r=r, out=out):
                share_ref[r] = out

            pl.when(chip_ref[0] ^ n == i)(keep)


def merge_last(chip, mine, core_part, near_state, chip_parts):
    vmem = pl.BlockSpec(memory_space=pltpu.VMEM)
    arrays = [mine, core_part, *near_state, *chip_parts]
    own, other, *shares = pl.pallas_call(
        merge_last_kernel,
        in_specs=[pl.BlockSpec(memory_space=pltpu.SMEM)] + [vmem] * len(arrays),
        out_specs=[vmem] * (2 + QB),
        out_shape=[jax.ShapeDtypeStruct((QB, HALF, HD), BF16)] * 2
        + [jax.ShapeDtypeStruct((2, HALF, HD), BF16)] * QB,
        name="merge_last",
    )(chip, *arrays)
    return own, other, shares


def assemble_kernel(core_ref, own_ref, other_ref, out_ref):
    for i in range(QB):
        for k, ref in enumerate((own_ref, other_ref)):
            first = pl.multiple_of(i * BLK + (core_ref[0] ^ k) * HALF, HALF)
            out_ref[pl.ds(first, HALF), :] = ref[i]


def assemble(core, own, other):
    vmem = pl.BlockSpec(memory_space=pltpu.VMEM)
    return pl.pallas_call(
        assemble_kernel,
        in_specs=[pl.BlockSpec(memory_space=pltpu.SMEM)] + [vmem] * 2,
        out_specs=vmem,
        out_shape=jax.ShapeDtypeStruct((QB * BLK, HD), BF16),
        name="assemble",
    )(core, own, other)


def project_kernel(*refs):
    a_refs, w_refs, out_ref = refs[:QB], refs[QB:-1], refs[-1]
    rows = jnp.concatenate([a_ref[r] for a_ref in a_refs for r in range(2)], axis=1)
    tile = 512
    for first in range(0, out_ref.shape[1], tile):
        weight = jnp.concatenate([w_ref[:, first : first + tile] for w_ref in w_refs], axis=0)
        out_ref[:, first : first + tile] = jnp.dot(
            rows, weight, preferred_element_type=F32
        ).astype(BF16)


def project(parts, weights):
    vmem = pl.BlockSpec(memory_space=pltpu.VMEM)
    return pl.pallas_call(
        project_kernel,
        in_specs=[vmem] * (len(parts) + len(weights)),
        out_specs=vmem,
        out_shape=jax.ShapeDtypeStruct((parts[0].shape[1], weights[0].shape[1]), BF16),
        compiler_params=pltpu.CompilerParams(vmem_limit_bytes=24 << 20),
        name="project",
    )(*parts, *weights)


def shift(array, dz, dx):
    pairs = []
    for z in range(NZ):
        for x in range(NX):
            pairs.append((z * NX + x, (z + dz) % NZ * NX + (x + dx) % NX))
    return lax.ppermute(array, "ctx", pairs)


def swap(array, bits):
    return lax.ppermute(array, "head", [(h, h ^ bits) for h in range(lax.axis_size("head"))])


def after(value, *earlier):
    return lax.optimization_barrier((value, earlier))[0]


def body(queries, block_picks, span_keys, span_values, cache_keys, cache_values, out_weight):
    heads = lax.axis_size("head")
    head = lax.axis_index("head")
    part = head % GROUP
    kv = head // GROUP
    share = BLK // GROUP

    def cut(first, rows):
        pieces = []
        for cache in (cache_keys, cache_values):
            view = cache.reshape(BLOCKS, BLK, cache.shape[1])
            pieces.append(
                lax.dynamic_slice(view, (0, part * share + first, kv * HD), (BLOCKS, rows, HD))
            )
        return jnp.stack(pieces, axis=1)

    whole = lax.all_gather(cut(0, share - RING_ROWS), "ctx", axis=0, tiled=True)

    ring = cut(share - RING_ROWS, RING_ROWS)
    z1, z2 = shift(ring, 1, 0), shift(ring, -1, 0)
    z3, z4 = shift(z1, 1, 0), shift(z2, -1, 0)
    groups = [jnp.concatenate([ring, z1], axis=0), jnp.concatenate([z2, z3], axis=0)]
    z5, z6 = shift(z3, 1, 0), shift(z4, -1, 0)
    half = BLOCKS // 2
    z7, z8 = shift(z5[:half], 1, 0), shift(z6[half:], -1, 0)
    groups += [jnp.concatenate([z4, z5], axis=0), jnp.concatenate([z6, z7, z8], axis=0)]
    from_below = [shift(group, 0, 1) for group in groups]
    from_above = [shift(group, 0, -1) for group in groups]
    farthest = [shift(group, 0, 1) for group in from_below[:2]]
    farthest += [shift(group, 0, -1) for group in from_above[2:]]
    ring_arrays = groups + from_below + from_above + farthest

    core, chip = head % 2, head // 2
    queries_core = swap(after(queries, groups[3]), 1)
    near_queries = after([queries, queries_core], *from_below, *from_above)
    near_state = near(
        jnp.stack([kv, core]).astype(jnp.int32), near_queries, span_keys, span_values
    )
    picks_chip = swap(after(block_picks, from_below[1], from_above[1]), 2)
    queries_early, weight_early = after(
        (queries, out_weight), *from_below, *from_above, *farthest, picks_chip
    )
    queries_chip = swap(queries_early, 2)
    picks_pair = jnp.stack([block_picks, picks_chip])
    weights = [out_weight] + [None] * (heads - 1)
    for bits in range(2, heads, 2):
        weights[bits] = swap(weight_early, bits)
    queries_chip, picks_pair, weights[::2] = after(
        (queries_chip, picks_pair, weights[::2]), *ring_arrays
    )
    group_queries = [queries, queries_core, queries_chip, swap(queries_chip, 1)]
    picks_core = swap(picks_pair, 1)
    group_picks = [picks_pair[0], picks_core[0], picks_pair[1], picks_core[1]]
    for bits in range(0, heads, 2):
        weights[bits + 1] = swap(weights[bits], 1)
    picks = [group_pick.reshape(QB * SEL) for group_pick in group_picks]

    every_pick = jnp.concatenate([picks[r] for r in (2, 3, 0, 1)])
    owner, local = every_pick // BLOCKS, every_pick % BLOCKS
    ctx = lax.axis_index("ctx")
    dz = (owner // NX - ctx // NX) % NZ
    dx = (owner % NX - ctx % NX) % NX
    order_x = jnp.where(dx == 0, 0, jnp.where(dx == 3, 1, jnp.where(dx == 1, 2, 3)))
    order_z = jnp.where(dz == 0, 0, jnp.where(dz > NZ // 2, 2 * (NZ - dz) - 1, 2 * dz))
    order_z = jnp.where(dz == NZ // 2, NZ - 1, order_z)
    where = jnp.stack(
        [len(groups) * order_x + order_z // 2, order_z % 2 * BLOCKS + local], axis=-1
    )
    early = collect(where.astype(jnp.int32), ring_arrays)

    picks, group_queries, weights, near_state, early = lax.optimization_barrier(
        (picks, group_queries, weights, near_state, early)
    )

    def far_of(first, second, earlier, half):
        return far(
            after(jnp.concatenate([picks[first], picks[second], core[None]]), *earlier),
            [group_queries[first], group_queries[second]],
            whole,
            early,
            half,
        )

    chip_here, chip_there = far_of(2, 3, [], 0)
    for_chip = merge_two(chip_here, swap(chip_there, 1))
    chip_parts = [swap(piece, 2) for piece in for_chip]
    own_here, own_there = far_of(0, 1, for_chip, 1)
    core_part = swap(own_there, 1)
    chip_parts = hold(chip_parts)
    own, other, shares = merge_last(chip[None], own_here, core_part, near_state, chip_parts)
    parts = [shares[0]] + [swap(shares[n], 2 * n) for n in range(1, QB)]
    attention = assemble(core[None], own, swap(other, 1))
    return attention, project(after(parts, attention), weights)


def solution(mesh):
    placed = (
        P("ctx", "head"),
        P("ctx", "head", None),
        P("ctx", None),
        P("ctx", None),
        P("ctx", None),
        P("ctx", None),
        P("head", None),
    )
    return jax.shard_map(
        body,
        mesh=mesh,
        in_specs=placed,
        out_specs=(P("ctx", "head"), P(("ctx", "head"), None)),
        check_vma=False,
    )
```
